256 devices in a mesh: table: 64 (over x, z, core), row: 4 (over y).
Axes of the slice: x: 4, y: 4, z: 8, core: 2. Of those that a mesh axis runs over, the one named last changes fastest.
Arguments:
- emb_rows: float32 [512, 512, 256], P('table', 'row'), may hold values from -3 to 3
- entry_ids: int32 [512, 4096], P('table'), may hold values from 0 to 511
- entry_sample: int32 [512, 4096], P('table'), may hold values from 0 to 1023, never falling along the last dimension, each value on 1 to 16 neighbouring positions
- cross_v: bfloat16 [2, 131072, 512], P(None, 'table'), may hold values from -0.015625 to 0.015625
- cross_u: bfloat16 [2, 512, 131072], P(None, None, 'table'), may hold values from -0.25 to 0.25
- cross_bias: float32 [2, 131072], P(None, 'table'), may hold values from -3 to 3
- cotangent: bfloat16 [1024, 131072], P('row', 'table'), may hold values from -6 to 6
Outputs:
- crossed: bfloat16 [1024, 131072], P('row', 'table')
- row_grads: float32 [512, 512, 256], P('table', 'row')
The draws below stay inside these ranges and needn't reach their ends.
Inputs may be any that keep to these rules, and one draw needn't show every extreme that they name: entry_sample never falls along a table's entries, and each sample has 1 to 16 entries in every table.
All inputs are finite; a program needn't handle non-finite values.
Results may differ from the reference program's by a relative error of at most 0.035.
Values may be sent and summed in bfloat16 or wider, within the bound.
No kernel may reach another device: no remote copies, remote signals or barrier semaphores. Data moves between devices by JAX's collectives and lax.ppermute only.
A program may use at most 128 MiB of HBM per device.

```python
import math
import jax
import jax.numpy as jnp
import numpy as np
from jax import lax

EMB = 256
RANK = 512
LAYERS = 2
MOSTBAG = 16
ROWS_DEV = 128
TABLES = 512
FEATS = 131072
SAMPLES = 1024
ROWS = 512
ENTRIES = 4096
N_ROW = 4


def touch_ends(array, stream_key, least, largest):
    longest = array.shape.index(max(array.shape))
    spots = []
    for shift in (0, 1):
        where = [jax.random.randint(jax.random.fold_in(stream_key, axis), (), 0, length) for axis, length in enumerate(array.shape)]
        where[longest] = (where[longest] + shift) % array.shape[longest]
        spots.append(tuple(where))
    return array.at[spots[0]].set(least).at[spots[1]].set(largest)


def block_scale(own_key, dims, pieces, low, top_value):
    loudness = 1.0
    for position, blocks in pieces:
        heights = jax.random.uniform(jax.random.fold_in(jax.random.fold_in(own_key, 6), position), (blocks,), jnp.float32, low / len(pieces), top_value / len(pieces))
        loudness = loudness * jnp.repeat(jnp.exp(heights), dims[position] // blocks).reshape((-1,) + (1,) * (len(dims) - 1 - position))
    return loudness


def cumulative_ranks(count, slope):
    weights = [(1 << 20) // math.isqrt(grade ** slope) + 1 for grade in range(1, count + 1)]
    deviation = 1 + sum(weights) // (1 << 30)
    return np.cumsum(np.array([max(1, weight // deviation) for weight in weights]))


def skewed_ids(stream_key, shape, number_of, lean):
    table = cumulative_ranks(number_of, lean)
    ticket = jax.random.randint(jax.random.fold_in(stream_key, 1), shape, 0, int(table[number_of - 1]))
    grade = jnp.searchsorted(jnp.asarray(table, jnp.int32), ticket, side="right")
    return jax.random.permutation(jax.random.fold_in(stream_key, 2), number_of)[grade].astype(jnp.int32)


def profile(count, total, bound, slope):
    weights = [(1 << 20) // math.isqrt(grade ** slope) + 1 for grade in range(2, count + 1)]
    spare, given = total - bound - (count - 1), [1] * (count - 1)
    while spare > 0:
        candidates = [i for i in range(count - 1) if given[i] < bound]
        whole, budget = sum([weights[i] for i in candidates]), spare
        for i in candidates:
            addition = min(bound - given[i], max(1, budget * weights[i] // whole), spare)
            given[i] = given[i] + addition
            spare = spare - addition
    return np.array([bound] + given)


def uneven_parts(own_key, amount, total, reach, skew):
    if amount == 2:
        one = jax.random.randint(own_key, (), max(1, total - reach), min(reach, total - 1) + 1)
        return jnp.stack([one, total - one])
    lengths = jnp.asarray(profile(amount, total, reach, skew), jnp.int32)
    twos = (amount - 1) // 2
    donor, taker = lengths[1:1 + 2 * twos:2], lengths[2:2 + 2 * twos:2]
    room = jnp.minimum(donor - 1, reach - taker)
    shifted = jax.random.randint(jax.random.fold_in(own_key, 1), (twos,), 0, 1 << 20) % (room + 1)
    lengths = lengths.at[1:1 + 2 * twos:2].set(donor - shifted).at[2:2 + 2 * twos:2].set(taker + shifted)
    return lengths[jax.random.permutation(jax.random.fold_in(own_key, 2), amount)]


def normal_values(stream_key, extent, spread, bound, split=(), held_as=jnp.bfloat16):
    drawn = spread * jax.random.normal(stream_key, extent, jnp.float32)
    if split:
        drawn = drawn * block_scale(stream_key, extent, split, -0.22, 0.18)
    return jnp.clip(drawn, -bound, bound).astype(held_as)


def setup_inputs(seed: int = 0) -> dict:
    splits = jax.random.split(jax.random.key(seed), 8)
    return {
        "emb_rows": normal_values(splits[0], (TABLES, ROWS, EMB), 0.5, 3.0, ((0, 64), (1, 4)), jnp.float32),
        "entry_ids": touch_ends(skewed_ids(splits[1], (TABLES, ENTRIES), ROWS, 2), jax.random.fold_in(splits[1], 3), 0, ROWS - 1).astype(jnp.int32),
        "entry_sample": jax.vmap(lambda own: jnp.searchsorted(jnp.cumsum(uneven_parts(own, SAMPLES, ENTRIES, MOSTBAG, 2)), jnp.arange(ENTRIES), side="right"))(jax.random.split(splits[2], TABLES)).reshape((TABLES, ENTRIES)).astype(jnp.int32),
        "cross_v": normal_values(splits[3], (LAYERS, FEATS, RANK), FEATS ** -0.5, 0.015625, ((1, 64),)),
        "cross_u": normal_values(splits[4], (LAYERS, RANK, FEATS), RANK ** -0.5, 0.25, ((2, 64),)),
        "cross_bias": normal_values(splits[5], (LAYERS, FEATS), 0.5, 3.0, ((1, 64),), jnp.float32),
        "cotangent": normal_values(splits[6], (SAMPLES, FEATS), 1.0, 6.0, ((0, 4), (1, 64))),
    }


def block_counts(entry_ids, entry_sample, start, block):
    local = entry_sample - start
    inside = ((local >= 0) & (local < block)).astype(jnp.float32)
    spots = jnp.clip(local, 0, block - 1)

    def single(spot, ids, weight):
        return jnp.zeros((block, ROWS), jnp.float32).at[spot, ids].add(weight)

    return jax.vmap(single)(spots, entry_ids, inside)


def reference(emb_rows, entry_ids, entry_sample, cross_v, cross_u, cross_bias, cotangent):
    block = math.gcd(SAMPLES, 128)
    nblocks = SAMPLES // block
    row_groups = emb_rows.reshape(TABLES, N_ROW, ROWS_DEV, EMB)

    def advance(grad_rows, index):
        start = (index * block).astype(jnp.int32)
        counts = block_counts(entry_ids, entry_sample, start, block)
        grouped = counts.reshape(TABLES, block, N_ROW, ROWS_DEV)
        partial_value = jnp.einsum("tbqr,tqre->qbte", grouped, row_groups, precision=lax.Precision.HIGHEST)
        pooled = jnp.sum(partial_value.astype(jnp.bfloat16).astype(jnp.float32), axis=0)
        pooled = pooled.astype(jnp.bfloat16).reshape(block, FEATS)
        base = pooled.astype(jnp.float32)
        layer_in = pooled
        saved = []
        for layer in range(LAYERS):
            narrow = jnp.dot(layer_in, cross_v[layer], preferred_element_type=jnp.float32).astype(jnp.bfloat16)
            wide = jnp.dot(narrow, cross_u[layer], preferred_element_type=jnp.float32) + cross_bias[layer]
            saved.append(wide)
            layer_in = (base * wide + layer_in.astype(jnp.float32)).astype(jnp.bfloat16)
        grad = lax.dynamic_slice_in_dim(cotangent, start, block, 0).astype(jnp.float32)
        accum = jnp.zeros((block, FEATS), jnp.float32)
        for layer in reversed(range(LAYERS)):
            grad_wide = (grad * base).astype(jnp.bfloat16)
            grad_narrow = jnp.dot(grad_wide, cross_u[layer].T, preferred_element_type=jnp.float32).astype(jnp.bfloat16)
            accum = accum + grad * saved[layer]
            grad = grad + jnp.dot(grad_narrow, cross_v[layer].T, preferred_element_type=jnp.float32)
        grad_pooled = (accum + grad).astype(jnp.bfloat16).astype(jnp.float32).reshape(block, TABLES, EMB)
        grad_rows = grad_rows + jnp.einsum("tbr,bte->tre", counts, grad_pooled, precision=lax.Precision.HIGHEST)
        return grad_rows, layer_in

    grad_rows, outputs = lax.scan(advance, jnp.zeros((TABLES, ROWS, EMB), jnp.float32), jnp.arange(nblocks, dtype=jnp.int32))
    return outputs.reshape(SAMPLES, FEATS), grad_rows
```

```python
import functools

import jax
import jax.numpy as jnp
from jax import lax
from jax.experimental import pallas as pl
from jax.experimental.pallas import tpu as pltpu
from jax.sharding import PartitionSpec as P

F32 = jnp.float32
BF16 = jnp.bfloat16
EB = 512
NT = (((1,), (1,)), ((), ()))
TN = (((0,), (0,)), ((), ()))


def vmem():
    return pl.BlockSpec(memory_space=pltpu.VMEM)


def smem():
    return pl.BlockSpec(memory_space=pltpu.SMEM)


def params(mib):
    return pltpu.CompilerParams(vmem_limit_bytes=mib * 2**20)


def cost(flops, moved):
    return pl.CostEstimate(flops=flops, bytes_accessed=moved, transcendentals=0)


def cast_kernel(in_ref, out_ref):
    out_ref[...] = in_ref[...].astype(BF16)


def cast_half(emb_rows, side):
    tabs, rows, emb = emb_rows.shape
    block = (tabs // 2, rows, emb)
    return pl.pallas_call(
        cast_kernel,
        grid=(1,),
        in_specs=[pl.BlockSpec(block, lambda t: (side, 0, 0))],
        out_specs=pl.BlockSpec(block, lambda t: (0, 0, 0)),
        out_shape=jax.ShapeDtypeStruct(block, BF16),
        compiler_params=params(16),
        cost_estimate=cost(1 << 17, 3 << 18),
        name="cast",
    )(emb_rows)


def counts_kernel(mine_ref, ids_ref, own_ref, *refs, first_table):
    out_ref, turned_ref, acc_ref = refs[-3:]
    t = pl.program_id(0) + first_table
    samp, rows = acc_ref.shape
    mine = mine_ref[0]
    low = mine * samp
    turn = mine * (rows // 4)
    owners = own_ref[pl.ds(t, 1), :]
    first = jnp.sum((owners < low).astype(jnp.int32))
    last = jnp.sum((owners < low + samp).astype(jnp.int32))
    acc_ref[...] = jnp.zeros_like(acc_ref)

    def step(block, carry):
        at = pl.ds(pl.multiple_of(block * EB, EB), EB)
        who = own_ref[pl.ds(t, 1), at] - low
        row = (ids_ref[pl.ds(t, 1), at] - turn) & (rows - 1)
        who_hot = lax.broadcasted_iota(jnp.int32, (samp, EB), 0) == who
        row_hot = lax.broadcasted_iota(jnp.int32, (rows, EB), 0) == row
        acc_ref[...] += lax.dot_general(
            who_hot.astype(F32).astype(BF16), row_hot.astype(F32).astype(BF16), NT, preferred_element_type=F32
        )
        return carry

    lax.fori_loop(first // EB, (last + EB - 1) // EB, step, 0)
    total = acc_ref[...]
    out_ref[0] = total.astype(BF16)
    turned_ref[0] = total.T.astype(BF16)


def make_counts(mine, ids, owners, samp, rows, side, before):
    tabs, entries = ids.shape
    half = tabs // 2
    at = half * side
    whole = pl.BlockSpec((tabs, entries), lambda t: (0, 0))
    return pl.pallas_call(
        functools.partial(counts_kernel, first_table=at),
        grid=(half,),
        in_specs=[smem(), whole, whole] + [pl.BlockSpec(memory_space=pl.ANY)] * len(before),
        out_specs=[
            pl.BlockSpec((1, samp, rows), lambda t: (t + at, 0, 0)),
            pl.BlockSpec((1, rows, samp), lambda t: (t + at, 0, 0)),
        ],
        out_shape=[
            jax.ShapeDtypeStruct((tabs, samp, rows), BF16),
            jax.ShapeDtypeStruct((tabs, rows, samp), BF16),
        ],
        scratch_shapes=[pltpu.VMEM((samp, rows), F32)],
        input_output_aliases={3: 0, 4: 1} if before else {},
        compiler_params=params(56),
        cost_estimate=cost(half * samp * rows * 3072, 3 << 20),
        name="counts",
    )(mine, ids, owners, *before)


def chunk_at(i):
    x, z = i // 8, i % 8
    return (x & 1) * 128 + (x >> 1) * 64 + (z & 1) * 32 + ((z >> 1) & 1) * 16, (z >> 2) * 256


def add_sums(core_ref, z, g, z_ref, g_ref, keep_ref, send_ref):
    t = pl.program_id(0)

    @pl.when(t == 0)
    def _():
        z_ref[...] = z
        g_ref[...] = g

    @pl.when(t > 0)
    def _():
        z_ref[...] += z
        g_ref[...] += g

    @pl.when(t == pl.num_programs(0) - 1)
    def _():
        even = core_ref[0] == 0
        z, g = z_ref[...], g_ref[...]
        keep_ref[...] = jnp.where(even, z, g)
        send_ref[...] = jnp.where(even, g, z).astype(BF16)


def first_kernel(core_ref, counts_ref, *refs):
    (oa, ob, ra, rb, pa, pb, la, lb, cot_ref, v_ref, u_ref, pooled_ref, keep_ref, send_ref, z_ref, g_ref) = refs
    front = pl.program_id(0) < pl.num_programs(0) // 2
    parts = []
    for i in range(counts_ref.shape[0]):
        rows = jnp.concatenate(
            [jnp.where(front, a[i], b[i]) for a, b in ((oa, ob), (ra, rb), (pa, pb), (la, lb))], axis=0
        )
        parts.append(jnp.dot(counts_ref[i], rows, preferred_element_type=F32).astype(BF16))
    pooled = jnp.concatenate(parts, axis=1)
    pooled_ref[...] = pooled
    wide = (cot_ref[...].astype(F32) * pooled.astype(F32)).astype(BF16)
    z = jnp.dot(pooled, v_ref[0], preferred_element_type=F32)
    g = lax.dot_general(wide, u_ref[0], NT, preferred_element_type=F32)
    add_sums(core_ref, z, g, z_ref, g_ref, keep_ref, send_ref)


def first_sums(core, counts, embs, cot, v, u):
    tabs, samp, rows = counts.shape
    emb = embs[0].shape[-1]
    rank = v.shape[-1]
    steps = tabs // 2
    half = steps // 2
    block = (2, rows // 4, emb)
    a_spec = pl.BlockSpec(block, lambda t: (jnp.minimum(t, half - 1), 0, 0))
    b_spec = pl.BlockSpec(block, lambda t: (jnp.maximum(t - half, 0), 0, 0))
    feat = pl.BlockSpec((samp, 2 * emb), lambda t: (0, t))
    sums = pl.BlockSpec((samp, rank), lambda t: (0, 0))
    return pl.pallas_call(
        first_kernel,
        grid=(steps,),
        in_specs=[smem(), pl.BlockSpec((2, samp, rows), lambda t: (t, 0, 0))]
        + [a_spec, b_spec] * 4
        + [
            feat,
            pl.BlockSpec((1, 2 * emb, rank), lambda t: (0, t, 0)),
            pl.BlockSpec((1, rank, 2 * emb), lambda t: (1, 0, t)),
        ],
        out_specs=[feat, sums, sums],
        out_shape=[
            jax.ShapeDtypeStruct((samp, tabs * emb), BF16),
            jax.ShapeDtypeStruct((samp, rank), F32),
            jax.ShapeDtypeStruct((samp, rank), BF16),
        ],
        scratch_shapes=[pltpu.VMEM((samp, rank), F32)] * 2,
        compiler_params=params(48),
        cost_estimate=cost(3 << 29, 10 << 20),
        name="first_sums",
    )(core, counts, *embs, cot, v, u)


def to_core(arr):
    return lax.ppermute(arr, "c", [(0, 1), (1, 0)])


def along(arr, axis, bit):
    size = 4 if axis == "x" else 8
    return lax.ppermute(arr, axis, [(i, i ^ bit) for i in range(size)])


def small(kernel, out_shape, name, *args, scalars=0):
    return pl.pallas_call(
        kernel,
        in_specs=[smem()] * scalars + [vmem()] * (len(args) - scalars),
        out_specs=jax.tree.map(lambda _: vmem(), out_shape),
        out_shape=out_shape,
        compiler_params=params(8),
        cost_estimate=cost(1 << 20, 1 << 20),
        name=name,
    )(*args)


def cut_kernel(keep_ref, got_ref, out_ref):
    for i in range(out_ref.shape[0]):
        r, c = chunk_at(i)
        at = (slice(r, r + 16), slice(c, c + 256))
        out_ref[i] = (keep_ref[at] + got_ref[at].astype(F32)).astype(BF16)


def total_kernel(in_ref, out_ref):
    total = in_ref[0].astype(F32)
    for i in range(1, in_ref.shape[0]):
        total = total + in_ref[i].astype(F32)
    total = total.astype(BF16)
    for i in range(out_ref.shape[0]):
        out_ref[i] = total


def copies_kernel(in_ref, out_ref):
    for i in range(out_ref.shape[0]):
        out_ref[i] = in_ref[...]


def halve_kernel(bit_ref, keep_ref, got_ref, kept_ref, send_ref):
    rows, cols = kept_ref.shape
    total = keep_ref[...] + got_ref[...].astype(F32)
    if rows == total.shape[0]:
        low, high = total[:, :cols], total[:, cols:]
    else:
        low, high = total[:rows], total[rows:]
    even = bit_ref[0] == 0
    kept_ref[...] = jnp.where(even, low, high)
    send_ref[...] = jnp.where(even, high, low).astype(BF16)


def sum_by_exchange(keep, send):
    chunks = small(cut_kernel, jax.ShapeDtypeStruct((32, 16, 256), BF16), "cut", keep, to_core(send))
    parts = lax.all_to_all(chunks, ("x", "z"), 0, 0, tiled=True)
    copies = small(total_kernel, jax.ShapeDtypeStruct((32, 16, 256), BF16), "total", parts)
    mine = lax.all_to_all(copies, ("x", "z"), 0, 0, tiled=True)
    return mine, to_core(mine)


def sum_by_halves(xpos, zpos, keep, send):
    got = to_core(send)
    for axis, bit, pos in (("x", 1, xpos), ("x", 2, xpos >> 1), ("z", 1, zpos), ("z", 2, zpos >> 1), ("z", 4, zpos >> 2)):
        rows, cols = keep.shape
        shape = (rows, cols // 2) if (axis, bit) == ("z", 4) else (rows // 2, cols)
        keep, send = small(
            halve_kernel,
            [jax.ShapeDtypeStruct(shape, F32), jax.ShapeDtypeStruct(shape, BF16)],
            "halve",
            pos & 1,
            keep,
            got,
            scalars=1,
        )
        got = along(send, axis, bit)
    done = small(
        lambda a, b, out: copies_kernel((a[...] + b[...].astype(F32)).astype(BF16), out),
        jax.ShapeDtypeStruct((8, 16, 256), BF16),
        "done",
        keep,
        got,
    )
    part = lax.all_to_all(done, "z", 0, 0, tiled=True)
    copies = small(copies_kernel, jax.ShapeDtypeStruct((4, 8, 16, 256), BF16), "copies", part)
    mine = lax.all_to_all(copies, "x", 0, 0, tiled=True).reshape(32, 16, 256)
    return mine, to_core(mine)


def spread(core_ref, mine_ref, other_ref, in_ref):
    core = core_ref[0]
    for side, ref in ((core, mine_ref), (1 - core, other_ref)):
        for i in range(32):
            r, c = chunk_at(i)
            in_ref[side, r : r + 16, c : c + 256] = ref[i]


def middle_kernel(core_ref, mine_ref, other_ref, pooled_ref, cot_ref, u_ref, b_ref, v_ref, *refs):
    x1_ref, a_ref, keep_ref, send_ref, in_ref, z_ref, g_ref = refs

    @pl.when(pl.program_id(0) == 0)
    def _():
        spread(core_ref, mine_ref, other_ref, in_ref)

    u, v = u_ref[0], v_ref[0]
    pooled = pooled_ref[...].astype(F32)
    cot = cot_ref[...].astype(F32)
    h0 = jnp.dot(in_ref[0], u, preferred_element_type=F32) + b_ref[0:1, :]
    x1 = (pooled * h0 + pooled).astype(BF16)
    x1_ref[...] = x1
    g1 = cot + lax.dot_general(in_ref[1], v, NT, preferred_element_type=F32)
    a_ref[...] = (g1 * h0 + g1).astype(BF16)
    wide = (g1 * pooled).astype(BF16)
    z = jnp.dot(x1, v, preferred_element_type=F32)
    g = lax.dot_general(wide, u, NT, preferred_element_type=F32)
    add_sums(core_ref, z, g, z_ref, g_ref, keep_ref, send_ref)


def middle(core, mine, other, pooled, cot, u, bias, v):
    samp, feats = pooled.shape
    rank = v.shape[-1]
    step = 512
    wide = pl.BlockSpec((samp, step), lambda t: (0, t))
    whole = pl.BlockSpec(mine.shape, lambda t: (0, 0, 0))
    sums = pl.BlockSpec((samp, rank), lambda t: (0, 0))
    feat = jax.ShapeDtypeStruct((samp, feats), BF16)
    return pl.pallas_call(
        middle_kernel,
        grid=(feats // step,),
        in_specs=[
            smem(),
            whole,
            whole,
            wide,
            wide,
            pl.BlockSpec((1, rank, step), lambda t: (0, 0, t)),
            pl.BlockSpec((2, step), lambda t: (0, t)),
            pl.BlockSpec((1, step, rank), lambda t: (1, t, 0)),
        ],
        out_specs=[wide, wide, sums, sums],
        out_shape=[feat, feat, jax.ShapeDtypeStruct((samp, rank), F32), jax.ShapeDtypeStruct((samp, rank), BF16)],
        scratch_shapes=[pltpu.VMEM((2, samp, rank), BF16)] + [pltpu.VMEM((samp, rank), F32)] * 2,
        compiler_params=params(56),
        cost_estimate=cost(1 << 31, 8 << 20),
        name="middle",
    )(core, mine, other, pooled, cot, u, bias, v)


def last_kernel(core_ref, mine_ref, other_ref, turned_ref, pooled_ref, cot_ref, x1_ref, a_ref, u_ref, b_ref, v_ref, *refs):
    crossed_ref, p0, p1a, p1b, p2a, p2b, p3a, p3b, in_ref = refs
    t = pl.program_id(0)
    half = pl.num_programs(0) // 2

    @pl.when(t == 0)
    def _():
        spread(core_ref, mine_ref, other_ref, in_ref)

    pooled = pooled_ref[...].astype(F32)
    cot = cot_ref[...].astype(F32)
    h1 = jnp.dot(in_ref[0], u_ref[0], preferred_element_type=F32) + b_ref[1:2, :]
    crossed_ref[...] = (pooled * h1 + x1_ref[...].astype(F32)).astype(BF16)
    grad = cot * h1 + a_ref[...].astype(F32) + lax.dot_general(in_ref[1], v_ref[0], NT, preferred_element_type=F32)
    grad = grad.astype(BF16)
    tables, rows, emb = p0.shape
    for i in range(tables):
        part = jnp.dot(turned_ref[i], grad[:, i * emb : (i + 1) * emb], preferred_element_type=F32)
        p0[i] = part[:rows]

        @pl.when(t < half)
        def _():
            for k, ref in enumerate((p1a, p2a, p3a)):
                ref[i] = part[(k + 1) * rows : (k + 2) * rows].astype(BF16)

        @pl.when(t >= half)
        def _():
            for k, ref in enumerate((p1b, p2b, p3b)):
                ref[i] = part[(k + 1) * rows : (k + 2) * rows].astype(BF16)


def last(core, mine, other, turned, pooled, cot, x1, a, u, bias, v):
    tabs, rows, samp = turned.shape
    rank = v.shape[-1]
    emb = pooled.shape[1] // tabs
    steps = tabs // 2
    half = steps // 2
    whole = pl.BlockSpec(mine.shape, lambda t: (0, 0, 0))
    feat = pl.BlockSpec((samp, 2 * emb), lambda t: (0, t))
    block = (2, rows // 4, emb)
    a_spec = pl.BlockSpec(block, lambda t: (jnp.minimum(t, half - 1), 0, 0))
    b_spec = pl.BlockSpec(block, lambda t: (jnp.maximum(t - half, 0), 0, 0))
    piece = jax.ShapeDtypeStruct((tabs // 2, rows // 4, emb), BF16)
    return pl.pallas_call(
        last_kernel,
        grid=(steps,),
        in_specs=[smem(), whole, whole, pl.BlockSpec((2, rows, samp), lambda t: (t, 0, 0))]
        + [feat] * 4
        + [
            pl.BlockSpec((1, rank, 2 * emb), lambda t: (1, 0, t)),
            pl.BlockSpec((2, 2 * emb), lambda t: (0, t)),
            pl.BlockSpec((1, 2 * emb, rank), lambda t: (0, t, 0)),
        ],
        out_specs=[feat, pl.BlockSpec(block, lambda t: (t, 0, 0))] + [a_spec, b_spec] * 3,
        out_shape=[
            jax.ShapeDtypeStruct((samp, tabs * emb), BF16),
            jax.ShapeDtypeStruct((tabs, rows // 4, emb), F32),
        ]
        + [piece] * 6,
        scratch_shapes=[pltpu.VMEM((2, samp, rank), BF16)],
        compiler_params=params(56),
        cost_estimate=cost(3 << 29, 14 << 20),
        name="last",
    )(core, mine, other, turned, pooled, cot, x1, a, u, bias, v)


def right(arr):
    return lax.ppermute(arr, "row", [(i, (i + 1) & 3) for i in range(4)])


def left(arr):
    return lax.ppermute(arr, "row", [(i, (i + 3) & 3) for i in range(4)])


def scatter_rows(p0, p1a, p1b, p2a, p2b, p3a, p3b):
    from_left, from_right = right(p2a), left(p2b)
    sum_b, sum_a = right(p1b), left(p3a)
    far_a = right((p1a.astype(F32) + from_left.astype(F32)).astype(BF16))
    far_b = left((p3b.astype(F32) + from_right.astype(F32)).astype(BF16))
    others = jnp.concatenate(
        [sum_a.astype(F32) + far_a.astype(F32), sum_b.astype(F32) + far_b.astype(F32)], axis=0
    )
    return p0 + others


def scalar(axis):
    return lax.axis_index(axis).astype(jnp.int32).reshape(1)


def local(emb_rows, entry_ids, entry_sample, cross_v, cross_u, cross_bias, cotangent):
    samp = cotangent.shape[0]
    rows = emb_rows.shape[1] * lax.axis_size("row")
    mine, core, xpos, zpos = scalar("row"), scalar("c"), scalar("x"), scalar("z")
    own_a, own_b = cast_half(emb_rows, 0), cast_half(emb_rows, 1)
    left_a, right_b = right(own_a), left(own_b)
    left_b, right_a = right(own_b), left(own_a)
    counted = make_counts(mine, entry_ids, entry_sample, samp, rows, 0, ())
    left_a, right_b, *counted = lax.optimization_barrier((left_a, right_b, *counted))
    far_a, far_b = right(left_a), left(right_b)
    counts, turned = make_counts(mine, entry_ids, entry_sample, samp, rows, 1, counted)
    embs = (own_a, own_b, right_a, right_b, far_a, far_b, left_a, left_b)
    pooled, keep, send = first_sums(core, counts, embs, cotangent, cross_v, cross_u)
    sums = sum_by_exchange(keep, send)
    x1, a, keep, send = middle(core, *sums, pooled, cotangent, cross_u, cross_bias, cross_v)
    sums = sum_by_halves(xpos, zpos, keep, send)
    crossed, *pieces = last(core, *sums, turned, pooled, cotangent, x1, a, cross_u, cross_bias, cross_v)
    return crossed, scatter_rows(*pieces)


def solution(mesh):
    fine = jax.sharding.Mesh(mesh.devices.reshape(4, 8, 2, 4), ("x", "z", "c", "row"))
    table = ("x", "z", "c")
    placed = (
        P(table, "row", None),
        P(table, None),
        P(table, None),
        P(None, table, None),
        P(None, None, table),
        P(None, table),
        P("row", table),
    )
    return jax.shard_map(
        local,
        mesh=fine,
        in_specs=placed,
        out_specs=(P("row", table), P(table, "row", None)),
        check_vma=False,
    )
```

```python
import functools

import jax
import jax.numpy as jnp
from jax import lax
from jax.experimental import pallas as pl
from jax.experimental.pallas import tpu as pltpu
from jax.sharding import PartitionSpec as P

F32 = jnp.float32
BF16 = jnp.bfloat16
EB = 512
NT = (((1,), (1,)), ((), ()))
TN = (((0,), (0,)), ((), ()))


def vmem():
    return pl.BlockSpec(memory_space=pltpu.VMEM)


def smem():
    return pl.BlockSpec(memory_space=pltpu.SMEM)


def params(mib):
    return pltpu.CompilerParams(vmem_limit_bytes=mib * 2**20)


def cost(flops, moved):
    return pl.CostEstimate(flops=flops, bytes_accessed=moved, transcendentals=0)


def pinned(arr):
    return pltpu.with_memory_space_constraint(arr, pltpu.HBM)


def hbm():
    return pl.BlockSpec(memory_space=pltpu.HBM)


def cast_kernel(in_ref, a_ref, b_ref, held, sems):
    half = a_ref.shape[0]
    outs = (a_ref, b_ref)
    copies = fetch(sems, [(in_ref.at[pl.ds(i * half, half)], held.at[i]) for i in range(2)])
    for i in range(2):
        copies[i].wait()
        outs[i][...] = held[i].astype(BF16)


def cast_halves(emb_rows):
    tabs, rows, emb = emb_rows.shape
    half = (tabs // 2, rows, emb)
    return pl.pallas_call(
        cast_kernel,
        in_specs=[hbm()],
        out_specs=[vmem()] * 2,
        out_shape=[jax.ShapeDtypeStruct(half, BF16)] * 2,
        scratch_shapes=[pltpu.VMEM((2,) + half, F32), pltpu.SemaphoreType.DMA((2,))],
        compiler_params=params(16),
        cost_estimate=cost(1 << 18, 3 << 19),
        name="cast",
    )(pinned(emb_rows))


def counts_kernel(mine_ref, ids_ref, own_ref, *refs, first_table):
    step = pl.program_id(0)
    t = step + first_table
    if first_table:
        edges_ref, out_ref, turned_ref, acc_ref, ids, own, sems = refs
    else:
        out_ref, turned_ref, edges_ref, acc_ref, ids, own, sems = refs
    samp, rows = acc_ref.shape
    tabs, entries = own.shape
    mine = mine_ref[0]
    low = mine * samp
    turn = mine * (rows // 4)

    @pl.when(step == 0)
    def _():
        copies = fetch(sems, [(own_ref, own), (ids_ref, ids)])
        copies[0].wait()
        if not first_table:
            owners = own[...]
            first = jnp.sum((owners < low).astype(jnp.int32), axis=1, keepdims=True)
            last = jnp.sum((owners < low + samp).astype(jnp.int32), axis=1, keepdims=True)
            for i in range(tabs):
                edges_ref[i] = first[i, 0]
                edges_ref[tabs + i] = last[i, 0]
        copies[1].wait()

    start = edges_ref[t] // 128
    steps = (edges_ref[tabs + t] - start * 128 + EB - 1) // EB
    start = jnp.minimum(start, (entries - steps * EB) // 128)
    acc_ref[...] = jnp.zeros_like(acc_ref)
    grid = lax.broadcasted_iota(jnp.int32, (samp, EB), 0).astype(F32).astype(BF16)
    one, zero = jnp.ones((), BF16), jnp.zeros((), BF16)

    def body(block, carry):
        at = pl.ds(pl.multiple_of(start * 128 + block * EB, 128), EB)
        who = own[pl.ds(t, 1), at] - low
        row = (ids[pl.ds(t, 1), at] - turn) & (rows - 1)
        hot = [
            jnp.where(grid == values.astype(F32).astype(BF16), one, zero) for values in (who, row, row - samp)
        ]
        acc_ref[...] += lax.dot_general(
            hot[0], jnp.concatenate(hot[1:], axis=0), NT, preferred_element_type=F32
        )
        return carry

    lax.fori_loop(0, steps, body, 0)
    total = acc_ref[...].astype(BF16)
    out_ref[0] = total
    turned_ref[0] = total.T


def make_counts(mine, ids, owners, samp, rows, side, edges=None):
    tabs, entries = ids.shape
    assert rows == 2 * samp and samp <= 256
    half = tabs // 2
    first = edges is None
    out_specs = [
        pl.BlockSpec((1, samp, rows), lambda t: (t, 0, 0)),
        pl.BlockSpec((1, rows, samp), lambda t: (t, 0, 0)),
    ]
    out_shape = [pltpu.HBM((half, samp, rows), BF16), pltpu.HBM((half, rows, samp), BF16)]
    if first:
        out_specs.append(smem())
        out_shape.append(jax.ShapeDtypeStruct((2 * tabs,), jnp.int32))
    return pl.pallas_call(
        functools.partial(counts_kernel, first_table=half * side),
        grid=(half,),
        in_specs=[smem(), hbm(), hbm()] + ([] if first else [smem()]),
        out_specs=out_specs,
        out_shape=out_shape,
        scratch_shapes=[
            pltpu.VMEM((samp, rows), F32),
            pltpu.VMEM((tabs, entries), jnp.int32),
            pltpu.VMEM((tabs, entries), jnp.int32),
            pltpu.SemaphoreType.DMA((2,)),
        ],
        compiler_params=params(16),
        cost_estimate=cost(half * samp * rows * 3072, 3 << 20),
        name="counts",
    )(mine, pinned(ids), pinned(owners), *([] if first else [edges]))


WIDE = 512


def fetch(sems, pairs):
    copies = [pltpu.make_async_copy(src, dst, sems.at[i]) for i, (src, dst) in enumerate(pairs)]
    for copy in copies:
        copy.start()
    return copies


def features(f):
    return pl.ds(f * WIDE, WIDE)


def emit(core_ref, z, g, keep_ref, send_ref):
    even = core_ref[0] == 0
    keep_ref[...] = jnp.where(even, z, g)
    send_ref[...] = jnp.where(even, g, z).astype(BF16)


def anyspace():
    return pl.BlockSpec(memory_space=pl.ANY)


def first_kernel(core_ref, counts_a, counts_b, *refs):
    embs, refs = refs[:8], refs[8:]
    (cot_ref, v_ref, u_ref, pooled_ref, keep_ref, send_ref, counts, cot, v, u, sems) = refs
    steps = counts.shape[0]
    pairs = []
    for f in range(steps):
        pairs += [
            ((counts_a, counts_b)[2 * f // steps].at[pl.ds(2 * f % steps, 2)], counts.at[f]),
            (cot_ref.at[:, features(f)], cot.at[f]),
            (v_ref.at[0, features(f), :], v.at[f]),
            (u_ref.at[1, :, features(f)], u.at[f]),
        ]
    copies = fetch(sems, pairs)
    z = g = None
    for f in range(steps):
        for copy in copies[4 * f : 4 * f + 4]:
            copy.wait()
        parts = []
        for i in range(2):
            half, at = divmod(2 * f + i, steps)
            rows = jnp.concatenate([embs[2 * k + half][at] for k in range(4)], axis=0)
            parts.append(jnp.dot(counts[f, i], rows, preferred_element_type=F32).astype(BF16))
        pooled = jnp.concatenate(parts, axis=1)
        pooled_ref[:, f * WIDE : (f + 1) * WIDE] = pooled
        wide = (cot[f].astype(F32) * pooled.astype(F32)).astype(BF16)
        more_z = jnp.dot(pooled, v[f], preferred_element_type=F32)
        more_g = lax.dot_general(wide, u[f], NT, preferred_element_type=F32)
        z, g = (more_z, more_g) if f == 0 else (z + more_z, g + more_g)
    emit(core_ref, z, g, keep_ref, send_ref)


def first_sums(core, counts, embs, cot, v, u):
    half, samp, rows = counts[0].shape
    tabs = 2 * half
    emb = embs[0].shape[-1]
    rank = v.shape[-1]
    steps = tabs * emb // WIDE
    assert 2 * emb == WIDE and steps == tabs // 2
    return pl.pallas_call(
        first_kernel,
        in_specs=[smem(), hbm(), hbm()] + [vmem()] * 8 + [hbm()] * 3,
        out_specs=[vmem()] * 3,
        out_shape=[
            jax.ShapeDtypeStruct((samp, tabs * emb), BF16),
            jax.ShapeDtypeStruct((samp, rank), F32),
            jax.ShapeDtypeStruct((samp, rank), BF16),
        ],
        scratch_shapes=[
            pltpu.VMEM((steps, 2, samp, rows), BF16),
            pltpu.VMEM((steps, samp, WIDE), BF16),
            pltpu.VMEM((steps, WIDE, rank), BF16),
            pltpu.VMEM((steps, rank, WIDE), BF16),
            pltpu.SemaphoreType.DMA((4 * steps,)),
        ],
        compiler_params=params(24),
        cost_estimate=cost(3 << 29, 10 << 20),
        name="first_sums",
    )(core, *map(pinned, counts), *embs, pinned(cot), pinned(v), pinned(u))


def to_core(arr):
    return lax.ppermute(arr, "c", [(0, 1), (1, 0)])


def small(kernel, out_shape, name, *args):
    return pl.pallas_call(
        kernel,
        in_specs=[vmem()] * len(args),
        out_specs=vmem(),
        out_shape=out_shape,
        compiler_params=params(8),
        cost_estimate=cost(1 << 20, 1 << 20),
        name=name,
    )(*args)


def chunk_at(i):
    return 16 * (i // 2), 256 * (i % 2)


def cut_kernel(keep_ref, got_ref, out_ref):
    for i in range(out_ref.shape[0]):
        r, c = chunk_at(i)
        at = (slice(r, r + 16), slice(c, c + 256))
        out_ref[i] = (keep_ref[at] + got_ref[at].astype(F32)).astype(BF16)


def total_kernel(in_ref, out_ref):
    total = in_ref[0].astype(F32)
    for i in range(1, in_ref.shape[0]):
        total = total + in_ref[i].astype(F32)
    total = total.astype(BF16)
    for i in range(out_ref.shape[0]):
        out_ref[i] = total


def exchange(chunks, copies):
    parts = lax.all_to_all(chunks, ("x", "z"), 0, 0, tiled=True)
    return small(total_kernel, jax.ShapeDtypeStruct((copies, 16, 256), BF16), "total", parts)


def sum_by_gather(keep, send):
    chunks = small(cut_kernel, jax.ShapeDtypeStruct((32, 16, 256), BF16), "cut", keep, to_core(send))
    mine = lax.all_gather(exchange(chunks, 1), ("x", "z"), axis=0, tiled=True)
    return mine, to_core(mine)


def sum_by_psum(keep, send):
    chunks = small(cut_kernel, jax.ShapeDtypeStruct((32, 16, 256), BF16), "cut", keep, to_core(send))
    mine = lax.psum(chunks, ("x", "z"))
    return mine, to_core(mine)


def spread(core_ref, mine_ref, other_ref, in_ref):
    core = core_ref[0]
    for side, ref in ((core, mine_ref), (1 - core, other_ref)):
        for i in range(32):
            r, c = chunk_at(i)
            in_ref[side, r : r + 16, c : c + 256] = ref[i]


def middle_kernel(core_ref, mine_ref, other_ref, b_ref, pooled_ref, cot_ref, u_ref, v_ref, *refs):
    x1_ref, a_ref, keep_ref, send_ref, sums, pooled, cot, u, v, sems = refs
    steps = u.shape[0]
    pairs = []
    for f in range(steps):
        pairs += [
            (u_ref.at[0, :, features(f)], u.at[f]),
            (v_ref.at[1, features(f), :], v.at[f]),
            (pooled_ref.at[:, features(f)], pooled.at[f]),
            (cot_ref.at[:, features(f)], cot.at[f]),
        ]
    copies = fetch(sems, pairs)
    spread(core_ref, mine_ref, other_ref, sums)
    z = g = None
    for f in range(steps):
        for copy in copies[4 * f : 4 * f + 4]:
            copy.wait()
        at = slice(f * WIDE, (f + 1) * WIDE)
        base = pooled[f].astype(F32)
        h0 = jnp.dot(sums[0], u[f], preferred_element_type=F32) + b_ref[0:1, at]
        x1 = (base * h0 + base).astype(BF16)
        x1_ref[:, at] = x1
        g1 = cot[f].astype(F32) + lax.dot_general(sums[1], v[f], NT, preferred_element_type=F32)
        a_ref[:, at] = (g1 * h0 + g1).astype(BF16)
        wide = (g1 * base).astype(BF16)
        more_z = jnp.dot(x1, v[f], preferred_element_type=F32)
        more_g = lax.dot_general(wide, u[f], NT, preferred_element_type=F32)
        z, g = (more_z, more_g) if f == 0 else (z + more_z, g + more_g)
    emit(core_ref, z, g, keep_ref, send_ref)


def middle(core, mine, other, bias, pooled, cot, u, v):
    samp, feats = pooled.shape
    rank = v.shape[-1]
    steps = feats // WIDE
    feat = jax.ShapeDtypeStruct((samp, feats), BF16)
    return pl.pallas_call(
        middle_kernel,
        in_specs=[smem()] + [vmem()] * 3 + [anyspace()] + [hbm()] * 3,
        out_specs=[vmem()] * 4,
        out_shape=[feat, feat, jax.ShapeDtypeStruct((samp, rank), F32), jax.ShapeDtypeStruct((samp, rank), BF16)],
        scratch_shapes=[
            pltpu.VMEM((2, samp, rank), BF16),
            pltpu.VMEM((steps, samp, WIDE), BF16),
            pltpu.VMEM((steps, samp, WIDE), BF16),
            pltpu.VMEM((steps, rank, WIDE), BF16),
            pltpu.VMEM((steps, WIDE, rank), BF16),
            pltpu.SemaphoreType.DMA((4 * steps,)),
        ],
        compiler_params=params(24),
        cost_estimate=cost(1 << 31, 8 << 20),
        name="middle",
    )(core, mine, other, bias, pooled, pinned(cot), pinned(u), pinned(v))


def last_kernel(core_ref, mine_ref, other_ref, b_ref, turned_ref, pooled_ref, cot_ref, x1_ref, a_ref, u_ref, v_ref, *refs, side):
    crossed_ref, p0, p1, p2, p3, sums, turned, pooled, cot, x1, a, u, v, crossed, sems = refs[-15:]
    steps = u.shape[0]
    pairs = []
    for f in range(steps):
        from_f = features(side * steps + f)
        pairs += [
            (u_ref.at[1, :, from_f], u.at[f]),
            (v_ref.at[0, from_f, :], v.at[f]),
            (pooled_ref.at[:, from_f], pooled.at[f]),
            (cot_ref.at[:, from_f], cot.at[f]),
            (x1_ref.at[:, from_f], x1.at[f]),
            (a_ref.at[:, from_f], a.at[f]),
            (turned_ref.at[pl.ds(2 * f, 2)], turned.at[f]),
        ]
    n = len(pairs) // steps
    copies = fetch(sems, pairs)
    spread(core_ref, mine_ref, other_ref, sums)
    outs = []
    rows, emb = p0.shape[1:]
    for f in range(steps):
        for copy in copies[n * f : n * f + n]:
            copy.wait()
        at = slice((side * steps + f) * WIDE, (side * steps + f + 1) * WIDE)
        h1 = jnp.dot(sums[0], u[f], preferred_element_type=F32) + b_ref[1:2, at]
        crossed[f] = (pooled[f].astype(F32) * h1 + x1[f].astype(F32)).astype(BF16)
        out = pltpu.make_async_copy(
            crossed.at[f], crossed_ref.at[:, features(side * steps + f)], sems.at[n * steps + f]
        )
        out.start()
        outs.append(out)
        grad = cot[f].astype(F32) * h1 + a[f].astype(F32)
        grad = (grad + lax.dot_general(sums[1], v[f], NT, preferred_element_type=F32)).astype(BF16)
        for i in range(2):
            part = jnp.dot(turned[f, i], grad[:, i * emb : (i + 1) * emb], preferred_element_type=F32)
            p0[2 * f + i] = part[:rows]
            for k, ref in enumerate((p1, p2, p3)):
                ref[2 * f + i] = part[(k + 1) * rows : (k + 2) * rows].astype(BF16)
    for out in outs:
        out.wait()


def last(side, before, core, mine, other, bias, turned, pooled, cot, x1, a, u, v):
    half, rows, samp = turned.shape
    rank = v.shape[-1]
    emb = pooled.shape[1] // (2 * half)
    steps = pooled.shape[1] // WIDE // 2
    block = (half, rows // 4, emb)
    feat = pltpu.VMEM((steps, samp, WIDE), BF16)
    args = (core, mine, other, bias, pinned(turned), pooled, pinned(cot), x1, a, pinned(u), pinned(v), *before)
    return pl.pallas_call(
        functools.partial(last_kernel, side=side),
        in_specs=[smem()] + [vmem()] * 3 + [hbm(), anyspace(), hbm(), anyspace(), anyspace(), hbm(), hbm()] + [anyspace()] * len(before),
        out_specs=[anyspace()] + [vmem()] * 4,
        out_shape=[jax.ShapeDtypeStruct(pooled.shape, BF16), jax.ShapeDtypeStruct(block, F32)]
        + [jax.ShapeDtypeStruct(block, BF16)] * 3,
        scratch_shapes=[
            pltpu.VMEM((2, samp, rank), BF16),
            pltpu.VMEM((steps, 2, rows, samp), BF16),
            feat,
            feat,
            feat,
            feat,
            pltpu.VMEM((steps, rank, WIDE), BF16),
            pltpu.VMEM((steps, WIDE, rank), BF16),
            feat,
            pltpu.SemaphoreType.DMA((8 * steps,)),
        ],
        input_output_aliases={11: 0} if before else {},
        compiler_params=params(24),
        cost_estimate=cost(3 << 28, 7 << 20),
        name="last",
    )(*args)


def right(arr):
    return lax.ppermute(arr, "row", [(i, (i + 1) & 3) for i in range(4)])


def left(arr):
    return lax.ppermute(arr, "row", [(i, (i + 3) & 3) for i in range(4)])


def add(a, b):
    return a.astype(F32) + b.astype(F32)


def scalar(axis):
    return lax.axis_index(axis).astype(jnp.int32).reshape(1)


def local(emb_rows, entry_ids, entry_sample, cross_v, cross_u, cross_bias, cotangent):
    samp = cotangent.shape[0]
    rows = emb_rows.shape[1] * lax.axis_size("row")
    mine, core = scalar("row"), scalar("c")
    own_a, own_b = cast_halves(emb_rows)
    left_a, right_b = right(own_a), left(own_b)
    left_b, right_a = right(own_b), left(own_a)
    counts_a, turned_a, edges = make_counts(mine, entry_ids, entry_sample, samp, rows, 0)
    left_a, right_b, edges = lax.optimization_barrier((left_a, right_b, edges))
    far_a, far_b = right(left_a), left(right_b)
    counts_b, turned_b = make_counts(mine, entry_ids, entry_sample, samp, rows, 1, edges)
    embs = (own_a, own_b, right_a, right_b, far_a, far_b, left_a, left_b)
    pooled, keep, send = first_sums(core, (counts_a, counts_b), embs, cotangent, cross_v, cross_u)
    sums = sum_by_gather(keep, send)
    x1, a, keep, send = middle(core, *sums, cross_bias, pooled, cotangent, cross_u, cross_v)
    sums = sum_by_psum(keep, send)
    front = (core, *sums, cross_bias)
    rest = (pooled, cotangent, x1, a, cross_u, cross_v)
    crossed, p0a, p1a, p2a, p3a = last(0, (), *front, turned_a, *rest)
    from_left, sum_a = lax.optimization_barrier((right(p2a), left(p3a)))
    crossed, p0b, p1b, p2b, p3b = last(1, (crossed,), *front, turned_b, *rest)
    from_right, sum_b = lax.optimization_barrier((left(p2b), right(p1b)))
    far_a = right(add(p1a, from_left).astype(BF16))
    far_b = left(add(p3b, from_right).astype(BF16))
    grads = jnp.concatenate([p0a + add(sum_a, far_a), p0b + add(sum_b, far_b)], axis=0)
    return crossed, grads


def solution(mesh):
    fine = jax.sharding.Mesh(mesh.devices.reshape(4, 8, 2, 4), ("x", "z", "c", "row"))
    table = ("x", "z", "c")
    placed = (
        P(table, "row", None),
        P(table, None),
        P(table, None),
        P(None, table, None),
        P(None, None, table),
        P(None, table),
        P("row", table),
    )
    return jax.shard_map(
        local,
        mesh=fine,
        in_specs=placed,
        out_specs=(P("row", table), P(table, "row", None)),
        check_vma=False,
    )
```

```python
import functools

import jax
import jax.numpy as jnp
from jax import lax
from jax.experimental import pallas as pl
from jax.experimental.pallas import tpu as pltpu
from jax.sharding import PartitionSpec as P

F32 = jnp.float32
BF16 = jnp.bfloat16
EB = 512
NT = (((1,), (1,)), ((), ()))
TN = (((0,), (0,)), ((), ()))


def vmem():
    return pl.BlockSpec(memory_space=pltpu.VMEM)


def smem():
    return pl.BlockSpec(memory_space=pltpu.SMEM)


def params(mib):
    return pltpu.CompilerParams(vmem_limit_bytes=mib * 2**20)


def cost(flops, moved):
    return pl.CostEstimate(flops=flops, bytes_accessed=moved, transcendentals=0)


def pinned(arr):
    return pltpu.with_memory_space_constraint(arr, pltpu.HBM)


def kept(*arrs):
    return [pltpu.with_memory_space_constraint(arr, pltpu.VMEM) for arr in arrs]


def hbm():
    return pl.BlockSpec(memory_space=pltpu.HBM)


def cast_kernel(in_ref, a_ref, b_ref, held, sems):
    half = a_ref.shape[0]
    outs = (a_ref, b_ref)
    copies = fetch(sems, [(in_ref.at[pl.ds(i * half, half)], held.at[i]) for i in range(2)])
    for i in range(2):
        copies[i].wait()
        outs[i][...] = held[i].astype(BF16)


def cast_halves(emb_rows):
    tabs, rows, emb = emb_rows.shape
    half = (tabs // 2, rows, emb)
    return pl.pallas_call(
        cast_kernel,
        in_specs=[hbm()],
        out_specs=[vmem()] * 2,
        out_shape=[pltpu.VMEM(half, BF16)] * 2,
        scratch_shapes=[pltpu.VMEM((2,) + half, F32), pltpu.SemaphoreType.DMA((2,))],
        compiler_params=params(16),
        cost_estimate=cost(1 << 18, 3 << 19),
        name="cast",
    )(pinned(emb_rows))


def counts_kernel(mine_ref, ids_ref, own_ref, *refs, first_table):
    if first_table:
        edges_ref, *loads, out_ref, turned_ref = refs[: (len(refs) - 1) // 2]
        loaded, (acc_ref, ids, own, sems) = refs[len(loads) + 3 : -4], refs[-4:]
    else:
        out_ref, turned_ref, edges_ref, acc_ref, ids, own, sems = refs
        loads = loaded = ()
    samp, rows = acc_ref.shape
    tabs, entries = own.shape
    mine = mine_ref[0]
    low = mine * samp
    turn = mine * (rows // 4)
    copies = fetch(sems, [(own_ref, own), (ids_ref, ids), *zip(loads, loaded)])
    copies[0].wait()
    if not first_table:
        owners = own[...]
        first = jnp.sum((owners < low).astype(jnp.int32), axis=1, keepdims=True)
        last = jnp.sum((owners < low + samp).astype(jnp.int32), axis=1, keepdims=True)
        for i in range(tabs):
            edges_ref[i] = first[i, 0]
            edges_ref[tabs + i] = last[i, 0]
    copies[1].wait()
    grid = lax.broadcasted_iota(jnp.int32, (samp, EB), 0).astype(F32).astype(BF16)
    one, zero = jnp.ones((), BF16), jnp.zeros((), BF16)

    @pl.loop(0, out_ref.shape[0])
    def _(i):
        t = i + first_table
        start = edges_ref[t] // 128
        steps = (edges_ref[tabs + t] - start * 128 + EB - 1) // EB
        start = jnp.minimum(start, (entries - steps * EB) // 128)
        acc_ref[...] = jnp.zeros_like(acc_ref)

        def body(block, carry):
            at = pl.ds(pl.multiple_of(start * 128 + block * EB, 128), EB)
            who = own[pl.ds(t, 1), at] - low
            row = (ids[pl.ds(t, 1), at] - turn) & (rows - 1)
            hot = [
                jnp.where(grid == values.astype(F32).astype(BF16), one, zero) for values in (who, row, row - samp)
            ]
            acc_ref[...] += lax.dot_general(
                hot[0], jnp.concatenate(hot[1:], axis=0), NT, preferred_element_type=F32
            )
            return carry

        lax.fori_loop(0, steps, body, 0)
        total = acc_ref[...].astype(BF16)
        out_ref[i] = total
        turned_ref[i] = total.T

    for copy in copies[2:]:
        copy.wait()


def make_counts(mine, ids, owners, samp, rows, edges=None, loads=()):
    tabs, entries = ids.shape
    assert rows == 2 * samp and samp <= 256
    half = tabs // 2
    first = edges is None
    out_shape = [pltpu.VMEM((half, samp, rows), BF16), pltpu.VMEM((half, rows, samp), BF16)]
    if first:
        out_specs = [vmem(), vmem(), smem()]
        out_shape.append(jax.ShapeDtypeStruct((2 * tabs,), jnp.int32))
    else:
        out_specs = [vmem()] * (2 + len(loads))
        out_shape += [pltpu.VMEM(arr.shape, arr.dtype) for arr in loads]
    return pl.pallas_call(
        functools.partial(counts_kernel, first_table=0 if first else half),
        in_specs=[smem(), hbm(), hbm()] + ([] if first else [smem()] + [hbm()] * len(loads)),
        out_specs=out_specs,
        out_shape=out_shape,
        scratch_shapes=[
            pltpu.VMEM((samp, rows), F32),
            pltpu.VMEM((tabs, entries), jnp.int32),
            pltpu.VMEM((tabs, entries), jnp.int32),
            pltpu.SemaphoreType.DMA((2 + len(loads),)),
        ],
        compiler_params=params(16),
        cost_estimate=cost(half * samp * rows * 3072, 3 << 20),
        name="counts",
    )(mine, pinned(ids), pinned(owners), *([] if first else [edges, *map(pinned, loads)]))


WIDE = 512


def fetch(sems, pairs):
    copies = [pltpu.make_async_copy(src, dst, sems.at[i]) for i, (src, dst) in enumerate(pairs)]
    for copy in copies:
        copy.start()
    return copies


def emit(core_ref, z, g, keep_ref, send_ref):
    even = core_ref[0] == 0
    keep_ref[...] = jnp.where(even, z, g)
    send_ref[...] = jnp.where(even, g, z).astype(BF16)


def anyspace():
    return pl.BlockSpec(memory_space=pl.ANY)


def first_kernel(core_ref, counts_a, counts_b, *refs):
    embs, (cot, v, u, pooled_ref, keep_ref, send_ref) = refs[:8], refs[8:]
    half = counts_a.shape[0]
    z = g = None
    for f in range(half):
        parts = []
        for t in (2 * f, 2 * f + 1):
            side, at = divmod(t, half)
            rows = jnp.concatenate([embs[2 * k + side][at] for k in range(4)], axis=0)
            parts.append(jnp.dot((counts_a, counts_b)[side][at], rows, preferred_element_type=F32).astype(BF16))
        pooled = jnp.concatenate(parts, axis=1)
        at = slice(f * WIDE, (f + 1) * WIDE)
        pooled_ref[:, at] = pooled
        wide = (cot[:, at].astype(F32) * pooled.astype(F32)).astype(BF16)
        more_z = jnp.dot(pooled, v[0, at, :], preferred_element_type=F32)
        more_g = lax.dot_general(wide, u[1, :, at], NT, preferred_element_type=F32)
        z, g = (more_z, more_g) if f == 0 else (z + more_z, g + more_g)
    emit(core_ref, z, g, keep_ref, send_ref)


def first_sums(core, counts, embs, cot, v, u):
    half, samp, rows = counts[0].shape
    emb = embs[0].shape[-1]
    rank = v.shape[-1]
    assert 2 * emb == WIDE
    return pl.pallas_call(
        first_kernel,
        in_specs=[smem()] + [vmem()] * 13,
        out_specs=[vmem()] * 3,
        out_shape=[
            pltpu.VMEM((samp, 2 * half * emb), BF16),
            pltpu.VMEM((samp, rank), F32),
            pltpu.VMEM((samp, rank), BF16),
        ],
        compiler_params=params(16),
        cost_estimate=cost(3 << 29, 10 << 20),
        name="first_sums",
    )(core, *kept(*counts), *embs, *kept(cot, v, u))


def swap(arr, axis):
    return lax.ppermute(arr, axis, [(0, 1), (1, 0)])


def small(kernel, out_shape, name, *args):
    return pl.pallas_call(
        kernel,
        in_specs=[vmem()] * len(args),
        out_specs=jax.tree.map(lambda _: vmem(), out_shape),
        out_shape=out_shape,
        compiler_params=params(8),
        cost_estimate=cost(1 << 20, 1 << 20),
        name=name,
    )(*args)


CHUNKS = 16
CHUNK = (32, 256)


def chunk_at(i):
    r, c = CHUNK[0] * (i // 2), CHUNK[1] * (i % 2)
    return slice(r, r + CHUNK[0]), slice(c, c + CHUNK[1])


def cut_kernel(keep_ref, got_ref, out_ref):
    for i in range(CHUNKS):
        at = chunk_at(i)
        out_ref[i] = (keep_ref[at] + got_ref[at].astype(F32)).astype(BF16)


def total_kernel(in_ref, keep_ref, send_ref):
    total = in_ref[0].astype(F32)
    for i in range(1, CHUNKS):
        total = total + in_ref[i].astype(F32)
    keep_ref[...] = total
    send_ref[...] = total.astype(BF16)


def copies_kernel(keep_ref, got_ref, out_ref):
    total = (keep_ref[...] + got_ref[...].astype(F32)).astype(BF16)
    for i in range(CHUNKS):
        out_ref[i] = total


def sum_all(keep, send):
    among = ("x", "zh")
    shape = pltpu.VMEM((CHUNKS,) + CHUNK, BF16)
    chunks = small(cut_kernel, shape, "cut", keep, swap(send, "c"))
    parts = lax.all_to_all(chunks, among, 0, 0, tiled=True)
    keep, send = small(total_kernel, [pltpu.VMEM(CHUNK, F32), pltpu.VMEM(CHUNK, BF16)], "total", parts)
    copies = small(copies_kernel, shape, "copies", keep, swap(send, "zl"))
    mine = lax.all_to_all(copies, among, 0, 0, tiled=True)
    return mine, swap(mine, "c")


def spread(core_ref, mine_ref, other_ref, in_ref):
    core = core_ref[0]
    for side, ref in ((core, mine_ref), (1 - core, other_ref)):
        for i in range(CHUNKS):
            in_ref[(side, *chunk_at(i))] = ref[i]


def middle_kernel(core_ref, mine_ref, other_ref, b_ref, pooled, cot, u_ref, v_ref, x1_ref, a_ref, keep_ref, send_ref, sums):
    spread(core_ref, mine_ref, other_ref, sums)
    z = g = None
    for f in range(pooled.shape[1] // WIDE):
        at = slice(f * WIDE, (f + 1) * WIDE)
        u, v = u_ref[0, :, at], v_ref[1, at, :]
        base = pooled[:, at].astype(F32)
        h0 = jnp.dot(sums[0], u, preferred_element_type=F32) + b_ref[0:1, at]
        x1 = (base * h0 + base).astype(BF16)
        x1_ref[:, at] = x1
        g1 = cot[:, at].astype(F32) + lax.dot_general(sums[1], v, NT, preferred_element_type=F32)
        a_ref[:, at] = (g1 * h0 + g1).astype(BF16)
        wide = (g1 * base).astype(BF16)
        more_z = jnp.dot(x1, v, preferred_element_type=F32)
        more_g = lax.dot_general(wide, u, NT, preferred_element_type=F32)
        z, g = (more_z, more_g) if f == 0 else (z + more_z, g + more_g)
    emit(core_ref, z, g, keep_ref, send_ref)


def middle(core, mine, other, bias, pooled, cot, u, v):
    samp, feats = pooled.shape
    rank = v.shape[-1]
    feat = pltpu.VMEM((samp, feats), BF16)
    return pl.pallas_call(
        middle_kernel,
        in_specs=[smem()] + [vmem()] * 7,
        out_specs=[vmem()] * 4,
        out_shape=[feat, feat, pltpu.VMEM((samp, rank), F32), pltpu.VMEM((samp, rank), BF16)],
        scratch_shapes=[pltpu.VMEM((2, samp, rank), BF16)],
        compiler_params=params(16),
        cost_estimate=cost(1 << 31, 8 << 20),
        name="middle",
    )(core, mine, other, bias, *kept(pooled, cot, u, v))


def last_kernel(core_ref, mine_ref, other_ref, b_ref, turned, pooled, cot, x1, a, u_ref, v_ref, *refs, side):
    crossed_ref, p0, p1, p2, p3, sums, crossed, sems = refs[-8:]
    steps = crossed.shape[0]
    spread(core_ref, mine_ref, other_ref, sums)
    outs = []
    rows, emb = p0.shape[1:]
    for f in range(steps):
        at = slice((side * steps + f) * WIDE, (side * steps + f + 1) * WIDE)
        h1 = jnp.dot(sums[0], u_ref[1, :, at], preferred_element_type=F32) + b_ref[1:2, at]
        crossed[f] = (pooled[:, at].astype(F32) * h1 + x1[:, at].astype(F32)).astype(BF16)
        out = pltpu.make_async_copy(crossed.at[f], crossed_ref.at[:, at], sems.at[f])
        out.start()
        outs.append(out)
        grad = cot[:, at].astype(F32) * h1 + a[:, at].astype(F32)
        grad = (grad + lax.dot_general(sums[1], v_ref[0, at, :], NT, preferred_element_type=F32)).astype(BF16)
        for i in range(2):
            part = jnp.dot(turned[2 * f + i], grad[:, i * emb : (i + 1) * emb], preferred_element_type=F32)
            p0[2 * f + i] = part[:rows]
            for k, ref in enumerate((p1, p2, p3)):
                ref[2 * f + i] = part[(k + 1) * rows : (k + 2) * rows].astype(BF16)
    for out in outs:
        out.wait()


def last(side, before, core, mine, other, bias, turned, pooled, cot, x1, a, u, v):
    half, rows, samp = turned.shape
    rank = v.shape[-1]
    emb = pooled.shape[1] // (2 * half)
    steps = pooled.shape[1] // WIDE // 2
    block = (half, rows // 4, emb)
    args = (core, mine, other, bias, *kept(turned, pooled, cot, x1, a, u, v), *before)
    return pl.pallas_call(
        functools.partial(last_kernel, side=side),
        in_specs=[smem()] + [vmem()] * 10 + [anyspace()] * len(before),
        out_specs=[anyspace()] + [vmem()] * 4,
        out_shape=[pltpu.HBM(pooled.shape, BF16), pltpu.VMEM(block, F32)] + [pltpu.VMEM(block, BF16)] * 3,
        scratch_shapes=[
            pltpu.VMEM((2, samp, rank), BF16),
            pltpu.VMEM((steps, samp, WIDE), BF16),
            pltpu.SemaphoreType.DMA((steps,)),
        ],
        input_output_aliases={11: 0} if before else {},
        compiler_params=params(16),
        cost_estimate=cost(3 << 28, 7 << 20),
        name="last",
    )(*args)


def right(arr):
    return lax.ppermute(arr, "row", [(i, (i + 1) & 3) for i in range(4)])


def left(arr):
    return lax.ppermute(arr, "row", [(i, (i + 3) & 3) for i in range(4)])


def add(a, b):
    return a.astype(F32) + b.astype(F32)


def scalar(axis):
    return lax.axis_index(axis).astype(jnp.int32).reshape(1)


def local(emb_rows, entry_ids, entry_sample, cross_v, cross_u, cross_bias, cotangent):
    samp = cotangent.shape[0]
    rows = emb_rows.shape[1] * lax.axis_size("row")
    mine, core = scalar("row"), scalar("c")
    own_a, own_b = cast_halves(emb_rows)
    left_a, right_b = right(own_a), left(own_b)
    left_b, right_a = right(own_b), left(own_a)
    counts_a, turned_a, edges = make_counts(mine, entry_ids, entry_sample, samp, rows)
    left_a, right_b, edges = lax.optimization_barrier((left_a, right_b, edges))
    far_a, far_b = right(left_a), left(right_b)
    loads = (cotangent, cross_v, cross_u)
    counts_b, turned_b, cot, v, u = make_counts(mine, entry_ids, entry_sample, samp, rows, edges, loads)
    embs = (own_a, own_b, right_a, right_b, far_a, far_b, left_a, left_b)
    pooled, keep, send = first_sums(core, (counts_a, counts_b), embs, cot, v, u)
    sums = sum_all(keep, send)
    x1, a, keep, send = middle(core, *sums, cross_bias, pooled, cot, u, v)
    sums = sum_all(keep, send)
    front = (core, *sums, cross_bias)
    rest = (pooled, cot, x1, a, u, v)
    crossed, p0a, p1a, p2a, p3a = last(0, (), *front, turned_a, *rest)
    from_left, sum_a = lax.optimization_barrier((right(p2a), left(p3a)))
    crossed, p0b, p1b, p2b, p3b = last(1, (crossed,), *front, turned_b, *rest)
    from_right, sum_b = lax.optimization_barrier((left(p2b), right(p1b)))
    far_a = right(add(p1a, from_left).astype(BF16))
    far_b = left(add(p3b, from_right).astype(BF16))
    grads = jnp.concatenate([p0a + add(sum_a, far_a), p0b + add(sum_b, far_b)], axis=0)
    return crossed, grads


def solution(mesh):
    fine = jax.sharding.Mesh(mesh.devices.reshape(4, 4, 2, 2, 4), ("x", "zh", "zl", "c", "row"))
    table = ("x", "zh", "zl", "c")
    placed = (
        P(table, "row", None),
        P(table, None),
        P(table, None),
        P(None, table, None),
        P(None, None, table),
        P(None, table),
        P("row", table),
    )
    return jax.shard_map(
        local,
        mesh=fine,
        in_specs=placed,
        out_specs=(P("row", table), P(table, "row", None)),
        check_vma=False,
    )
```

```python
import functools

import jax
import jax.numpy as jnp
from jax import lax
from jax.experimental import pallas as pl
from jax.experimental.pallas import tpu as pltpu
from jax.sharding import PartitionSpec as P

F32 = jnp.float32
BF16 = jnp.bfloat16
EB = 512
NT = (((1,), (1,)), ((), ()))
TN = (((0,), (0,)), ((), ()))


def vmem():
    return pl.BlockSpec(memory_space=pltpu.VMEM)


def smem():
    return pl.BlockSpec(memory_space=pltpu.SMEM)


def params(mib):
    return pltpu.CompilerParams(vmem_limit_bytes=mib * 2**20)


def cost(flops, moved):
    return pl.CostEstimate(flops=flops, bytes_accessed=moved, transcendentals=0)


def pinned(arr):
    return pltpu.with_memory_space_constraint(arr, pltpu.HBM)


def kept(*arrs):
    return [pltpu.with_memory_space_constraint(arr, pltpu.VMEM) for arr in arrs]


def hbm():
    return pl.BlockSpec(memory_space=pltpu.HBM)


def cast_kernel(in_ref, a_ref, b_ref, held, sems):
    half = a_ref.shape[0]
    outs = (a_ref, b_ref)
    copies = fetch(sems, [(in_ref.at[pl.ds(i * half, half)], held.at[i]) for i in range(2)])
    for i in range(2):
        copies[i].wait()
        outs[i][...] = held[i].astype(BF16)


def cast_halves(emb_rows):
    tabs, rows, emb = emb_rows.shape
    half = (tabs // 2, rows, emb)
    return pl.pallas_call(
        cast_kernel,
        in_specs=[hbm()],
        out_specs=[vmem()] * 2,
        out_shape=[pltpu.VMEM(half, BF16)] * 2,
        scratch_shapes=[pltpu.VMEM((2,) + half, F32), pltpu.SemaphoreType.DMA((2,))],
        compiler_params=params(16),
        cost_estimate=cost(1 << 18, 3 << 19),
        name="cast",
    )(pinned(emb_rows))


def counts_kernel(mine_ref, ids_ref, own_ref, *refs, first_table):
    if first_table:
        edges_ref, *loads, out_ref, turned_ref = refs[: (len(refs) - 1) // 2]
        loaded, (acc_ref, ids, own, sems) = refs[len(loads) + 3 : -4], refs[-4:]
    else:
        out_ref, turned_ref, edges_ref, acc_ref, ids, own, sems = refs
        loads = loaded = ()
    samp, rows = acc_ref.shape
    tabs, entries = own.shape
    mine = mine_ref[0]
    low = mine * samp
    turn = mine * (rows // 4)
    copies = fetch(sems, [(own_ref, own), (ids_ref, ids), *zip(loads, loaded)])
    copies[0].wait()
    if not first_table:
        owners = own[...]
        first = jnp.sum((owners < low).astype(jnp.int32), axis=1, keepdims=True)
        last = jnp.sum((owners < low + samp).astype(jnp.int32), axis=1, keepdims=True)
        for i in range(tabs):
            edges_ref[i] = first[i, 0]
            edges_ref[tabs + i] = last[i, 0]
    copies[1].wait()
    grid = lax.broadcasted_iota(jnp.int32, (samp, EB), 0).astype(F32).astype(BF16)
    one, zero = jnp.ones((), BF16), jnp.zeros((), BF16)

    @pl.loop(0, out_ref.shape[0])
    def _(i):
        t = i + first_table
        start = edges_ref[t] // 128
        steps = (edges_ref[tabs + t] - start * 128 + EB - 1) // EB
        start = jnp.minimum(start, (entries - steps * EB) // 128)
        acc_ref[...] = jnp.zeros_like(acc_ref)

        def body(block, carry):
            at = pl.ds(pl.multiple_of(start * 128 + block * EB, 128), EB)
            who = own[pl.ds(t, 1), at] - low
            row = (ids[pl.ds(t, 1), at] - turn) & (rows - 1)
            hot = [
                jnp.where(grid == values.astype(F32).astype(BF16), one, zero) for values in (who, row, row - samp)
            ]
            acc_ref[...] += lax.dot_general(
                hot[0], jnp.concatenate(hot[1:], axis=0), NT, preferred_element_type=F32
            )
            return carry

        lax.fori_loop(0, steps, body, 0)
        total = acc_ref[...].astype(BF16)
        out_ref[i] = total
        turned_ref[i] = total.T

    for copy in copies[2:]:
        copy.wait()


def make_counts(mine, ids, owners, samp, rows, edges=None, loads=()):
    tabs, entries = ids.shape
    assert rows == 2 * samp and samp <= 256
    half = tabs // 2
    first = edges is None
    out_shape = [pltpu.VMEM((half, samp, rows), BF16), pltpu.VMEM((half, rows, samp), BF16)]
    if first:
        out_specs = [vmem(), vmem(), smem()]
        out_shape.append(jax.ShapeDtypeStruct((2 * tabs,), jnp.int32))
    else:
        out_specs = [vmem()] * (2 + len(loads))
        out_shape += [pltpu.VMEM(arr.shape, arr.dtype) for arr in loads]
    return pl.pallas_call(
        functools.partial(counts_kernel, first_table=0 if first else half),
        in_specs=[smem(), hbm(), hbm()] + ([] if first else [smem()] + [hbm()] * len(loads)),
        out_specs=out_specs,
        out_shape=out_shape,
        scratch_shapes=[
            pltpu.VMEM((samp, rows), F32),
            pltpu.VMEM((tabs, entries), jnp.int32),
            pltpu.VMEM((tabs, entries), jnp.int32),
            pltpu.SemaphoreType.DMA((2 + len(loads),)),
        ],
        compiler_params=params(16),
        cost_estimate=cost(half * samp * rows * 3072, 3 << 20),
        name="counts",
    )(mine, pinned(ids), pinned(owners), *([] if first else [edges, *map(pinned, loads)]))


WIDE = 512


def fetch(sems, pairs):
    copies = [pltpu.make_async_copy(src, dst, sems.at[i]) for i, (src, dst) in enumerate(pairs)]
    for copy in copies:
        copy.start()
    return copies


def emit(core_ref, z, g, keep_ref, send_ref):
    even = core_ref[0] == 0
    keep_ref[...] = jnp.where(even, z, g)
    send_ref[...] = jnp.where(even, g, z).astype(BF16)


def anyspace():
    return pl.BlockSpec(memory_space=pl.ANY)


def first_kernel(core_ref, counts_a, counts_b, *refs):
    embs, (cot, v, u, pooled_ref, keep_ref, send_ref) = refs[:8], refs[8:]
    half = counts_a.shape[0]
    z = g = None
    for f in range(half):
        parts = []
        for t in (2 * f, 2 * f + 1):
            side, at = divmod(t, half)
            rows = jnp.concatenate([embs[2 * k + side][at] for k in range(4)], axis=0)
            parts.append(jnp.dot((counts_a, counts_b)[side][at], rows, preferred_element_type=F32).astype(BF16))
        pooled = jnp.concatenate(parts, axis=1)
        at = slice(f * WIDE, (f + 1) * WIDE)
        pooled_ref[:, at] = pooled
        wide = (cot[:, at].astype(F32) * pooled.astype(F32)).astype(BF16)
        more_z = jnp.dot(pooled, v[0, at, :], preferred_element_type=F32)
        more_g = lax.dot_general(wide, u[1, :, at], NT, preferred_element_type=F32)
        z, g = (more_z, more_g) if f == 0 else (z + more_z, g + more_g)
    emit(core_ref, z, g, keep_ref, send_ref)


def first_sums(core, counts, embs, cot, v, u):
    half, samp, rows = counts[0].shape
    emb = embs[0].shape[-1]
    rank = v.shape[-1]
    assert 2 * emb == WIDE
    return pl.pallas_call(
        first_kernel,
        in_specs=[smem()] + [vmem()] * 13,
        out_specs=[vmem()] * 3,
        out_shape=[
            pltpu.VMEM((samp, 2 * half * emb), BF16),
            pltpu.VMEM((samp, rank), F32),
            pltpu.VMEM((samp, rank), BF16),
        ],
        compiler_params=params(16),
        cost_estimate=cost(3 << 29, 10 << 20),
        name="first_sums",
    )(core, *kept(*counts), *embs, *kept(cot, v, u))


def swap(arr, axis):
    return lax.ppermute(arr, axis, [(0, 1), (1, 0)])


def small(kernel, out_shape, name, *args):
    return pl.pallas_call(
        kernel,
        in_specs=[vmem()] * len(args),
        out_specs=jax.tree.map(lambda _: vmem(), out_shape),
        out_shape=out_shape,
        compiler_params=params(8),
        cost_estimate=cost(1 << 20, 1 << 20),
        name=name,
    )(*args)


CHUNKS = 8
CHUNK = (32, 512)


def chunk_at(i):
    return slice(CHUNK[0] * i, CHUNK[0] * (i + 1)), slice(None)


def cut_kernel(keep_ref, got_ref, out_ref):
    for i in range(CHUNKS):
        at = chunk_at(i)
        out_ref[i] = (keep_ref[at] + got_ref[at].astype(F32)).astype(BF16)


def total_kernel(*refs):
    *ins, out_ref = refs
    total = sum(ref[i].astype(F32) for ref in ins for i in range(ref.shape[0])).astype(BF16)
    for i in range(out_ref.shape[0]):
        out_ref[i] = total


def total(copies, *arrays):
    return small(total_kernel, pltpu.VMEM((copies,) + CHUNK, BF16), "total", *arrays)


def swap_all(arr):
    return lax.all_to_all(arr, ("x", "zl"), 0, 0, tiled=True)


def turn(arr, k):
    return lax.ppermute(arr, "zh", [(i, (i + k) & 3) for i in range(4)])


def sum_all(keep, send, by_turns):
    shape = pltpu.VMEM((CHUNKS,) + CHUNK, BF16)
    parts = swap_all(small(cut_kernel, shape, "cut", keep, swap(send, "c")))
    if by_turns:
        own = total(1, parts)
        near = (own, turn(own, 1), turn(own, 3), turn(own, 2))
    else:
        near = (lax.all_to_all(total(4, parts), "zh", 0, 0, tiled=True),)
    mine = swap_all(total(CHUNKS, *near))
    return mine, swap(mine, "c")


def spread(core_ref, mine_ref, other_ref, in_ref):
    core = core_ref[0]
    for side, ref in ((core, mine_ref), (1 - core, other_ref)):
        for i in range(CHUNKS):
            in_ref[(side, *chunk_at(i))] = ref[i]


def middle_kernel(core_ref, mine_ref, other_ref, b_ref, pooled, cot, u_ref, v_ref, x1_ref, a_ref, keep_ref, send_ref, sums):
    spread(core_ref, mine_ref, other_ref, sums)
    z = g = None
    for f in range(pooled.shape[1] // WIDE):
        at = slice(f * WIDE, (f + 1) * WIDE)
        u, v = u_ref[0, :, at], v_ref[1, at, :]
        base = pooled[:, at].astype(F32)
        h0 = jnp.dot(sums[0], u, preferred_element_type=F32) + b_ref[0:1, at]
        x1 = (base * h0 + base).astype(BF16)
        x1_ref[:, at] = x1
        g1 = cot[:, at].astype(F32) + lax.dot_general(sums[1], v, NT, preferred_element_type=F32)
        a_ref[:, at] = (g1 * h0 + g1).astype(BF16)
        wide = (g1 * base).astype(BF16)
        more_z = jnp.dot(x1, v, preferred_element_type=F32)
        more_g = lax.dot_general(wide, u, NT, preferred_element_type=F32)
        z, g = (more_z, more_g) if f == 0 else (z + more_z, g + more_g)
    emit(core_ref, z, g, keep_ref, send_ref)


def middle(core, mine, other, bias, pooled, cot, u, v):
    samp, feats = pooled.shape
    rank = v.shape[-1]
    feat = pltpu.VMEM((samp, feats), BF16)
    return pl.pallas_call(
        middle_kernel,
        in_specs=[smem()] + [vmem()] * 7,
        out_specs=[vmem()] * 4,
        out_shape=[feat, feat, pltpu.VMEM((samp, rank), F32), pltpu.VMEM((samp, rank), BF16)],
        scratch_shapes=[pltpu.VMEM((2, samp, rank), BF16)],
        compiler_params=params(16),
        cost_estimate=cost(1 << 31, 8 << 20),
        name="middle",
    )(core, mine, other, bias, *kept(pooled, cot, u, v))


def row_grads(turned_ref, table, first, count, grad):
    return jnp.dot(turned_ref[table, first : first + count, :], grad, preferred_element_type=F32)


def far_kernel(core_ref, mine_ref, other_ref, b_ref, turned_a, turned_b, pooled, cot, x1, a, u_ref, v_ref, *refs):
    crossed_ref, grad_ref, far_a, far_b, sums = refs
    half, rows, emb = far_a.shape
    spread(core_ref, mine_ref, other_ref, sums)
    for f in range(pooled.shape[1] // WIDE):
        at = slice(f * WIDE, (f + 1) * WIDE)
        h1 = jnp.dot(sums[0], u_ref[1, :, at], preferred_element_type=F32) + b_ref[1:2, at]
        crossed_ref[:, at] = (pooled[:, at].astype(F32) * h1 + x1[:, at].astype(F32)).astype(BF16)
        grad = cot[:, at].astype(F32) * h1 + a[:, at].astype(F32)
        grad = (grad + lax.dot_general(sums[1], v_ref[0, at, :], NT, preferred_element_type=F32)).astype(BF16)
        grad_ref[:, at] = grad
        for i in range(2):
            side, t = divmod(2 * f + i, half)
            part = row_grads((turned_a, turned_b)[side], t, 2 * rows, rows, grad[:, i * emb : (i + 1) * emb])
            (far_a, far_b)[side][t] = part.astype(BF16)


def far_rows(core, mine, other, bias, turned, pooled, cot, x1, a, u, v):
    half, rows, samp = turned[0].shape
    rank = v.shape[-1]
    feats = pooled.shape[1]
    piece = pltpu.VMEM((half, rows // 4, feats // (2 * half)), BF16)
    return pl.pallas_call(
        far_kernel,
        in_specs=[smem()] + [vmem()] * 11,
        out_specs=[vmem()] * 4,
        out_shape=[pltpu.VMEM(pooled.shape, BF16)] * 2 + [piece, piece],
        scratch_shapes=[pltpu.VMEM((2, samp, rank), BF16)],
        compiler_params=params(16),
        cost_estimate=cost(5 << 28, 7 << 20),
        name="far_rows",
    )(core, mine, other, bias, *kept(*turned, pooled, cot, x1, a, u, v))


def near_kernel(turned_a, turned_b, grad, made_ref, crossed_ref, p0_ref, p1_a, p1_b, p3_a, p3_b, sem):
    copy = pltpu.make_async_copy(made_ref, crossed_ref, sem)
    copy.start()
    half, rows, emb = p1_a.shape
    for t in range(2 * half):
        side, at = divmod(t, half)
        part = grad[:, t * emb : (t + 1) * emb]
        turned = (turned_a, turned_b)[side]
        first = row_grads(turned, at, 0, 2 * rows, part)
        p0_ref[t] = first[:rows]
        (p1_a, p1_b)[side][at] = first[rows:].astype(BF16)
        (p3_a, p3_b)[side][at] = row_grads(turned, at, 3 * rows, rows, part).astype(BF16)
    copy.wait()


def near_rows(turned, grad, crossed):
    half, rows, samp = turned[0].shape
    block = (half, rows // 4, grad.shape[1] // (2 * half))
    return pl.pallas_call(
        near_kernel,
        in_specs=[vmem()] * 4,
        out_specs=[anyspace()] + [vmem()] * 5,
        out_shape=[pltpu.HBM(crossed.shape, BF16), pltpu.VMEM((2 * half,) + block[1:], F32)]
        + [pltpu.VMEM(block, BF16)] * 4,
        scratch_shapes=[pltpu.SemaphoreType.DMA],
        compiler_params=params(16),
        cost_estimate=cost(3 << 28, 7 << 20),
        name="near_rows",
    )(*kept(*turned, grad, crossed))


def finish_kernel(p0, sum_ref, far_ref, *refs, side):
    out_ref, held, sem = refs[-3:]
    half = held.shape[0]
    held[...] = p0[side * half : (side + 1) * half] + (sum_ref[...].astype(F32) + far_ref[...].astype(F32))
    copy = pltpu.make_async_copy(held, out_ref.at[pl.ds(side * half, half)], sem)
    copy.start()
    copy.wait()


def finish(side, before, p0, near, far):
    return pl.pallas_call(
        functools.partial(finish_kernel, side=side),
        in_specs=[vmem()] * 3 + [anyspace()] * len(before),
        out_specs=anyspace(),
        out_shape=pltpu.HBM(p0.shape, F32),
        scratch_shapes=[pltpu.VMEM(near.shape, F32), pltpu.SemaphoreType.DMA],
        input_output_aliases={3: 0} if before else {},
        compiler_params=params(8),
        cost_estimate=cost(1 << 20, 1 << 20),
        name="finish",
    )(*kept(p0), near, far, *before)


def right(arr):
    return lax.ppermute(arr, "row", [(i, (i + 1) & 3) for i in range(4)])


def left(arr):
    return lax.ppermute(arr, "row", [(i, (i + 3) & 3) for i in range(4)])


def add(a, b):
    return a.astype(F32) + b.astype(F32)


def scalar(axis):
    return lax.axis_index(axis).astype(jnp.int32).reshape(1)


def local(emb_rows, entry_ids, entry_sample, cross_v, cross_u, cross_bias, cotangent):
    samp = cotangent.shape[0]
    rows = emb_rows.shape[1] * lax.axis_size("row")
    mine, core = scalar("row"), scalar("c")
    own_a, own_b = cast_halves(emb_rows)
    left_a, right_b = right(own_a), left(own_b)
    left_b, right_a = right(own_b), left(own_a)
    counts_a, turned_a, edges = make_counts(mine, entry_ids, entry_sample, samp, rows)
    left_a, right_b, edges = lax.optimization_barrier((left_a, right_b, edges))
    far_a, far_b = right(left_a), left(right_b)
    loads = (cotangent, cross_v, cross_u)
    counts_b, turned_b, cot, v, u = make_counts(mine, entry_ids, entry_sample, samp, rows, edges, loads)
    embs = (own_a, own_b, right_a, right_b, far_a, far_b, left_a, left_b)
    pooled, keep, send = first_sums(core, (counts_a, counts_b), embs, cot, v, u)
    sums = sum_all(keep, send, False)
    x1, a, keep, send = middle(core, *sums, cross_bias, pooled, cot, u, v)
    sums = sum_all(keep, send, True)
    turned = (turned_a, turned_b)
    crossed, grad, p2a, p2b = far_rows(core, *sums, cross_bias, turned, pooled, cot, x1, a, u, v)
    from_left, from_right = right(p2a), left(p2b)
    crossed, p0, p1a, p1b, p3a, p3b = near_rows(turned, grad, crossed)
    sum_b, sum_a = right(p1b), left(p3a)
    far_a = right(add(p1a, from_left).astype(BF16))
    far_b = left(add(p3b, from_right).astype(BF16))
    grads = finish(0, (), p0, sum_a, far_a)
    return crossed, finish(1, (grads,), p0, sum_b, far_b)


def solution(mesh):
    fine = jax.sharding.Mesh(mesh.devices.reshape(4, 4, 2, 2, 4), ("x", "zh", "zl", "c", "row"))
    table = ("x", "zh", "zl", "c")
    placed = (
        P(table, "row", None),
        P(table, None),
        P(table, None),
        P(None, table, None),
        P(None, None, table),
        P(None, table),
        P("row", table),
    )
    return jax.shard_map(
        local,
        mesh=fine,
        in_specs=placed,
        out_specs=(P("row", table), P(table, "row", None)),
        check_vma=False,
    )
```

```python
import functools

import jax
import jax.numpy as jnp
from jax import lax
from jax.experimental import pallas as pl
from jax.experimental.pallas import tpu as pltpu
from jax.sharding import PartitionSpec as P

F32 = jnp.float32
BF16 = jnp.bfloat16
EB = 512
NT = (((1,), (1,)), ((), ()))
TN = (((0,), (0,)), ((), ()))


def vmem():
    return pl.BlockSpec(memory_space=pltpu.VMEM)


def smem():
    return pl.BlockSpec(memory_space=pltpu.SMEM)


def params(mib):
    return pltpu.CompilerParams(vmem_limit_bytes=mib * 2**20)


def cost(flops, moved):
    return pl.CostEstimate(flops=flops, bytes_accessed=moved, transcendentals=0)


def pinned(arr):
    return pltpu.with_memory_space_constraint(arr, pltpu.HBM)


def kept(*arrs):
    return [pltpu.with_memory_space_constraint(arr, pltpu.VMEM) for arr in arrs]


def hbm():
    return pl.BlockSpec(memory_space=pltpu.HBM)


def cast_kernel(in_ref, a_ref, b_ref, held, sems):
    half = a_ref.shape[0]
    outs = (a_ref, b_ref)
    copies = fetch(sems, [(in_ref.at[pl.ds(i * half, half)], held.at[i]) for i in range(2)])
    for i in range(2):
        copies[i].wait()
        outs[i][...] = held[i].astype(BF16)


def cast_halves(emb_rows):
    tabs, rows, emb = emb_rows.shape
    half = (tabs // 2, rows, emb)
    return pl.pallas_call(
        cast_kernel,
        in_specs=[hbm()],
        out_specs=[vmem()] * 2,
        out_shape=[pltpu.VMEM(half, BF16)] * 2,
        scratch_shapes=[pltpu.VMEM((2,) + half, F32), pltpu.SemaphoreType.DMA((2,))],
        compiler_params=params(16),
        cost_estimate=cost(1 << 18, 3 << 19),
        name="cast",
    )(pinned(emb_rows))


def counts_kernel(mine_ref, ids_ref, own_ref, *refs, first_table):
    if first_table:
        edges_ref, *loads, out_ref = refs[: (len(refs) - 2) // 2]
        loaded, (acc_ref, ids, own, sems) = refs[len(loads) + 2 : -4], refs[-4:]
    else:
        out_ref, edges_ref, acc_ref, ids, own, sems = refs
        loads = loaded = ()
    samp, rows = acc_ref.shape
    tabs, entries = own.shape
    mine = mine_ref[0]
    low = mine * samp
    turn = mine * (rows // 4)
    copies = fetch(sems, [(own_ref, own), (ids_ref, ids), *zip(loads, loaded)])
    copies[0].wait()
    if not first_table:
        owners = own[...]
        first = jnp.sum((owners < low).astype(jnp.int32), axis=1, keepdims=True)
        last = jnp.sum((owners < low + samp).astype(jnp.int32), axis=1, keepdims=True)
        for i in range(tabs):
            edges_ref[i] = first[i, 0]
            edges_ref[tabs + i] = last[i, 0]
    copies[1].wait()
    grid = lax.broadcasted_iota(jnp.int32, (samp, EB), 0).astype(F32).astype(BF16)
    one, zero = jnp.ones((), BF16), jnp.zeros((), BF16)

    @pl.loop(0, out_ref.shape[0])
    def _(i):
        t = i + first_table
        start = edges_ref[t] // 128
        steps = (edges_ref[tabs + t] - start * 128 + EB - 1) // EB
        start = jnp.minimum(start, (entries - steps * EB) // 128)
        acc_ref[...] = jnp.zeros_like(acc_ref)

        def body(block, carry):
            at = pl.ds(pl.multiple_of(start * 128 + block * EB, 128), EB)
            who = own[pl.ds(t, 1), at] - low
            row = (ids[pl.ds(t, 1), at] - turn) & (rows - 1)
            hot = [
                jnp.where(grid == values.astype(F32).astype(BF16), one, zero) for values in (who, row, row - samp)
            ]
            acc_ref[...] += lax.dot_general(
                hot[0], jnp.concatenate(hot[1:], axis=0), NT, preferred_element_type=F32
            )
            return carry

        lax.fori_loop(0, steps, body, 0)
        out_ref[i] = acc_ref[...].astype(BF16)

    for copy in copies[2:]:
        copy.wait()


def make_counts(mine, ids, owners, samp, rows, edges=None, loads=()):
    tabs, entries = ids.shape
    assert rows == 2 * samp and samp <= 256
    half = tabs // 2
    first = edges is None
    out_shape = [pltpu.VMEM((half, samp, rows), BF16)]
    if first:
        out_specs = [vmem(), smem()]
        out_shape.append(jax.ShapeDtypeStruct((2 * tabs,), jnp.int32))
    else:
        out_specs = [vmem()] * (1 + len(loads))
        out_shape += [pltpu.VMEM(arr.shape, arr.dtype) for arr in loads]
    return pl.pallas_call(
        functools.partial(counts_kernel, first_table=0 if first else half),
        in_specs=[smem(), hbm(), hbm()] + ([] if first else [smem()] + [hbm()] * len(loads)),
        out_specs=out_specs,
        out_shape=out_shape,
        scratch_shapes=[
            pltpu.VMEM((samp, rows), F32),
            pltpu.VMEM((tabs, entries), jnp.int32),
            pltpu.VMEM((tabs, entries), jnp.int32),
            pltpu.SemaphoreType.DMA((2 + len(loads),)),
        ],
        compiler_params=params(16),
        cost_estimate=cost(half * samp * rows * 3072, 3 << 20),
        name="counts",
    )(mine, pinned(ids), pinned(owners), *([] if first else [edges, *map(pinned, loads)]))


def turned_kernel(in_ref, out_ref, *, first):
    for i in range(out_ref.shape[0]):
        out_ref[i] = in_ref[first + i].T


def turned_pair(counts, first):
    half, samp, rows = counts.shape
    return pl.pallas_call(
        functools.partial(turned_kernel, first=first),
        in_specs=[vmem()],
        out_specs=vmem(),
        out_shape=pltpu.VMEM((2, rows, samp), BF16),
        compiler_params=params(8),
        cost_estimate=cost(1 << 30, 1 << 20),
        name="turned",
    )(*kept(counts))


WIDE = 512


def fetch(sems, pairs):
    copies = [pltpu.make_async_copy(src, dst, sems.at[i]) for i, (src, dst) in enumerate(pairs)]
    for copy in copies:
        copy.start()
    return copies


def emit(core_ref, z, g, keep_ref, send_ref):
    even = core_ref[0] == 0
    keep_ref[...] = jnp.where(even, z, g)
    send_ref[...] = jnp.where(even, g, z).astype(BF16)


def anyspace():
    return pl.BlockSpec(memory_space=pl.ANY)


def first_kernel(core_ref, counts_a, counts_b, *refs):
    embs, (cot, v, u, pooled_ref, keep_ref, send_ref) = refs[:8], refs[8:]
    half = counts_a.shape[0]
    z = g = None
    for f in range(half):
        parts = []
        for t in (2 * f, 2 * f + 1):
            side, at = divmod(t, half)
            rows = jnp.concatenate([embs[2 * k + side][at] for k in range(4)], axis=0)
            parts.append(jnp.dot((counts_a, counts_b)[side][at], rows, preferred_element_type=F32).astype(BF16))
        pooled = jnp.concatenate(parts, axis=1)
        at = slice(f * WIDE, (f + 1) * WIDE)
        pooled_ref[:, at] = pooled
        wide = (cot[:, at].astype(F32) * pooled.astype(F32)).astype(BF16)
        more_z = jnp.dot(pooled, v[0, at, :], preferred_element_type=F32)
        more_g = lax.dot_general(wide, u[1, :, at], NT, preferred_element_type=F32)
        z, g = (more_z, more_g) if f == 0 else (z + more_z, g + more_g)
    emit(core_ref, z, g, keep_ref, send_ref)


def first_sums(core, counts, embs, cot, v, u):
    half, samp, rows = counts[0].shape
    emb = embs[0].shape[-1]
    rank = v.shape[-1]
    assert 2 * emb == WIDE
    return pl.pallas_call(
        first_kernel,
        in_specs=[smem()] + [vmem()] * 13,
        out_specs=[vmem()] * 3,
        out_shape=[
            pltpu.VMEM((samp, 2 * half * emb), BF16),
            pltpu.VMEM((samp, rank), F32),
            pltpu.VMEM((samp, rank), BF16),
        ],
        compiler_params=params(16),
        cost_estimate=cost(3 << 29, 10 << 20),
        name="first_sums",
    )(core, *kept(*counts), *embs, *kept(cot, v, u))


def swap(arr, axis):
    return lax.ppermute(arr, axis, [(0, 1), (1, 0)])


def small(kernel, out_shape, name, *args):
    return pl.pallas_call(
        kernel,
        in_specs=[vmem()] * len(args),
        out_specs=jax.tree.map(lambda _: vmem(), out_shape),
        out_shape=out_shape,
        compiler_params=params(8),
        cost_estimate=cost(1 << 20, 1 << 20),
        name=name,
    )(*args)


CHUNKS = 8
CHUNK = (32, 512)


def chunk_at(i):
    return slice(CHUNK[0] * i, CHUNK[0] * (i + 1)), slice(None)


def cut_kernel(keep_ref, got_ref, out_ref):
    for i in range(CHUNKS):
        at = chunk_at(i)
        out_ref[i] = (keep_ref[at] + got_ref[at].astype(F32)).astype(BF16)


def total_kernel(*refs):
    *ins, out_ref = refs
    total = sum(ref[i].astype(F32) for ref in ins for i in range(ref.shape[0])).astype(BF16)
    for i in range(out_ref.shape[0]):
        out_ref[i] = total


def total(copies, *arrays):
    return small(total_kernel, pltpu.VMEM((copies,) + CHUNK, BF16), "total", *arrays)


def swap_all(arr):
    return lax.all_to_all(arr, ("x", "zl"), 0, 0, tiled=True)


def turn(arr, k):
    return lax.ppermute(arr, "zh", [(i, (i + k) & 3) for i in range(4)])


def beside(arr, counts, first):
    arr, counts = lax.optimization_barrier((arr, counts))
    return lax.optimization_barrier((swap(arr, "c"), turned_pair(counts, first)))


def sum_all(keep, send, counts, by_neighbours):
    got, turned_front = beside(send, counts, 0)
    shape = pltpu.VMEM((CHUNKS,) + CHUNK, BF16)
    own = total(1, swap_all(small(cut_kernel, shape, "cut", keep, got)))
    up, down = turn(own, 1), turn(own, 3)
    far = turn(up, 1) if by_neighbours else turn(own, 2)
    mine = swap_all(total(CHUNKS, own, up, down, far))
    other, turned_back = beside(mine, counts, 2)
    return mine, other, (turned_front, turned_back)


def spread(core_ref, mine_ref, other_ref, in_ref):
    core = core_ref[0]
    for side, ref in ((core, mine_ref), (1 - core, other_ref)):
        for i in range(CHUNKS):
            in_ref[(side, *chunk_at(i))] = ref[i]


def middle_kernel(core_ref, mine_ref, other_ref, b_ref, pooled, cot, u_ref, v_ref, x1_ref, a_ref, keep_ref, send_ref, sums):
    spread(core_ref, mine_ref, other_ref, sums)
    z = g = None
    for f in range(pooled.shape[1] // WIDE):
        at = slice(f * WIDE, (f + 1) * WIDE)
        u, v = u_ref[0, :, at], v_ref[1, at, :]
        base = pooled[:, at].astype(F32)
        h0 = jnp.dot(sums[0], u, preferred_element_type=F32) + b_ref[0:1, at]
        x1 = (base * h0 + base).astype(BF16)
        x1_ref[:, at] = x1
        g1 = cot[:, at].astype(F32) + lax.dot_general(sums[1], v, NT, preferred_element_type=F32)
        a_ref[:, at] = (g1 * h0 + g1).astype(BF16)
        wide = (g1 * base).astype(BF16)
        more_z = jnp.dot(x1, v, preferred_element_type=F32)
        more_g = lax.dot_general(wide, u, NT, preferred_element_type=F32)
        z, g = (more_z, more_g) if f == 0 else (z + more_z, g + more_g)
    emit(core_ref, z, g, keep_ref, send_ref)


def middle(core, mine, other, bias, pooled, cot, u, v):
    samp, feats = pooled.shape
    rank = v.shape[-1]
    feat = pltpu.VMEM((samp, feats), BF16)
    return pl.pallas_call(
        middle_kernel,
        in_specs=[smem()] + [vmem()] * 7,
        out_specs=[vmem()] * 4,
        out_shape=[feat, feat, pltpu.VMEM((samp, rank), F32), pltpu.VMEM((samp, rank), BF16)],
        scratch_shapes=[pltpu.VMEM((2, samp, rank), BF16)],
        compiler_params=params(16),
        cost_estimate=cost(1 << 31, 8 << 20),
        name="middle",
    )(core, mine, other, bias, *kept(pooled, cot, u, v))


def row_grads(turned_ref, table, first, count, grad):
    return jnp.dot(turned_ref[table, first : first + count, :], grad, preferred_element_type=F32)


def far_kernel(core_ref, mine_ref, other_ref, b_ref, *refs):
    turned, refs = refs[:4], refs[4:]
    pooled, cot, x1, a, u_ref, v_ref, crossed_ref, grad_ref, far_a, far_b, sums = refs
    half, rows, emb = far_a.shape
    spread(core_ref, mine_ref, other_ref, sums)
    for f in range(pooled.shape[1] // WIDE):
        at = slice(f * WIDE, (f + 1) * WIDE)
        h1 = jnp.dot(sums[0], u_ref[1, :, at], preferred_element_type=F32) + b_ref[1:2, at]
        crossed_ref[:, at] = (pooled[:, at].astype(F32) * h1 + x1[:, at].astype(F32)).astype(BF16)
        grad = cot[:, at].astype(F32) * h1 + a[:, at].astype(F32)
        grad = (grad + lax.dot_general(sums[1], v_ref[0, at, :], NT, preferred_element_type=F32)).astype(BF16)
        grad_ref[:, at] = grad
        for i in range(2):
            side, t = divmod(2 * f + i, half)
            part = row_grads(turned[f], i, 2 * rows, rows, grad[:, i * emb : (i + 1) * emb])
            (far_a, far_b)[side][t] = part.astype(BF16)


def far_rows(core, mine, other, bias, turned, pooled, cot, x1, a, u, v):
    _, rows, samp = turned[0].shape
    half = 2 * len(turned) // 2
    rank = v.shape[-1]
    feats = pooled.shape[1]
    piece = pltpu.VMEM((half, rows // 4, feats // (2 * half)), BF16)
    return pl.pallas_call(
        far_kernel,
        in_specs=[smem()] + [vmem()] * 13,
        out_specs=[vmem()] * 4,
        out_shape=[pltpu.VMEM(pooled.shape, BF16)] * 2 + [piece, piece],
        scratch_shapes=[pltpu.VMEM((2, samp, rank), BF16)],
        compiler_params=params(16),
        cost_estimate=cost(5 << 28, 7 << 20),
        name="far_rows",
    )(core, mine, other, bias, *kept(*turned, pooled, cot, x1, a, u, v))


def near_kernel(*refs):
    turned, refs = refs[:4], refs[4:]
    grad, made_ref, crossed_ref, p0_ref, p1_a, p1_b, p3_a, p3_b, sem = refs
    copy = pltpu.make_async_copy(made_ref, crossed_ref, sem)
    copy.start()
    half, rows, emb = p1_a.shape
    for t in range(2 * half):
        side, at = divmod(t, half)
        part = grad[:, t * emb : (t + 1) * emb]
        first = row_grads(turned[t // 2], t % 2, 0, 2 * rows, part)
        p0_ref[t] = first[:rows]
        (p1_a, p1_b)[side][at] = first[rows:].astype(BF16)
        (p3_a, p3_b)[side][at] = row_grads(turned[t // 2], t % 2, 3 * rows, rows, part).astype(BF16)
    copy.wait()


def near_rows(turned, grad, crossed):
    _, rows, samp = turned[0].shape
    half = 2 * len(turned) // 2
    block = (half, rows // 4, grad.shape[1] // (2 * half))
    return pl.pallas_call(
        near_kernel,
        in_specs=[vmem()] * 6,
        out_specs=[anyspace()] + [vmem()] * 5,
        out_shape=[pltpu.HBM(crossed.shape, BF16), pltpu.VMEM((2 * half,) + block[1:], F32)]
        + [pltpu.VMEM(block, BF16)] * 4,
        scratch_shapes=[pltpu.SemaphoreType.DMA],
        compiler_params=params(16),
        cost_estimate=cost(3 << 28, 7 << 20),
        name="near_rows",
    )(*kept(*turned, grad, crossed))


def finish_kernel(p0, sum_ref, far_ref, *refs, side):
    out_ref, held, sem = refs[-3:]
    half = held.shape[0]
    held[...] = p0[side * half : (side + 1) * half] + (sum_ref[...].astype(F32) + far_ref[...].astype(F32))
    copy = pltpu.make_async_copy(held, out_ref.at[pl.ds(side * half, half)], sem)
    copy.start()
    copy.wait()


def finish(side, before, p0, near, far):
    return pl.pallas_call(
        functools.partial(finish_kernel, side=side),
        in_specs=[vmem()] * 3 + [anyspace()] * len(before),
        out_specs=anyspace(),
        out_shape=pltpu.HBM(p0.shape, F32),
        scratch_shapes=[pltpu.VMEM(near.shape, F32), pltpu.SemaphoreType.DMA],
        input_output_aliases={3: 0} if before else {},
        compiler_params=params(8),
        cost_estimate=cost(1 << 20, 1 << 20),
        name="finish",
    )(*kept(p0), near, far, *before)


def right(arr):
    return lax.ppermute(arr, "row", [(i, (i + 1) & 3) for i in range(4)])


def left(arr):
    return lax.ppermute(arr, "row", [(i, (i + 3) & 3) for i in range(4)])


def add(a, b):
    return a.astype(F32) + b.astype(F32)


def scalar(axis):
    return lax.axis_index(axis).astype(jnp.int32).reshape(1)


def local(emb_rows, entry_ids, entry_sample, cross_v, cross_u, cross_bias, cotangent):
    samp = cotangent.shape[0]
    rows = emb_rows.shape[1] * lax.axis_size("row")
    mine, core = scalar("row"), scalar("c")
    own_a, own_b = cast_halves(emb_rows)
    left_a, right_b = right(own_a), left(own_b)
    left_b, right_a = right(own_b), left(own_a)
    counts_a, edges = make_counts(mine, entry_ids, entry_sample, samp, rows)
    left_a, right_b, edges = lax.optimization_barrier((left_a, right_b, edges))
    far_a, far_b = right(left_a), left(right_b)
    loads = (cotangent, cross_v, cross_u)
    counts_b, cot, v, u = make_counts(mine, entry_ids, entry_sample, samp, rows, edges, loads)
    embs = (own_a, own_b, right_a, right_b, far_a, far_b, left_a, left_b)
    pooled, keep, send = first_sums(core, (counts_a, counts_b), embs, cot, v, u)
    *sums, turned_a = sum_all(keep, send, counts_a, True)
    x1, a, keep, send = middle(core, *sums, cross_bias, pooled, cot, u, v)
    *sums, turned_b = sum_all(keep, send, counts_b, False)
    turned = (*turned_a, *turned_b)
    crossed, grad, p2a, p2b = far_rows(core, *sums, cross_bias, turned, pooled, cot, x1, a, u, v)
    from_left, from_right = right(p2a), left(p2b)
    crossed, p0, p1a, p1b, p3a, p3b = near_rows(turned, grad, crossed)
    sum_b, sum_a = right(p1b), left(p3a)
    far_a = right(add(p1a, from_left).astype(BF16))
    far_b = left(add(p3b, from_right).astype(BF16))
    grads = finish(0, (), p0, sum_a, far_a)
    return crossed, finish(1, (grads,), p0, sum_b, far_b)


def solution(mesh):
    fine = jax.sharding.Mesh(mesh.devices.reshape(4, 4, 2, 2, 4), ("x", "zh", "zl", "c", "row"))
    table = ("x", "zh", "zl", "c")
    placed = (
        P(table, "row", None),
        P(table, None),
        P(table, None),
        P(None, table, None),
        P(None, None, table),
        P(None, table),
        P("row", table),
    )
    return jax.shard_map(
        local,
        mesh=fine,
        in_specs=placed,
        out_specs=(P("row", table), P(table, "row", None)),
        check_vma=False,
    )
```

```python
import functools

import jax
import jax.numpy as jnp
from jax import lax
from jax.experimental import pallas as pl
from jax.experimental.pallas import tpu as pltpu
from jax.sharding import PartitionSpec as P

F32 = jnp.float32
BF16 = jnp.bfloat16
EB = 512
NT = (((1,), (1,)), ((), ()))
TN = (((0,), (0,)), ((), ()))


def vmem():
    return pl.BlockSpec(memory_space=pltpu.VMEM)


def smem():
    return pl.BlockSpec(memory_space=pltpu.SMEM)


def params(mib):
    return pltpu.CompilerParams(vmem_limit_bytes=mib * 2**20)


def cost(flops, moved):
    return pl.CostEstimate(flops=flops, bytes_accessed=moved, transcendentals=0)


def pinned(arr):
    return pltpu.with_memory_space_constraint(arr, pltpu.HBM)


def kept(*arrs):
    return [pltpu.with_memory_space_constraint(arr, pltpu.VMEM) for arr in arrs]


def hbm():
    return pl.BlockSpec(memory_space=pltpu.HBM)


def cast_kernel(in_ref, a_ref, b_ref, held, sems):
    half = a_ref.shape[0]
    outs = (a_ref, b_ref)
    copies = fetch(sems, [(in_ref.at[pl.ds(i * half, half)], held.at[i]) for i in range(2)])
    for i in range(2):
        copies[i].wait()
        outs[i][...] = held[i].astype(BF16)


def cast_halves(emb_rows):
    tabs, rows, emb = emb_rows.shape
    half = (tabs // 2, rows, emb)
    return pl.pallas_call(
        cast_kernel,
        in_specs=[hbm()],
        out_specs=[vmem()] * 2,
        out_shape=[pltpu.VMEM(half, BF16)] * 2,
        scratch_shapes=[pltpu.VMEM((2,) + half, F32), pltpu.SemaphoreType.DMA((2,))],
        compiler_params=params(16),
        cost_estimate=cost(1 << 18, 3 << 19),
        name="cast",
    )(pinned(emb_rows))


def counts_kernel(mine_ref, ids_ref, own_ref, *refs, first_table):
    refs, (acc_ref, sems) = refs[:-2], refs[-2:]
    if first_table:
        ids, own = ids_ref, own_ref
        edges_ref, *loads = refs[: len(refs) // 2]
        out_ref, turned_ref, *loaded = refs[len(refs) // 2 :]
        copies = fetch(sems, zip(loads, loaded))
    else:
        out_ref, turned_ref, edges_ref, ids, own = refs
        copies = fetch(sems, [(own_ref, own), (ids_ref, ids)])
    _, rows, samp = acc_ref.shape
    tabs, entries = own.shape
    mine = mine_ref[0]
    low = mine * samp
    turn = mine * (rows // 4)
    if not first_table:
        copies[0].wait()
        owners = own[...]
        first = jnp.sum((owners < low).astype(jnp.int32), axis=1, keepdims=True)
        last = jnp.sum((owners < low + samp).astype(jnp.int32), axis=1, keepdims=True)
        for i in range(tabs):
            edges_ref[i] = first[i, 0]
            edges_ref[tabs + i] = last[i, 0]
        copies[1].wait()
    grid = lax.broadcasted_iota(jnp.int32, (samp, EB), 0).astype(F32).astype(BF16)
    one, zero = jnp.ones((), BF16), jnp.zeros((), BF16)

    @pl.loop(0, out_ref.shape[0] // 2)
    def _(pair):
        tables = [first_table + 2 * pair + j for j in range(2)]
        starts = [edges_ref[t] // 128 for t in tables]
        spans = [edges_ref[tabs + t] - start * 128 for t, start in zip(tables, starts)]
        steps = (jnp.maximum(*spans) + EB - 1) // EB
        starts = [jnp.minimum(start, (entries - steps * EB) // 128) * 128 for start in starts]
        acc_ref[...] = jnp.zeros_like(acc_ref)

        def body(block, carry):
            for j, t in enumerate(tables):
                at = pl.ds(pl.multiple_of(starts[j] + block * EB, 128), EB)
                who = own[pl.ds(t, 1), at] - low
                row = (ids[pl.ds(t, 1), at] - turn) & (rows - 1)
                hot = [
                    jnp.where(grid == values.astype(F32).astype(BF16), one, zero) for values in (who, row, row - samp)
                ]
                acc_ref[j] += lax.dot_general(
                    jnp.concatenate(hot[1:], axis=0), hot[0], NT, preferred_element_type=F32
                )
            return carry

        lax.fori_loop(0, steps, body, 0)
        for j in range(2):
            total = acc_ref[j].astype(BF16)
            turned_ref[2 * pair + j] = total
            out_ref[2 * pair + j] = total.T

    if first_table:
        for copy in copies:
            copy.wait()


def make_counts(mine, ids, owners, samp, rows, edges=None, loads=()):
    tabs, entries = ids.shape
    assert rows == 2 * samp and samp <= 256
    half = tabs // 2
    out_shape = [pltpu.VMEM((half, samp, rows), BF16), pltpu.VMEM((half, rows, samp), BF16)]
    if edges is None:
        args = (mine, pinned(ids), pinned(owners))
        in_specs = [smem(), hbm(), hbm()]
        out_specs = [vmem(), vmem(), smem(), vmem(), vmem()]
        out_shape.append(jax.ShapeDtypeStruct((2 * tabs,), jnp.int32))
        out_shape += [pltpu.VMEM(ids.shape, jnp.int32)] * 2
    else:
        args = (mine, *kept(ids, owners), edges, *map(pinned, loads))
        in_specs = [smem(), vmem(), vmem(), smem()] + [hbm()] * len(loads)
        out_specs = [vmem()] * (2 + len(loads))
        out_shape += [pltpu.VMEM(arr.shape, arr.dtype) for arr in loads]
    return pl.pallas_call(
        functools.partial(counts_kernel, first_table=0 if edges is None else half),
        in_specs=in_specs,
        out_specs=out_specs,
        out_shape=out_shape,
        scratch_shapes=[pltpu.VMEM((2, rows, samp), F32), pltpu.SemaphoreType.DMA((max(2, len(loads)),))],
        compiler_params=params(16),
        cost_estimate=cost(half * samp * rows * 3072, 3 << 20),
        name="counts",
    )(*args)


WIDE = 512


def fetch(sems, pairs):
    copies = [pltpu.make_async_copy(src, dst, sems.at[i]) for i, (src, dst) in enumerate(pairs)]
    for copy in copies:
        copy.start()
    return copies


def emit(core_ref, z, g, keep_ref, send_ref):
    even = core_ref[0] == 0
    keep_ref[...] = jnp.where(even, z, g)
    send_ref[...] = jnp.where(even, g, z).astype(BF16)


def anyspace():
    return pl.BlockSpec(memory_space=pl.ANY)


def first_kernel(core_ref, counts_a, counts_b, *refs):
    embs, (cot, v, u, pooled_ref, keep_ref, send_ref) = refs[:8], refs[8:]
    half = counts_a.shape[0]
    z = g = None
    for f in range(half):
        parts = []
        for t in (2 * f, 2 * f + 1):
            side, at = divmod(t, half)
            rows = jnp.concatenate([embs[2 * k + side][at] for k in range(4)], axis=0)
            parts.append(jnp.dot((counts_a, counts_b)[side][at], rows, preferred_element_type=F32).astype(BF16))
        pooled = jnp.concatenate(parts, axis=1)
        at = slice(f * WIDE, (f + 1) * WIDE)
        pooled_ref[:, at] = pooled
        wide = (cot[:, at].astype(F32) * pooled.astype(F32)).astype(BF16)
        more_z = jnp.dot(pooled, v[0, at, :], preferred_element_type=F32)
        more_g = lax.dot_general(wide, u[1, :, at], NT, preferred_element_type=F32)
        z, g = (more_z, more_g) if f == 0 else (z + more_z, g + more_g)
    emit(core_ref, z, g, keep_ref, send_ref)


def first_sums(core, counts, embs, cot, v, u):
    half, samp, rows = counts[0].shape
    emb = embs[0].shape[-1]
    rank = v.shape[-1]
    assert 2 * emb == WIDE
    return pl.pallas_call(
        first_kernel,
        in_specs=[smem()] + [vmem()] * 13,
        out_specs=[vmem()] * 3,
        out_shape=[
            pltpu.VMEM((samp, 2 * half * emb), BF16),
            pltpu.VMEM((samp, rank), F32),
            pltpu.VMEM((samp, rank), BF16),
        ],
        compiler_params=params(16),
        cost_estimate=cost(3 << 29, 10 << 20),
        name="first_sums",
    )(core, *kept(*counts), *embs, *kept(cot, v, u))


def swap(arr, axis):
    return lax.ppermute(arr, axis, [(0, 1), (1, 0)])


def small(kernel, out_shape, name, *args):
    return pl.pallas_call(
        kernel,
        in_specs=[vmem()] * len(args),
        out_specs=jax.tree.map(lambda _: vmem(), out_shape),
        out_shape=out_shape,
        compiler_params=params(8),
        cost_estimate=cost(1 << 20, 1 << 20),
        name=name,
    )(*args)


CHUNKS = 8
CHUNK = (32, 512)


def chunk_at(i):
    return slice(CHUNK[0] * i, CHUNK[0] * (i + 1)), slice(None)


def cut_kernel(keep_ref, got_ref, out_ref):
    for i in range(CHUNKS):
        at = chunk_at(i)
        out_ref[i] = (keep_ref[at] + got_ref[at].astype(F32)).astype(BF16)


def total_kernel(*refs):
    *ins, out_ref = refs
    total = sum(ref[i].astype(F32) for ref in ins for i in range(ref.shape[0])).astype(BF16)
    for i in range(out_ref.shape[0]):
        out_ref[i] = total


def total(copies, *arrays):
    return small(total_kernel, pltpu.VMEM((copies,) + CHUNK, BF16), "total", *arrays)


def swap_all(arr):
    return lax.all_to_all(arr, ("x", "zl"), 0, 0, tiled=True)


def turn(arr, k):
    return lax.ppermute(arr, "zh", [(i, (i + k) & 3) for i in range(4)])


def sum_all(keep, send, by_pairs):
    shape = pltpu.VMEM((CHUNKS,) + CHUNK, BF16)
    parts = swap_all(small(cut_kernel, shape, "cut", keep, swap(send, "c")))
    own = total(1, parts)
    if by_pairs:
        two = total(1, own, lax.ppermute(own, "zh", [(0, 1), (1, 0), (2, 3), (3, 2)]))
        near = (two, lax.ppermute(two, "zh", [(0, 3), (3, 0), (1, 2), (2, 1)]))
    else:
        near = (own, turn(own, 1), turn(own, 3), turn(own, 2))
    mine = swap_all(total(CHUNKS, *near))
    return mine, swap(mine, "c")


def spread(core_ref, mine_ref, other_ref, in_ref):
    core = core_ref[0]
    for side, ref in ((core, mine_ref), (1 - core, other_ref)):
        for i in range(CHUNKS):
            in_ref[(side, *chunk_at(i))] = ref[i]


def middle_kernel(core_ref, mine_ref, other_ref, b_ref, pooled, cot, u_ref, v_ref, x1_ref, a_ref, keep_ref, send_ref, sums):
    spread(core_ref, mine_ref, other_ref, sums)
    z = g = None
    for f in range(pooled.shape[1] // WIDE):
        at = slice(f * WIDE, (f + 1) * WIDE)
        u, v = u_ref[0, :, at], v_ref[1, at, :]
        base = pooled[:, at].astype(F32)
        h0 = jnp.dot(sums[0], u, preferred_element_type=F32) + b_ref[0:1, at]
        x1 = (base * h0 + base).astype(BF16)
        x1_ref[:, at] = x1
        g1 = cot[:, at].astype(F32) + lax.dot_general(sums[1], v, NT, preferred_element_type=F32)
        a_ref[:, at] = (g1 * h0 + g1).astype(BF16)
        wide = (g1 * base).astype(BF16)
        more_z = jnp.dot(x1, v, preferred_element_type=F32)
        more_g = lax.dot_general(wide, u, NT, preferred_element_type=F32)
        z, g = (more_z, more_g) if f == 0 else (z + more_z, g + more_g)
    emit(core_ref, z, g, keep_ref, send_ref)


def middle(core, mine, other, bias, pooled, cot, u, v):
    samp, feats = pooled.shape
    rank = v.shape[-1]
    feat = pltpu.VMEM((samp, feats), BF16)
    return pl.pallas_call(
        middle_kernel,
        in_specs=[smem()] + [vmem()] * 7,
        out_specs=[vmem()] * 4,
        out_shape=[feat, feat, pltpu.VMEM((samp, rank), F32), pltpu.VMEM((samp, rank), BF16)],
        scratch_shapes=[pltpu.VMEM((2, samp, rank), BF16)],
        compiler_params=params(16),
        cost_estimate=cost(1 << 31, 8 << 20),
        name="middle",
    )(core, mine, other, bias, *kept(pooled, cot, u, v))


def row_grads(turned_ref, table, first, count, grad):
    return jnp.dot(turned_ref[table, first : first + count, :], grad, preferred_element_type=F32)


def far_kernel(core_ref, mine_ref, other_ref, b_ref, *refs):
    turned, refs = refs[:2], refs[2:]
    pooled, cot, x1, a, u_ref, v_ref, crossed_ref, grad_ref, far_a, far_b, sums = refs
    half, rows, emb = far_a.shape
    spread(core_ref, mine_ref, other_ref, sums)
    for f in range(pooled.shape[1] // WIDE):
        at = slice(f * WIDE, (f + 1) * WIDE)
        h1 = jnp.dot(sums[0], u_ref[1, :, at], preferred_element_type=F32) + b_ref[1:2, at]
        crossed_ref[:, at] = (pooled[:, at].astype(F32) * h1 + x1[:, at].astype(F32)).astype(BF16)
        grad = cot[:, at].astype(F32) * h1 + a[:, at].astype(F32)
        grad = (grad + lax.dot_general(sums[1], v_ref[0, at, :], NT, preferred_element_type=F32)).astype(BF16)
        grad_ref[:, at] = grad
        for i in range(2):
            side, t = divmod(2 * f + i, half)
            part = row_grads(turned[side], t, 2 * rows, rows, grad[:, i * emb : (i + 1) * emb])
            (far_a, far_b)[side][t] = part.astype(BF16)


def far_rows(core, mine, other, bias, turned, pooled, cot, x1, a, u, v):
    half, rows, samp = turned[0].shape
    rank = v.shape[-1]
    feats = pooled.shape[1]
    piece = pltpu.VMEM((half, rows // 4, feats // (2 * half)), BF16)
    return pl.pallas_call(
        far_kernel,
        in_specs=[smem()] + [vmem()] * 11,
        out_specs=[vmem()] * 4,
        out_shape=[pltpu.VMEM(pooled.shape, BF16)] * 2 + [piece, piece],
        scratch_shapes=[pltpu.VMEM((2, samp, rank), BF16)],
        compiler_params=params(16),
        cost_estimate=cost(5 << 28, 7 << 20),
        name="far_rows",
    )(core, mine, other, bias, *kept(*turned, pooled, cot, x1, a, u, v))


def near_kernel(*refs):
    turned, refs = refs[:2], refs[2:]
    grad, made_ref, crossed_ref, p0_ref, p1_a, p1_b, p3_a, p3_b, sem = refs
    copy = pltpu.make_async_copy(made_ref, crossed_ref, sem)
    copy.start()
    half, rows, emb = p1_a.shape
    for t in range(2 * half):
        side, at = divmod(t, half)
        part = grad[:, t * emb : (t + 1) * emb]
        first = row_grads(turned[side], at, 0, 2 * rows, part)
        p0_ref[t] = first[:rows]
        (p1_a, p1_b)[side][at] = first[rows:].astype(BF16)
        (p3_a, p3_b)[side][at] = row_grads(turned[side], at, 3 * rows, rows, part).astype(BF16)
    copy.wait()


def near_rows(turned, grad, crossed):
    half, rows, samp = turned[0].shape
    block = (half, rows // 4, grad.shape[1] // (2 * half))
    return pl.pallas_call(
        near_kernel,
        in_specs=[vmem()] * 4,
        out_specs=[anyspace()] + [vmem()] * 5,
        out_shape=[pltpu.HBM(crossed.shape, BF16), pltpu.VMEM((2 * half,) + block[1:], F32)]
        + [pltpu.VMEM(block, BF16)] * 4,
        scratch_shapes=[pltpu.SemaphoreType.DMA],
        compiler_params=params(16),
        cost_estimate=cost(3 << 28, 7 << 20),
        name="near_rows",
    )(*kept(*turned, grad, crossed))


def finish_kernel(p0, sum_ref, far_ref, *refs, side):
    out_ref, held, sem = refs[-3:]
    half = held.shape[0]
    held[...] = p0[side * half : (side + 1) * half] + (sum_ref[...].astype(F32) + far_ref[...].astype(F32))
    copy = pltpu.make_async_copy(held, out_ref.at[pl.ds(side * half, half)], sem)
    copy.start()
    copy.wait()


def finish(side, before, p0, near, far):
    return pl.pallas_call(
        functools.partial(finish_kernel, side=side),
        in_specs=[vmem()] * 3 + [anyspace()] * len(before),
        out_specs=anyspace(),
        out_shape=pltpu.HBM(p0.shape, F32),
        scratch_shapes=[pltpu.VMEM(near.shape, F32), pltpu.SemaphoreType.DMA],
        input_output_aliases={3: 0} if before else {},
        compiler_params=params(8),
        cost_estimate=cost(1 << 20, 1 << 20),
        name="finish",
    )(*kept(p0), near, far, *before)


def right(arr):
    return lax.ppermute(arr, "row", [(i, (i + 1) & 3) for i in range(4)])


def left(arr):
    return lax.ppermute(arr, "row", [(i, (i + 3) & 3) for i in range(4)])


def add(a, b):
    return a.astype(F32) + b.astype(F32)


def scalar(axis):
    return lax.axis_index(axis).astype(jnp.int32).reshape(1)


def local(emb_rows, entry_ids, entry_sample, cross_v, cross_u, cross_bias, cotangent):
    samp = cotangent.shape[0]
    rows = emb_rows.shape[1] * lax.axis_size("row")
    mine, core = scalar("row"), scalar("c")
    own_a, own_b = cast_halves(emb_rows)
    left_a, right_b = right(own_a), left(own_b)
    left_b, right_a = right(own_b), left(own_a)
    counts_a, turned_a, edges, ids, owners = make_counts(mine, entry_ids, entry_sample, samp, rows)
    left_a, right_b, edges = lax.optimization_barrier((left_a, right_b, edges))
    far_a, far_b = right(left_a), left(right_b)
    loads = (cotangent, cross_v, cross_u)
    counts_b, turned_b, cot, v, u = make_counts(mine, ids, owners, samp, rows, edges, loads)
    embs = (own_a, own_b, right_a, right_b, far_a, far_b, left_a, left_b)
    pooled, keep, send = first_sums(core, (counts_a, counts_b), embs, cot, v, u)
    sums = sum_all(keep, send, False)
    x1, a, keep, send = middle(core, *sums, cross_bias, pooled, cot, u, v)
    sums = sum_all(keep, send, True)
    turned = (turned_a, turned_b)
    crossed, grad, p2a, p2b = far_rows(core, *sums, cross_bias, turned, pooled, cot, x1, a, u, v)
    from_left, from_right = right(p2a), left(p2b)
    crossed, p0, p1a, p1b, p3a, p3b = near_rows(turned, grad, crossed)
    sum_b, sum_a = right(p1b), left(p3a)
    far_a = right(add(p1a, from_left).astype(BF16))
    far_b = left(add(p3b, from_right).astype(BF16))
    grads = finish(0, (), p0, sum_a, far_a)
    return crossed, finish(1, (grads,), p0, sum_b, far_b)


def solution(mesh):
    fine = jax.sharding.Mesh(mesh.devices.reshape(4, 4, 2, 2, 4), ("x", "zh", "zl", "c", "row"))
    table = ("x", "zh", "zl", "c")
    placed = (
        P(table, "row", None),
        P(table, None),
        P(table, None),
        P(None, table, None),
        P(None, None, table),
        P(None, table),
        P("row", table),
    )
    return jax.shard_map(
        local,
        mesh=fine,
        in_specs=placed,
        out_specs=(P("row", table), P(table, "row", None)),
        check_vma=False,
    )
```

```python
import functools

import jax
import jax.numpy as jnp
from jax import lax
from jax.experimental import pallas as pl
from jax.experimental.pallas import tpu as pltpu
from jax.sharding import PartitionSpec as P

F32 = jnp.float32
BF16 = jnp.bfloat16
EB = 512
NT = (((1,), (1,)), ((), ()))
TN = (((0,), (0,)), ((), ()))


def vmem():
    return pl.BlockSpec(memory_space=pltpu.VMEM)


def smem():
    return pl.BlockSpec(memory_space=pltpu.SMEM)


def params(mib):
    return pltpu.CompilerParams(vmem_limit_bytes=mib * 2**20)


def cost(flops, moved):
    return pl.CostEstimate(flops=flops, bytes_accessed=moved, transcendentals=0)


def pinned(arr):
    return pltpu.with_memory_space_constraint(arr, pltpu.HBM)


def kept(*arrs):
    return [pltpu.with_memory_space_constraint(arr, pltpu.VMEM) for arr in arrs]


def hbm():
    return pl.BlockSpec(memory_space=pltpu.HBM)


def cast_kernel(in_ref, a_ref, b_ref, held, sems):
    half = a_ref.shape[0]
    copies = fetch(sems, [(in_ref.at[i], held.at[i]) for i in range(2 * half)])
    for i, copy in enumerate(copies):
        copy.wait()
        (a_ref, b_ref)[i // half][i % half] = held[i].astype(BF16)


def cast_halves(emb_rows):
    tabs, rows, emb = emb_rows.shape
    half = (tabs // 2, rows, emb)
    return pl.pallas_call(
        cast_kernel,
        in_specs=[hbm()],
        out_specs=[vmem()] * 2,
        out_shape=[pltpu.VMEM(half, BF16)] * 2,
        scratch_shapes=[pltpu.VMEM(emb_rows.shape, F32), pltpu.SemaphoreType.DMA((tabs,))],
        compiler_params=params(4),
        cost_estimate=cost(1 << 18, 3 << 19),
        name="cast",
    )(pinned(emb_rows))


def counts_kernel(mine_ref, ids_ref, own_ref, *refs, first_table):
    refs, (acc_ref, ids, own, sems) = refs[:-4], refs[-4:]
    if first_table:
        edges_ref, *loads = refs[: len(refs) // 2]
        out_ref, turned_ref, *loaded = refs[len(refs) // 2 :]
    else:
        out_ref, turned_ref, edges_ref = refs
        loads = loaded = ()
    copies = fetch(sems, [(own_ref, own), (ids_ref, ids), *zip(loads, loaded)])
    _, rows, samp = acc_ref.shape
    tabs, entries = own.shape
    mine = mine_ref[0]
    low = mine * samp
    turn = mine * (rows // 4)
    copies[0].wait()
    if not first_table:
        owners = own[...]
        first = jnp.sum((owners < low).astype(jnp.int32), axis=1, keepdims=True)
        last = jnp.sum((owners < low + samp).astype(jnp.int32), axis=1, keepdims=True)
        for i in range(tabs):
            edges_ref[i] = first[i, 0]
            edges_ref[tabs + i] = last[i, 0]
    copies[1].wait()
    grid = lax.broadcasted_iota(jnp.int32, (samp, EB), 0).astype(F32).astype(BF16)
    one, zero = jnp.ones((), BF16), jnp.zeros((), BF16)

    @pl.loop(0, out_ref.shape[0] // 2)
    def _(pair):
        tables = [first_table + 2 * pair + j for j in range(2)]
        starts = [edges_ref[t] // 128 for t in tables]
        spans = [edges_ref[tabs + t] - start * 128 for t, start in zip(tables, starts)]
        steps = (jnp.maximum(*spans) + EB - 1) // EB
        starts = [jnp.minimum(start, (entries - steps * EB) // 128) * 128 for start in starts]
        acc_ref[...] = jnp.zeros_like(acc_ref)

        def body(block, carry):
            for j, t in enumerate(tables):
                at = pl.ds(pl.multiple_of(starts[j] + block * EB, 128), EB)
                who = own[pl.ds(t, 1), at] - low
                row = (ids[pl.ds(t, 1), at] - turn) & (rows - 1)
                hot = [
                    jnp.where(grid == values.astype(F32).astype(BF16), one, zero) for values in (who, row, row - samp)
                ]
                acc_ref[j] += lax.dot_general(
                    jnp.concatenate(hot[1:], axis=0), hot[0], NT, preferred_element_type=F32
                )
            return carry

        lax.fori_loop(0, steps, body, 0)
        for j in range(2):
            total = acc_ref[j].astype(BF16)
            turned_ref[2 * pair + j] = total
            out_ref[2 * pair + j] = total.T

    for copy in copies[2:]:
        copy.wait()


def make_counts(mine, ids, owners, samp, rows, edges=None, loads=()):
    tabs, entries = ids.shape
    assert rows == 2 * samp and samp <= 256
    half = tabs // 2
    out_shape = [pltpu.VMEM((half, samp, rows), BF16), pltpu.VMEM((half, rows, samp), BF16)]
    args = (mine, pinned(ids), pinned(owners))
    in_specs, out_specs = [smem(), hbm(), hbm()], [vmem(), vmem()]
    if edges is None:
        out_specs.append(smem())
        out_shape.append(jax.ShapeDtypeStruct((2 * tabs,), jnp.int32))
    else:
        args += (edges, *map(pinned, loads))
        in_specs += [smem()] + [hbm()] * len(loads)
        out_specs += [vmem()] * len(loads)
        out_shape += [pltpu.VMEM(arr.shape, arr.dtype) for arr in loads]
    return pl.pallas_call(
        functools.partial(counts_kernel, first_table=0 if edges is None else half),
        in_specs=in_specs,
        out_specs=out_specs,
        out_shape=out_shape,
        scratch_shapes=[
            pltpu.VMEM((2, rows, samp), F32),
            pltpu.VMEM((tabs, entries), jnp.int32),
            pltpu.VMEM((tabs, entries), jnp.int32),
            pltpu.SemaphoreType.DMA((2 + len(loads),)),
        ],
        compiler_params=params(6),
        cost_estimate=cost(half * samp * rows * 3072, 3 << 20),
        name="counts",
    )(*args)


WIDE = 512


def fetch(sems, pairs):
    copies = [pltpu.make_async_copy(src, dst, sems.at[i]) for i, (src, dst) in enumerate(pairs)]
    for copy in copies:
        copy.start()
    return copies


def sum_z(x, v_ref, layer):
    return jnp.dot(x[...], v_ref[layer], preferred_element_type=F32)


def sum_g(wide, u_ref, layer):
    return lax.dot_general(wide[...], u_ref[layer], NT, preferred_element_type=F32)


def one_sum(even, x, wide, v_ref, u_ref, layer, out_ref):
    @pl.when(even)
    def _():
        out_ref[...] = sum_z(x, v_ref, layer).astype(out_ref.dtype)

    @pl.when(jnp.logical_not(even))
    def _():
        out_ref[...] = sum_g(wide, u_ref, 1 - layer).astype(out_ref.dtype)


def keep_kernel(core_ref, x, wide, v_ref, u_ref, out_ref, *, layer):
    one_sum(core_ref[0] == 0, x, wide, v_ref, u_ref, layer, out_ref)


def keep_sum(core, x, wide, v, u, layer):
    return pl.pallas_call(
        functools.partial(keep_kernel, layer=layer),
        in_specs=[smem()] + [vmem()] * 4,
        out_specs=vmem(),
        out_shape=pltpu.VMEM((x.shape[0], v.shape[-1]), F32),
        compiler_params=params(8),
        cost_estimate=cost(1 << 29, 4 << 20),
        name="keep_sum",
    )(core, *kept(x, wide, v, u))


def anyspace():
    return pl.BlockSpec(memory_space=pl.ANY)


def first_kernel(core_ref, counts_a, counts_b, *refs):
    embs, (cot, v_ref, u_ref, pooled_ref, wide_ref, send_ref) = refs[:8], refs[8:]
    half, _, emb = embs[0].shape
    for t in range(2 * half):
        side, i = divmod(t, half)
        rows = jnp.concatenate([embs[2 * k + side][i] for k in range(4)], axis=0)
        pooled = jnp.dot((counts_a, counts_b)[side][i], rows, preferred_element_type=F32).astype(BF16)
        at = slice(t * emb, (t + 1) * emb)
        pooled_ref[:, at] = pooled
        wide_ref[:, at] = (cot[:, at].astype(F32) * pooled.astype(F32)).astype(BF16)
    one_sum(core_ref[0] != 0, pooled_ref, wide_ref, v_ref, u_ref, 0, send_ref)


def first_sums(core, counts, embs, cot, v, u):
    half, samp, rows = counts[0].shape
    emb = embs[0].shape[-1]
    rank = v.shape[-1]
    return pl.pallas_call(
        first_kernel,
        in_specs=[smem()] + [vmem()] * 13,
        out_specs=[vmem()] * 3,
        out_shape=[
            pltpu.VMEM((samp, 2 * half * emb), BF16),
            pltpu.VMEM((samp, 2 * half * emb), BF16),
            pltpu.VMEM((samp, rank), BF16),
        ],
        compiler_params=params(8),
        cost_estimate=cost(3 << 29, 10 << 20),
        name="first_sums",
    )(core, *kept(*counts), *embs, *kept(cot, v, u))


def swap(arr, axis):
    return lax.ppermute(arr, axis, [(0, 1), (1, 0)])


def small(kernel, out_shape, name, *args):
    return pl.pallas_call(
        kernel,
        in_specs=[vmem()] * len(args),
        out_specs=jax.tree.map(lambda _: vmem(), out_shape),
        out_shape=out_shape,
        compiler_params=params(8),
        cost_estimate=cost(1 << 20, 1 << 20),
        name=name,
    )(*args)


CHUNKS = 8
CHUNK = (32, 512)


def chunk_at(i):
    return slice(CHUNK[0] * i, CHUNK[0] * (i + 1)), slice(None)


def cut_kernel(keep_ref, got_ref, out_ref):
    for i in range(CHUNKS):
        at = chunk_at(i)
        out_ref[i] = (keep_ref[at] + got_ref[at].astype(F32)).astype(BF16)


def total_kernel(*refs):
    *ins, out_ref = refs
    total = sum(ref[i].astype(F32) for ref in ins for i in range(ref.shape[0])).astype(BF16)
    for i in range(out_ref.shape[0]):
        out_ref[i] = total


def total(copies, *arrays):
    return small(total_kernel, pltpu.VMEM((copies,) + CHUNK, BF16), "total", *arrays)


def swap_all(arr):
    return lax.all_to_all(arr, ("x", "zl"), 0, 0, tiled=True)


def turn(arr, k):
    return lax.ppermute(arr, "zh", [(i, (i + k) & 3) for i in range(4)])


def sum_all(core, send, x, wide, v, u, layer):
    send, x = lax.optimization_barrier((send, x))
    got, keep = lax.optimization_barrier((swap(send, "c"), keep_sum(core, x, wide, v, u, layer)))
    shape = pltpu.VMEM((CHUNKS,) + CHUNK, BF16)
    parts = swap_all(small(cut_kernel, shape, "cut", keep, got))
    own = total(1, parts)
    mine = swap_all(total(CHUNKS, own, turn(own, 1), turn(own, 3), turn(own, 2)))
    return mine, swap(mine, "c")


def spread(core_ref, mine_ref, other_ref, in_ref):
    core = core_ref[0]
    for side, ref in ((core, mine_ref), (1 - core, other_ref)):
        for i in range(CHUNKS):
            in_ref[(side, *chunk_at(i))] = ref[i]


def middle_kernel(core_ref, mine_ref, other_ref, b_ref, pooled, cot, u_ref, v_ref, x1_ref, a_ref, wide_ref, send_ref, sums):
    spread(core_ref, mine_ref, other_ref, sums)
    for f in range(pooled.shape[1] // WIDE):
        at = slice(f * WIDE, (f + 1) * WIDE)
        base = pooled[:, at].astype(F32)
        h0 = jnp.dot(sums[0], u_ref[0, :, at], preferred_element_type=F32) + b_ref[0:1, at]
        x1_ref[:, at] = (base * h0 + base).astype(BF16)
        g1 = lax.dot_general(sums[1], v_ref[1, at, :], NT, preferred_element_type=F32)
        g1 = cot[:, at].astype(F32) + g1
        a_ref[:, at] = (g1 * h0 + g1).astype(BF16)
        wide_ref[:, at] = (g1 * base).astype(BF16)
    one_sum(core_ref[0] != 0, x1_ref, wide_ref, v_ref, u_ref, 1, send_ref)


def middle(core, mine, other, bias, pooled, cot, u, v):
    samp, feats = pooled.shape
    rank = v.shape[-1]
    feat = pltpu.VMEM((samp, feats), BF16)
    return pl.pallas_call(
        middle_kernel,
        in_specs=[smem()] + [vmem()] * 7,
        out_specs=[vmem()] * 4,
        out_shape=[feat, feat, feat, pltpu.VMEM((samp, rank), BF16)],
        scratch_shapes=[pltpu.VMEM((2, samp, rank), BF16)],
        compiler_params=params(10),
        cost_estimate=cost(1 << 31, 8 << 20),
        name="middle",
    )(core, mine, other, bias, *kept(pooled, cot, u, v))


def row_grads(turned_ref, table, first, count, grad):
    return jnp.dot(turned_ref[table, first : first + count, :], grad, preferred_element_type=F32)


def far_kernel(core_ref, mine_ref, other_ref, b_ref, *refs):
    turned, refs = refs[:2], refs[2:]
    pooled, cot, x1, a, u_ref, v_ref, crossed_ref, grad_ref, far_a, far_b, sums = refs
    half, rows, emb = far_a.shape
    spread(core_ref, mine_ref, other_ref, sums)
    for f in range(pooled.shape[1] // WIDE):
        at = slice(f * WIDE, (f + 1) * WIDE)
        h1 = jnp.dot(sums[0], u_ref[1, :, at], preferred_element_type=F32) + b_ref[1:2, at]
        crossed_ref[:, at] = (pooled[:, at].astype(F32) * h1 + x1[:, at].astype(F32)).astype(BF16)
        grad = cot[:, at].astype(F32) * h1 + a[:, at].astype(F32)
        grad = (grad + lax.dot_general(sums[1], v_ref[0, at, :], NT, preferred_element_type=F32)).astype(BF16)
        grad_ref[:, at] = grad
        for i in range(2):
            side, t = divmod(2 * f + i, half)
            part = row_grads(turned[side], t, 2 * rows, rows, grad[:, i * emb : (i + 1) * emb])
            (far_a, far_b)[side][t] = part.astype(BF16)


def far_rows(core, mine, other, bias, turned, pooled, cot, x1, a, u, v):
    half, rows, samp = turned[0].shape
    rank = v.shape[-1]
    feats = pooled.shape[1]
    piece = pltpu.VMEM((half, rows // 4, feats // (2 * half)), BF16)
    return pl.pallas_call(
        far_kernel,
        in_specs=[smem()] + [vmem()] * 11,
        out_specs=[vmem()] * 4,
        out_shape=[pltpu.VMEM(pooled.shape, BF16)] * 2 + [piece, piece],
        scratch_shapes=[pltpu.VMEM((2, samp, rank), BF16)],
        compiler_params=params(8),
        cost_estimate=cost(5 << 28, 7 << 20),
        name="far_rows",
    )(core, mine, other, bias, *kept(*turned, pooled, cot, x1, a, u, v))


def near_kernel(*refs):
    turned, refs = refs[:2], refs[2:]
    grad, made_ref, crossed_ref, p0_ref, p1_a, p1_b, p3_a, p3_b, sem = refs
    copy = pltpu.make_async_copy(made_ref, crossed_ref, sem)
    copy.start()
    half, rows, emb = p1_a.shape
    for t in range(2 * half):
        side, at = divmod(t, half)
        part = grad[:, t * emb : (t + 1) * emb]
        first = row_grads(turned[side], at, 0, 2 * rows, part)
        p0_ref[t] = first[:rows]
        (p1_a, p1_b)[side][at] = first[rows:].astype(BF16)
        (p3_a, p3_b)[side][at] = row_grads(turned[side], at, 3 * rows, rows, part).astype(BF16)
    copy.wait()


def near_rows(turned, grad, crossed):
    half, rows, samp = turned[0].shape
    block = (half, rows // 4, grad.shape[1] // (2 * half))
    return pl.pallas_call(
        near_kernel,
        in_specs=[vmem()] * 4,
        out_specs=[anyspace()] + [vmem()] * 5,
        out_shape=[pltpu.HBM(crossed.shape, BF16), pltpu.VMEM((2 * half,) + block[1:], F32)]
        + [pltpu.VMEM(block, BF16)] * 4,
        scratch_shapes=[pltpu.SemaphoreType.DMA],
        compiler_params=params(8),
        cost_estimate=cost(3 << 28, 7 << 20),
        name="near_rows",
    )(*kept(*turned, grad, crossed))


def finish_kernel(p0, sum_ref, far_ref, *refs, side):
    out_ref, held, sem = refs[-3:]
    half = held.shape[0]
    held[...] = p0[side * half : (side + 1) * half] + (sum_ref[...].astype(F32) + far_ref[...].astype(F32))
    copy = pltpu.make_async_copy(held, out_ref.at[pl.ds(side * half, half)], sem)
    copy.start()
    copy.wait()


def finish(side, before, p0, near, far):
    return pl.pallas_call(
        functools.partial(finish_kernel, side=side),
        in_specs=[vmem()] * 3 + [anyspace()] * len(before),
        out_specs=anyspace(),
        out_shape=pltpu.HBM(p0.shape, F32),
        scratch_shapes=[pltpu.VMEM(near.shape, F32), pltpu.SemaphoreType.DMA],
        input_output_aliases={3: 0} if before else {},
        compiler_params=params(4),
        cost_estimate=cost(1 << 20, 1 << 20),
        name="finish",
    )(*kept(p0), near, far, *before)


def right(arr):
    return lax.ppermute(arr, "row", [(i, (i + 1) & 3) for i in range(4)])


def left(arr):
    return lax.ppermute(arr, "row", [(i, (i + 3) & 3) for i in range(4)])


def add(a, b):
    return a.astype(F32) + b.astype(F32)


def scalar(axis):
    return lax.axis_index(axis).astype(jnp.int32).reshape(1)


def local(emb_rows, entry_ids, entry_sample, cross_v, cross_u, cross_bias, cotangent):
    samp = cotangent.shape[0]
    rows = emb_rows.shape[1] * lax.axis_size("row")
    mine, core = scalar("row"), scalar("c")
    own_a, own_b = cast_halves(emb_rows)
    left_a, right_b = right(own_a), left(own_b)
    left_b, right_a = right(own_b), left(own_a)
    counts_a, turned_a, edges = make_counts(mine, entry_ids, entry_sample, samp, rows)
    left_a, right_b, edges = lax.optimization_barrier((left_a, right_b, edges))
    far_a, far_b = right(left_a), left(right_b)
    loads = (cotangent, cross_v, cross_u)
    counts_b, turned_b, cot, v, u = make_counts(mine, entry_ids, entry_sample, samp, rows, edges, loads)
    embs = (own_a, own_b, right_a, right_b, far_a, far_b, left_a, left_b)
    pooled, wide, send = first_sums(core, (counts_a, counts_b), embs, cot, v, u)
    sums = sum_all(core, send, pooled, wide, v, u, 0)
    x1, a, wide, send = middle(core, *sums, cross_bias, pooled, cot, u, v)
    sums = sum_all(core, send, x1, wide, v, u, 1)
    turned = (turned_a, turned_b)
    crossed, grad, p2a, p2b = far_rows(core, *sums, cross_bias, turned, pooled, cot, x1, a, u, v)
    from_left, from_right = right(p2a), left(p2b)
    crossed, p0, p1a, p1b, p3a, p3b = near_rows(turned, grad, crossed)
    sum_b, sum_a = right(p1b), left(p3a)
    far_a = right(add(p1a, from_left).astype(BF16))
    far_b = left(add(p3b, from_right).astype(BF16))
    grads = finish(0, (), p0, sum_a, far_a)
    return crossed, finish(1, (grads,), p0, sum_b, far_b)


def solution(mesh):
    fine = jax.sharding.Mesh(mesh.devices.reshape(4, 4, 2, 2, 4), ("x", "zh", "zl", "c", "row"))
    table = ("x", "zh", "zl", "c")
    placed = (
        P(table, "row", None),
        P(table, None),
        P(table, None),
        P(None, table, None),
        P(None, None, table),
        P(None, table),
        P("row", table),
    )
    return jax.shard_map(
        local,
        mesh=fine,
        in_specs=placed,
        out_specs=(P("row", table), P(table, "row", None)),
        check_vma=False,
    )
```

```python
import functools

import jax
import jax.numpy as jnp
from jax import lax
from jax.experimental import pallas as pl
from jax.experimental.pallas import tpu as pltpu
from jax.sharding import PartitionSpec as P

F32 = jnp.float32
BF16 = jnp.bfloat16
EB = 512
NT = (((1,), (1,)), ((), ()))
TN = (((0,), (0,)), ((), ()))


def vmem():
    return pl.BlockSpec(memory_space=pltpu.VMEM)


def smem():
    return pl.BlockSpec(memory_space=pltpu.SMEM)


def params(mib):
    return pltpu.CompilerParams(vmem_limit_bytes=mib * 2**20)


def cost(flops, moved):
    return pl.CostEstimate(flops=flops, bytes_accessed=moved, transcendentals=0)


def pinned(arr):
    return pltpu.with_memory_space_constraint(arr, pltpu.HBM)


def kept(*arrs):
    return [pltpu.with_memory_space_constraint(arr, pltpu.VMEM) for arr in arrs]


def hbm():
    return pl.BlockSpec(memory_space=pltpu.HBM)


def cast_kernel(in_ref, a_ref, b_ref, held, sems):
    half = a_ref.shape[0]
    outs = (a_ref, b_ref)
    copies = fetch(sems, [(in_ref.at[pl.ds(i * half, half)], held.at[i]) for i in range(2)])
    for i in range(2):
        copies[i].wait()
        outs[i][...] = held[i].astype(BF16)


def cast_halves(emb_rows):
    tabs, rows, emb = emb_rows.shape
    half = (tabs // 2, rows, emb)
    return pl.pallas_call(
        cast_kernel,
        in_specs=[hbm()],
        out_specs=[vmem()] * 2,
        out_shape=[pltpu.VMEM(half, BF16)] * 2,
        scratch_shapes=[pltpu.VMEM((2,) + half, F32), pltpu.SemaphoreType.DMA((2,))],
        compiler_params=params(4),
        cost_estimate=cost(1 << 18, 3 << 19),
        name="cast",
    )(pinned(emb_rows))


def counts_kernel(mine_ref, ids_ref, own_ref, *refs, first_table):
    refs, (acc_ref, ids, own, sems) = refs[:-4], refs[-4:]
    if first_table:
        edges_ref, *loads = refs[: len(refs) // 2]
        out_ref, *loaded = refs[len(refs) // 2 :]
    else:
        out_ref, edges_ref = refs
        loads = loaded = ()
    copies = fetch(sems, [(own_ref, own), (ids_ref, ids), *zip(loads, loaded)])
    _, rows, samp = acc_ref.shape
    tabs, entries = own.shape
    mine = mine_ref[0]
    low = mine * samp
    turn = mine * (rows // 4)
    copies[0].wait()
    if not first_table:
        owners = own[...]
        first = jnp.sum((owners < low).astype(jnp.int32), axis=1, keepdims=True)
        last = jnp.sum((owners < low + samp).astype(jnp.int32), axis=1, keepdims=True)
        for i in range(tabs):
            edges_ref[i] = first[i, 0]
            edges_ref[tabs + i] = last[i, 0]
    copies[1].wait()
    grid = lax.broadcasted_iota(jnp.int32, (samp, EB), 0).astype(F32).astype(BF16)
    one, zero = jnp.ones((), BF16), jnp.zeros((), BF16)

    @pl.loop(0, out_ref.shape[0] // 2)
    def _(pair):
        tables = [first_table + 2 * pair + j for j in range(2)]
        starts = [edges_ref[t] // 128 for t in tables]
        spans = [edges_ref[tabs + t] - start * 128 for t, start in zip(tables, starts)]
        steps = (jnp.maximum(*spans) + EB - 1) // EB
        starts = [jnp.minimum(start, (entries - steps * EB) // 128) * 128 for start in starts]
        acc_ref[...] = jnp.zeros_like(acc_ref)

        def body(block, carry):
            for j, t in enumerate(tables):
                at = pl.ds(pl.multiple_of(starts[j] + block * EB, 128), EB)
                who = own[pl.ds(t, 1), at] - low
                row = (ids[pl.ds(t, 1), at] - turn) & (rows - 1)
                hot = [
                    jnp.where(grid == values.astype(F32).astype(BF16), one, zero) for values in (who, row, row - samp)
                ]
                acc_ref[j] += lax.dot_general(
                    jnp.concatenate(hot[1:], axis=0), hot[0], NT, preferred_element_type=F32
                )
            return carry

        lax.fori_loop(0, steps, body, 0)
        for j in range(2):
            out_ref[2 * pair + j] = acc_ref[j].astype(BF16).T

    for copy in copies[2:]:
        copy.wait()


def make_counts(mine, ids, owners, samp, rows, edges=None, loads=()):
    tabs, entries = ids.shape
    assert rows == 2 * samp and samp <= 256
    half = tabs // 2
    out_shape = [pltpu.VMEM((half, samp, rows), BF16)]
    args = (mine, pinned(ids), pinned(owners))
    in_specs, out_specs = [smem(), hbm(), hbm()], [vmem()]
    if edges is None:
        out_specs.append(smem())
        out_shape.append(jax.ShapeDtypeStruct((2 * tabs,), jnp.int32))
    else:
        args += (edges, *map(pinned, loads))
        in_specs += [smem()] + [hbm()] * len(loads)
        out_specs += [vmem()] * len(loads)
        out_shape += [pltpu.VMEM(arr.shape, arr.dtype) for arr in loads]
    return pl.pallas_call(
        functools.partial(counts_kernel, first_table=0 if edges is None else half),
        in_specs=in_specs,
        out_specs=out_specs,
        out_shape=out_shape,
        scratch_shapes=[
            pltpu.VMEM((2, rows, samp), F32),
            pltpu.VMEM((tabs, entries), jnp.int32),
            pltpu.VMEM((tabs, entries), jnp.int32),
            pltpu.SemaphoreType.DMA((2 + len(loads),)),
        ],
        compiler_params=params(6),
        cost_estimate=cost(half * samp * rows * 3072, 3 << 20),
        name="counts",
    )(*args)


def turned_kernel(in_ref, out_ref):
    for i in range(out_ref.shape[0]):
        out_ref[i] = in_ref[i].T


def turned_counts(counts):
    half, samp, rows = counts.shape
    return pl.pallas_call(
        turned_kernel,
        in_specs=[vmem()],
        out_specs=vmem(),
        out_shape=pltpu.VMEM((half, rows, samp), BF16),
        compiler_params=params(8),
        cost_estimate=cost(1 << 29, 2 << 20),
        name="turned",
    )(*kept(counts))


WIDE = 512


def fetch(sems, pairs):
    copies = [pltpu.make_async_copy(src, dst, sems.at[i]) for i, (src, dst) in enumerate(pairs)]
    for copy in copies:
        copy.start()
    return copies


def sum_z(x, v_ref, layer):
    return jnp.dot(x[...], v_ref[layer], preferred_element_type=F32)


def sum_g(wide, u_ref, layer):
    return lax.dot_general(wide[...], u_ref[layer], NT, preferred_element_type=F32)


def one_sum(even, x, wide, v_ref, u_ref, layer, out_ref):
    @pl.when(even)
    def _():
        out_ref[...] = sum_z(x, v_ref, layer).astype(out_ref.dtype)

    @pl.when(jnp.logical_not(even))
    def _():
        out_ref[...] = sum_g(wide, u_ref, 1 - layer).astype(out_ref.dtype)


def keep_kernel(core_ref, x, wide, v_ref, u_ref, out_ref, *, layer):
    one_sum(core_ref[0] == 0, x, wide, v_ref, u_ref, layer, out_ref)


def keep_sum(core, x, wide, v, u, layer):
    return pl.pallas_call(
        functools.partial(keep_kernel, layer=layer),
        in_specs=[smem()] + [vmem()] * 4,
        out_specs=vmem(),
        out_shape=pltpu.VMEM((x.shape[0], v.shape[-1]), F32),
        compiler_params=params(8),
        cost_estimate=cost(1 << 29, 4 << 20),
        name="keep_sum",
    )(core, *kept(x, wide, v, u))


def anyspace():
    return pl.BlockSpec(memory_space=pl.ANY)


def first_kernel(core_ref, counts_a, counts_b, *refs):
    embs, (cot, v_ref, u_ref, pooled_ref, wide_ref, send_ref) = refs[:8], refs[8:]
    half, _, emb = embs[0].shape
    for t in range(2 * half):
        side, i = divmod(t, half)
        rows = jnp.concatenate([embs[2 * k + side][i] for k in range(4)], axis=0)
        pooled = jnp.dot((counts_a, counts_b)[side][i], rows, preferred_element_type=F32).astype(BF16)
        at = slice(t * emb, (t + 1) * emb)
        pooled_ref[:, at] = pooled
        wide_ref[:, at] = (cot[:, at].astype(F32) * pooled.astype(F32)).astype(BF16)
    one_sum(core_ref[0] != 0, pooled_ref, wide_ref, v_ref, u_ref, 0, send_ref)


def first_sums(core, counts, embs, cot, v, u):
    half, samp, rows = counts[0].shape
    emb = embs[0].shape[-1]
    rank = v.shape[-1]
    return pl.pallas_call(
        first_kernel,
        in_specs=[smem()] + [vmem()] * 13,
        out_specs=[vmem()] * 3,
        out_shape=[
            pltpu.VMEM((samp, 2 * half * emb), BF16),
            pltpu.VMEM((samp, 2 * half * emb), BF16),
            pltpu.VMEM((samp, rank), BF16),
        ],
        compiler_params=params(8),
        cost_estimate=cost(3 << 29, 10 << 20),
        name="first_sums",
    )(core, *kept(*counts), *embs, *kept(cot, v, u))


def swap(arr, axis):
    return lax.ppermute(arr, axis, [(0, 1), (1, 0)])


def small(kernel, out_shape, name, *args):
    return pl.pallas_call(
        kernel,
        in_specs=[vmem()] * len(args),
        out_specs=jax.tree.map(lambda _: vmem(), out_shape),
        out_shape=out_shape,
        compiler_params=params(8),
        cost_estimate=cost(1 << 20, 1 << 20),
        name=name,
    )(*args)


CHUNKS = 8
CHUNK = (32, 512)


def chunk_at(i):
    return slice(CHUNK[0] * i, CHUNK[0] * (i + 1)), slice(None)


def cut_kernel(keep_ref, got_ref, out_ref):
    for i in range(CHUNKS):
        at = chunk_at(i)
        out_ref[i] = (keep_ref[at] + got_ref[at].astype(F32)).astype(BF16)


def total_kernel(*refs):
    *ins, out_ref = refs
    total = sum(ref[i].astype(F32) for ref in ins for i in range(ref.shape[0])).astype(BF16)
    for i in range(out_ref.shape[0]):
        out_ref[i] = total


def total(copies, *arrays):
    return small(total_kernel, pltpu.VMEM((copies,) + CHUNK, BF16), "total", *arrays)


def swap_all(arr):
    return lax.all_to_all(arr, ("x", "zl"), 0, 0, tiled=True)


def turn(arr, k):
    return lax.ppermute(arr, "zh", [(i, (i + k) & 3) for i in range(4)])


def layout(chunks_ref, sum_ref):
    for i in range(CHUNKS):
        sum_ref[chunk_at(i)] = chunks_ref[i]


def z_u(total, u_ref, layer, at):
    return jnp.dot(total, u_ref[layer, :, at], preferred_element_type=F32)


def g_v(total, v_ref, layer, at):
    return lax.dot_general(total, v_ref[layer, at, :], NT, preferred_element_type=F32)


def steps_of(feats):
    return [slice(f, f + WIDE) for f in range(0, feats, WIDE)]


def product_kernel(core_ref, mine_ref, v_ref, u_ref, out_ref, sum_ref, *, layer):
    layout(mine_ref, sum_ref)

    @pl.when(core_ref[0] == 0)
    def _():
        for at in steps_of(out_ref.shape[1]):
            out_ref[:, at] = z_u(sum_ref[...], u_ref, layer, at)

    @pl.when(core_ref[0] != 0)
    def _():
        for at in steps_of(out_ref.shape[1]):
            out_ref[:, at] = g_v(sum_ref[...], v_ref, 1 - layer, at)


def product(core, mine, v, u, layer):
    samp, rank = CHUNKS * CHUNK[0], CHUNK[1]
    return pl.pallas_call(
        functools.partial(product_kernel, layer=layer),
        in_specs=[smem()] + [vmem()] * 3,
        out_specs=vmem(),
        out_shape=pltpu.VMEM((samp, u.shape[-1]), F32),
        scratch_shapes=[pltpu.VMEM((samp, rank), BF16)],
        compiler_params=params(8),
        cost_estimate=cost(1 << 29, 4 << 20),
        name="product",
    )(core, mine, *kept(v, u))


def by_core(core_ref, body, prod, sum_ref, v_ref, u_ref, layer):
    @pl.when(core_ref[0] == 0)
    def _():
        body(lambda at: prod[:, at], lambda at: g_v(sum_ref[...], v_ref, 1 - layer, at))

    @pl.when(core_ref[0] != 0)
    def _():
        body(lambda at: z_u(sum_ref[...], u_ref, layer, at), lambda at: prod[:, at])


def sum_all(core, send, x, wide, v, u, layer, counts):
    send, x = lax.optimization_barrier((send, x))
    got, keep = lax.optimization_barrier((swap(send, "c"), keep_sum(core, x, wide, v, u, layer)))
    shape = pltpu.VMEM((CHUNKS,) + CHUNK, BF16)
    parts = swap_all(small(cut_kernel, shape, "cut", keep, got))
    own, counts = lax.optimization_barrier((total(1, parts), counts))
    near = (turn(own, 1), turn(own, 3), turn(own, 2), turned_counts(counts))
    *near, turned = lax.optimization_barrier(near)
    mine = swap_all(total(CHUNKS, own, *near))
    prod, other = lax.optimization_barrier((product(core, mine, v, u, layer), swap(mine, "c")))
    return prod, other, turned


def middle_kernel(core_ref, prod, other_ref, b_ref, pooled, cot, u_ref, v_ref, x1_ref, a_ref, wide_ref, send_ref, sum_ref):
    layout(other_ref, sum_ref)

    def body(h, g):
        for at in steps_of(pooled.shape[1]):
            base = pooled[:, at].astype(F32)
            h0 = h(at) + b_ref[0:1, at]
            x1_ref[:, at] = (base * h0 + base).astype(BF16)
            g1 = cot[:, at].astype(F32) + g(at)
            a_ref[:, at] = (g1 * h0 + g1).astype(BF16)
            wide_ref[:, at] = (g1 * base).astype(BF16)

    by_core(core_ref, body, prod, sum_ref, v_ref, u_ref, 0)
    one_sum(core_ref[0] != 0, x1_ref, wide_ref, v_ref, u_ref, 1, send_ref)


def middle(core, prod, other, bias, pooled, cot, u, v):
    samp, feats = pooled.shape
    rank = v.shape[-1]
    feat = pltpu.VMEM((samp, feats), BF16)
    return pl.pallas_call(
        middle_kernel,
        in_specs=[smem()] + [vmem()] * 7,
        out_specs=[vmem()] * 4,
        out_shape=[feat, feat, feat, pltpu.VMEM((samp, rank), BF16)],
        scratch_shapes=[pltpu.VMEM((samp, rank), BF16)],
        compiler_params=params(10),
        cost_estimate=cost(1 << 31, 8 << 20),
        name="middle",
    )(core, *kept(prod), other, bias, *kept(pooled, cot, u, v))


def row_grads(turned_ref, table, first, count, grad):
    return jnp.dot(turned_ref[table, first : first + count, :], grad, preferred_element_type=F32)


def far_kernel(core_ref, prod, other_ref, b_ref, turned_a, turned_b, pooled, cot, x1, a, u_ref, v_ref, *refs):
    crossed_ref, grad_ref, far_a, far_b, sum_ref = refs
    half, rows, emb = far_a.shape
    layout(other_ref, sum_ref)

    def body(h, g):
        for at in steps_of(pooled.shape[1]):
            h1 = h(at) + b_ref[1:2, at]
            crossed_ref[:, at] = (pooled[:, at].astype(F32) * h1 + x1[:, at].astype(F32)).astype(BF16)
            grad_ref[:, at] = (cot[:, at].astype(F32) * h1 + a[:, at].astype(F32) + g(at)).astype(BF16)

    by_core(core_ref, body, prod, sum_ref, v_ref, u_ref, 1)
    for t in range(2 * half):
        side, i = divmod(t, half)
        part = row_grads((turned_a, turned_b)[side], i, 2 * rows, rows, grad_ref[:, t * emb : (t + 1) * emb])
        (far_a, far_b)[side][i] = part.astype(BF16)


def far_rows(core, prod, other, bias, turned, pooled, cot, x1, a, u, v):
    half, rows, samp = turned[0].shape
    rank = v.shape[-1]
    feats = pooled.shape[1]
    piece = pltpu.VMEM((half, rows // 4, feats // (2 * half)), BF16)
    return pl.pallas_call(
        far_kernel,
        in_specs=[smem()] + [vmem()] * 11,
        out_specs=[vmem()] * 4,
        out_shape=[pltpu.VMEM(pooled.shape, BF16)] * 2 + [piece, piece],
        scratch_shapes=[pltpu.VMEM((samp, rank), BF16)],
        compiler_params=params(8),
        cost_estimate=cost(5 << 28, 7 << 20),
        name="far_rows",
    )(core, *kept(prod), other, bias, *kept(*turned, pooled, cot, x1, a, u, v))


def near_kernel(*refs):
    turned, refs = refs[:2], refs[2:]
    grad, made_ref, crossed_ref, p0_ref, p1_a, p1_b, p3_a, p3_b, sem = refs
    copy = pltpu.make_async_copy(made_ref, crossed_ref, sem)
    copy.start()
    half, rows, emb = p1_a.shape
    for t in range(2 * half):
        side, at = divmod(t, half)
        part = grad[:, t * emb : (t + 1) * emb]
        first = row_grads(turned[side], at, 0, 2 * rows, part)
        p0_ref[t] = first[:rows]
        (p1_a, p1_b)[side][at] = first[rows:].astype(BF16)
        (p3_a, p3_b)[side][at] = row_grads(turned[side], at, 3 * rows, rows, part).astype(BF16)
    copy.wait()


def near_rows(turned, grad, crossed):
    half, rows, samp = turned[0].shape
    block = (half, rows // 4, grad.shape[1] // (2 * half))
    return pl.pallas_call(
        near_kernel,
        in_specs=[vmem()] * 4,
        out_specs=[anyspace()] + [vmem()] * 5,
        out_shape=[pltpu.HBM(crossed.shape, BF16), pltpu.VMEM((2 * half,) + block[1:], F32)]
        + [pltpu.VMEM(block, BF16)] * 4,
        scratch_shapes=[pltpu.SemaphoreType.DMA],
        compiler_params=params(8),
        cost_estimate=cost(3 << 28, 7 << 20),
        name="near_rows",
    )(*kept(*turned, grad, crossed))


def finish_kernel(p0, near_a, far_a, near_b, far_b, out_ref, held, sems):
    half = near_a.shape[0]
    copies = []
    for side, (near, far) in enumerate(((near_a, far_a), (near_b, far_b))):
        at = pl.ds(side * half, half)
        held[at] = p0[at] + (near[...].astype(F32) + far[...].astype(F32))
        copies += [pltpu.make_async_copy(held.at[at], out_ref.at[at], sems.at[side])]
        copies[-1].start()
    for copy in copies:
        copy.wait()


def finish(p0, *others):
    return pl.pallas_call(
        finish_kernel,
        in_specs=[vmem()] * 5,
        out_specs=anyspace(),
        out_shape=pltpu.HBM(p0.shape, F32),
        scratch_shapes=[pltpu.VMEM(p0.shape, F32), pltpu.SemaphoreType.DMA((2,))],
        compiler_params=params(4),
        cost_estimate=cost(1 << 20, 1 << 20),
        name="finish",
    )(*kept(p0), *others)


def right(arr):
    return lax.ppermute(arr, "row", [(i, (i + 1) & 3) for i in range(4)])


def left(arr):
    return lax.ppermute(arr, "row", [(i, (i + 3) & 3) for i in range(4)])


def add(a, b):
    return a.astype(F32) + b.astype(F32)


def scalar(axis):
    return lax.axis_index(axis).astype(jnp.int32).reshape(1)


def local(emb_rows, entry_ids, entry_sample, cross_v, cross_u, cross_bias, cotangent):
    samp = cotangent.shape[0]
    rows = emb_rows.shape[1] * lax.axis_size("row")
    mine, core = scalar("row"), scalar("c")
    own_a, own_b = cast_halves(emb_rows)
    left_a, right_b = right(own_a), left(own_b)
    left_b, right_a = right(own_b), left(own_a)
    counts_a, edges = make_counts(mine, entry_ids, entry_sample, samp, rows)
    left_a, right_b, edges = lax.optimization_barrier((left_a, right_b, edges))
    far_a, far_b = right(left_a), left(right_b)
    loads = (cotangent, cross_v, cross_u)
    counts_b, cot, v, u = make_counts(mine, entry_ids, entry_sample, samp, rows, edges, loads)
    embs = (own_a, own_b, right_a, right_b, far_a, far_b, left_a, left_b)
    pooled, wide, send = first_sums(core, (counts_a, counts_b), embs, cot, v, u)
    prod, other, turned_a = sum_all(core, send, pooled, wide, v, u, 0, counts_a)
    x1, a, wide, send = middle(core, prod, other, cross_bias, pooled, cot, u, v)
    prod, other, turned_b = sum_all(core, send, x1, wide, v, u, 1, counts_b)
    turned = (turned_a, turned_b)
    crossed, grad, p2a, p2b = far_rows(core, prod, other, cross_bias, turned, pooled, cot, x1, a, u, v)
    from_left, from_right = right(p2a), left(p2b)
    crossed, p0, p1a, p1b, p3a, p3b = near_rows(turned, grad, crossed)
    sum_b, sum_a = right(p1b), left(p3a)
    far_a = right(add(p1a, from_left).astype(BF16))
    far_b = left(add(p3b, from_right).astype(BF16))
    return crossed, finish(p0, sum_a, far_a, sum_b, far_b)


def solution(mesh):
    fine = jax.sharding.Mesh(mesh.devices.reshape(4, 4, 2, 2, 4), ("x", "zh", "zl", "c", "row"))
    table = ("x", "zh", "zl", "c")
    placed = (
        P(table, "row", None),
        P(table, None),
        P(table, None),
        P(None, table, None),
        P(None, None, table),
        P(None, table),
        P("row", table),
    )
    return jax.shard_map(
        local,
        mesh=fine,
        in_specs=placed,
        out_specs=(P("row", table), P(table, "row", None)),
        check_vma=False,
    )
```

```python
import functools

import jax
import jax.numpy as jnp
from jax import lax
from jax.experimental import pallas as pl
from jax.experimental.pallas import tpu as pltpu
from jax.sharding import PartitionSpec as P

F32 = jnp.float32
BF16 = jnp.bfloat16
EB = 512
EARLY = 2
NT = (((1,), (1,)), ((), ()))
TN = (((0,), (0,)), ((), ()))


def vmem():
    return pl.BlockSpec(memory_space=pltpu.VMEM)


def smem():
    return pl.BlockSpec(memory_space=pltpu.SMEM)


def params(mib):
    return pltpu.CompilerParams(vmem_limit_bytes=mib * 2**20)


def cost(flops, moved):
    return pl.CostEstimate(flops=flops, bytes_accessed=moved, transcendentals=0)


def pinned(arr):
    return pltpu.with_memory_space_constraint(arr, pltpu.HBM)


def kept(*arrs):
    return [pltpu.with_memory_space_constraint(arr, pltpu.VMEM) for arr in arrs]


def hbm():
    return pl.BlockSpec(memory_space=pltpu.HBM)


def cast_kernel(in_ref, a_ref, b_ref, held, sems):
    half = a_ref.shape[0]
    outs = (a_ref, b_ref)
    copies = fetch(sems, [(in_ref.at[pl.ds(i * half, half)], held.at[i]) for i in range(2)])
    for i in range(2):
        copies[i].wait()
        outs[i][...] = held[i].astype(BF16)


def cast_halves(emb_rows):
    tabs, rows, emb = emb_rows.shape
    half = (tabs // 2, rows, emb)
    return pl.pallas_call(
        cast_kernel,
        in_specs=[hbm()],
        out_specs=[vmem()] * 2,
        out_shape=[pltpu.VMEM(half, BF16)] * 2,
        scratch_shapes=[pltpu.VMEM((2,) + half, F32), pltpu.SemaphoreType.DMA((2,))],
        compiler_params=params(4),
        cost_estimate=cost(1 << 18, 3 << 19),
        name="cast",
    )(pinned(emb_rows))


def counts_kernel(mine_ref, ids_ref, own_ref, *refs, first_table):
    refs, (acc_ref, ids, own, sems) = refs[:-4], refs[-4:]
    if first_table:
        edges_ref, *loads = refs[: len(refs) // 2]
        out_ref, *loaded = refs[len(refs) // 2 :]
    else:
        out_ref, edges_ref = refs
        loads = loaded = ()
    copies = fetch(sems, [(own_ref, own), (ids_ref, ids), *zip(loads, loaded)])
    _, rows, samp = acc_ref.shape
    tabs, entries = own.shape
    mine = mine_ref[0]
    low = mine * samp
    turn = mine * (rows // 4)
    copies[0].wait()
    if not first_table:
        owners = own[...]
        first = jnp.sum((owners < low).astype(jnp.int32), axis=1, keepdims=True)
        last = jnp.sum((owners < low + samp).astype(jnp.int32), axis=1, keepdims=True)
        for i in range(tabs):
            edges_ref[i] = first[i, 0]
            edges_ref[tabs + i] = last[i, 0]
    copies[1].wait()
    grid = lax.broadcasted_iota(jnp.int32, (samp, EB), 0).astype(F32).astype(BF16)
    one, zero = jnp.ones((), BF16), jnp.zeros((), BF16)

    @pl.loop(0, out_ref.shape[0] // 2)
    def _(pair):
        tables = [first_table + 2 * pair + j for j in range(2)]
        starts = [edges_ref[t] // 128 for t in tables]
        spans = [edges_ref[tabs + t] - start * 128 for t, start in zip(tables, starts)]
        steps = (jnp.maximum(*spans) + EB - 1) // EB
        starts = [jnp.minimum(start, (entries - steps * EB) // 128) * 128 for start in starts]
        acc_ref[...] = jnp.zeros_like(acc_ref)

        def body(block, carry):
            for j, t in enumerate(tables):
                at = pl.ds(pl.multiple_of(starts[j] + block * EB, 128), EB)
                who = own[pl.ds(t, 1), at] - low
                row = (ids[pl.ds(t, 1), at] - turn) & (rows - 1)
                hot = [
                    jnp.where(grid == values.astype(F32).astype(BF16), one, zero) for values in (who, row, row - samp)
                ]
                acc_ref[j] += lax.dot_general(
                    jnp.concatenate(hot[1:], axis=0), hot[0], NT, preferred_element_type=F32
                )
            return carry

        lax.fori_loop(0, steps, body, 0)
        for j in range(2):
            out_ref[2 * pair + j] = acc_ref[j].astype(BF16).T

    for copy in copies[2:]:
        copy.wait()


def make_counts(mine, ids, owners, samp, rows, edges=None, loads=()):
    tabs, entries = ids.shape
    assert rows == 2 * samp and samp <= 256
    count = EARLY if edges is None else tabs - EARLY
    out_shape = [pltpu.VMEM((count, samp, rows), BF16)]
    args = (mine, pinned(ids), pinned(owners))
    in_specs, out_specs = [smem(), hbm(), hbm()], [vmem()]
    if edges is None:
        out_specs.append(smem())
        out_shape.append(jax.ShapeDtypeStruct((2 * tabs,), jnp.int32))
    else:
        args += (edges, *map(pinned, loads))
        in_specs += [smem()] + [hbm()] * len(loads)
        out_specs += [vmem()] * len(loads)
        out_shape += [pltpu.VMEM(arr.shape, arr.dtype) for arr in loads]
    return pl.pallas_call(
        functools.partial(counts_kernel, first_table=0 if edges is None else EARLY),
        in_specs=in_specs,
        out_specs=out_specs,
        out_shape=out_shape,
        scratch_shapes=[
            pltpu.VMEM((2, rows, samp), F32),
            pltpu.VMEM((tabs, entries), jnp.int32),
            pltpu.VMEM((tabs, entries), jnp.int32),
            pltpu.SemaphoreType.DMA((2 + len(loads),)),
        ],
        compiler_params=params(6),
        cost_estimate=cost(count * samp * rows * 3072, 3 << 20),
        name="counts",
    )(*args)


def turned_kernel(in_ref, out_ref):
    for i in range(out_ref.shape[0]):
        out_ref[i] = in_ref[i].T


def turned_counts(counts):
    count, samp, rows = counts.shape
    return pl.pallas_call(
        turned_kernel,
        in_specs=[vmem()],
        out_specs=vmem(),
        out_shape=pltpu.VMEM((count, rows, samp), BF16),
        compiler_params=params(8),
        cost_estimate=cost(1 << 29, 2 << 20),
        name="turned",
    )(*kept(counts))


def of_table(pair, t):
    return pair[0][t] if t < EARLY else pair[1][t - EARLY]


WIDE = 512


def fetch(sems, pairs):
    copies = [pltpu.make_async_copy(src, dst, sems.at[i]) for i, (src, dst) in enumerate(pairs)]
    for copy in copies:
        copy.start()
    return copies


def sum_z(x, v_ref, layer):
    return jnp.dot(x[...], v_ref[layer], preferred_element_type=F32)


def sum_g(wide, u_ref, layer):
    return lax.dot_general(wide[...], u_ref[layer], NT, preferred_element_type=F32)


def one_sum(even, x, wide, v_ref, u_ref, layer, out_ref):
    @pl.when(even)
    def _():
        out_ref[...] = sum_z(x, v_ref, layer).astype(out_ref.dtype)

    @pl.when(jnp.logical_not(even))
    def _():
        out_ref[...] = sum_g(wide, u_ref, 1 - layer).astype(out_ref.dtype)


def keep_kernel(core_ref, x, wide, v_ref, u_ref, out_ref, *, layer):
    one_sum(core_ref[0] == 0, x, wide, v_ref, u_ref, layer, out_ref)


def keep_sum(core, x, wide, v, u, layer):
    return pl.pallas_call(
        functools.partial(keep_kernel, layer=layer),
        in_specs=[smem()] + [vmem()] * 4,
        out_specs=vmem(),
        out_shape=pltpu.VMEM((x.shape[0], v.shape[-1]), F32),
        compiler_params=params(8),
        cost_estimate=cost(1 << 29, 4 << 20),
        name="keep_sum",
    )(core, *kept(x, wide, v, u))


def anyspace():
    return pl.BlockSpec(memory_space=pl.ANY)


def first_kernel(core_ref, counts_a, counts_b, *refs):
    embs, (cot, v_ref, u_ref, pooled_ref, wide_ref, send_ref) = refs[:8], refs[8:]
    half, _, emb = embs[0].shape
    for t in range(2 * half):
        side, i = divmod(t, half)
        rows = jnp.concatenate([embs[2 * k + side][i] for k in range(4)], axis=0)
        pooled = jnp.dot(of_table((counts_a, counts_b), t), rows, preferred_element_type=F32).astype(BF16)
        at = slice(t * emb, (t + 1) * emb)
        pooled_ref[:, at] = pooled
        wide_ref[:, at] = (cot[:, at].astype(F32) * pooled.astype(F32)).astype(BF16)
    one_sum(core_ref[0] != 0, pooled_ref, wide_ref, v_ref, u_ref, 0, send_ref)


def first_sums(core, counts, embs, cot, v, u):
    _, samp, rows = counts[0].shape
    half, _, emb = embs[0].shape
    rank = v.shape[-1]
    return pl.pallas_call(
        first_kernel,
        in_specs=[smem()] + [vmem()] * 13,
        out_specs=[vmem()] * 3,
        out_shape=[
            pltpu.VMEM((samp, 2 * half * emb), BF16),
            pltpu.VMEM((samp, 2 * half * emb), BF16),
            pltpu.VMEM((samp, rank), BF16),
        ],
        compiler_params=params(8),
        cost_estimate=cost(3 << 29, 10 << 20),
        name="first_sums",
    )(core, *kept(*counts), *embs, *kept(cot, v, u))


def swap(arr, axis):
    return lax.ppermute(arr, axis, [(0, 1), (1, 0)])


def small(kernel, out_shape, name, *args):
    return pl.pallas_call(
        kernel,
        in_specs=[vmem()] * len(args),
        out_specs=jax.tree.map(lambda _: vmem(), out_shape),
        out_shape=out_shape,
        compiler_params=params(8),
        cost_estimate=cost(1 << 20, 1 << 20),
        name=name,
    )(*args)


CHUNKS = 8
CHUNK = (32, 512)


def chunk_at(i):
    return slice(CHUNK[0] * i, CHUNK[0] * (i + 1)), slice(None)


def cut_kernel(keep_ref, got_ref, out_ref):
    for i in range(CHUNKS):
        at = chunk_at(i)
        out_ref[i] = (keep_ref[at] + got_ref[at].astype(F32)).astype(BF16)


def total_kernel(*refs):
    *ins, out_ref = refs
    total = sum(ref[i].astype(F32) for ref in ins for i in range(ref.shape[0])).astype(BF16)
    for i in range(out_ref.shape[0]):
        out_ref[i] = total


def total(copies, *arrays):
    return small(total_kernel, pltpu.VMEM((copies,) + CHUNK, BF16), "total", *arrays)


def swap_all(arr):
    return lax.all_to_all(arr, ("x", "zl"), 0, 0, tiled=True)


def turn(arr, k):
    return lax.ppermute(arr, "zh", [(i, (i + k) & 3) for i in range(4)])


def layout(chunks_ref, sum_ref):
    for i in range(CHUNKS):
        sum_ref[chunk_at(i)] = chunks_ref[i]


def z_u(total, u_ref, layer, at):
    return jnp.dot(total, u_ref[layer, :, at], preferred_element_type=F32)


def g_v(total, v_ref, layer, at):
    return lax.dot_general(total, v_ref[layer, at, :], NT, preferred_element_type=F32)


def steps_of(feats):
    return [slice(f, f + WIDE) for f in range(0, feats, WIDE)]


def product_kernel(core_ref, mine_ref, v_ref, u_ref, out_ref, sum_ref, *, layer):
    layout(mine_ref, sum_ref)

    @pl.when(core_ref[0] == 0)
    def _():
        for at in steps_of(out_ref.shape[1]):
            out_ref[:, at] = z_u(sum_ref[...], u_ref, layer, at)

    @pl.when(core_ref[0] != 0)
    def _():
        for at in steps_of(out_ref.shape[1]):
            out_ref[:, at] = g_v(sum_ref[...], v_ref, 1 - layer, at)


def product(core, mine, v, u, layer):
    samp, rank = CHUNKS * CHUNK[0], CHUNK[1]
    return pl.pallas_call(
        functools.partial(product_kernel, layer=layer),
        in_specs=[smem()] + [vmem()] * 3,
        out_specs=vmem(),
        out_shape=pltpu.VMEM((samp, u.shape[-1]), F32),
        scratch_shapes=[pltpu.VMEM((samp, rank), BF16)],
        compiler_params=params(8),
        cost_estimate=cost(1 << 29, 4 << 20),
        name="product",
    )(core, mine, *kept(v, u))


def by_core(core_ref, body, prod, sum_ref, v_ref, u_ref, layer):
    @pl.when(core_ref[0] == 0)
    def _():
        body(lambda at: prod[:, at], lambda at: g_v(sum_ref[...], v_ref, 1 - layer, at))

    @pl.when(core_ref[0] != 0)
    def _():
        body(lambda at: z_u(sum_ref[...], u_ref, layer, at), lambda at: prod[:, at])


def sum_all(core, send, x, wide, v, u, layer, counts):
    send, x = lax.optimization_barrier((send, x))
    got, keep = lax.optimization_barrier((swap(send, "c"), keep_sum(core, x, wide, v, u, layer)))
    shape = pltpu.VMEM((CHUNKS,) + CHUNK, BF16)
    parts = swap_all(small(cut_kernel, shape, "cut", keep, got))
    own, counts = lax.optimization_barrier((total(1, parts), counts))
    near = (turn(own, 1), turn(own, 3), turn(own, 2), turned_counts(counts))
    *near, turned = lax.optimization_barrier(near)
    mine = swap_all(total(CHUNKS, own, *near))
    prod, other = lax.optimization_barrier((product(core, mine, v, u, layer), swap(mine, "c")))
    return prod, other, turned


def middle_kernel(core_ref, prod, other_ref, b_ref, pooled, cot, u_ref, v_ref, x1_ref, a_ref, wide_ref, send_ref, sum_ref):
    layout(other_ref, sum_ref)

    def body(h, g):
        for at in steps_of(pooled.shape[1]):
            base = pooled[:, at].astype(F32)
            h0 = h(at) + b_ref[0:1, at]
            x1_ref[:, at] = (base * h0 + base).astype(BF16)
            g1 = cot[:, at].astype(F32) + g(at)
            a_ref[:, at] = (g1 * h0 + g1).astype(BF16)
            wide_ref[:, at] = (g1 * base).astype(BF16)

    by_core(core_ref, body, prod, sum_ref, v_ref, u_ref, 0)
    one_sum(core_ref[0] != 0, x1_ref, wide_ref, v_ref, u_ref, 1, send_ref)


def middle(core, prod, other, bias, pooled, cot, u, v):
    samp, feats = pooled.shape
    rank = v.shape[-1]
    feat = pltpu.VMEM((samp, feats), BF16)
    return pl.pallas_call(
        middle_kernel,
        in_specs=[smem()] + [vmem()] * 7,
        out_specs=[vmem()] * 4,
        out_shape=[feat, feat, feat, pltpu.VMEM((samp, rank), BF16)],
        scratch_shapes=[pltpu.VMEM((samp, rank), BF16)],
        compiler_params=params(10),
        cost_estimate=cost(1 << 31, 8 << 20),
        name="middle",
    )(core, *kept(prod), other, bias, *kept(pooled, cot, u, v))


def row_grads(turned, table, first, count, grad):
    return jnp.dot(of_table(turned, table)[first : first + count, :], grad, preferred_element_type=F32)


def far_kernel(core_ref, prod, other_ref, b_ref, turned_a, turned_b, pooled, cot, x1, a, u_ref, v_ref, *refs):
    crossed_ref, grad_ref, far_a, far_b, sum_ref = refs
    half, rows, emb = far_a.shape
    layout(other_ref, sum_ref)

    def body(h, g):
        for at in steps_of(pooled.shape[1]):
            h1 = h(at) + b_ref[1:2, at]
            crossed_ref[:, at] = (pooled[:, at].astype(F32) * h1 + x1[:, at].astype(F32)).astype(BF16)
            grad_ref[:, at] = (cot[:, at].astype(F32) * h1 + a[:, at].astype(F32) + g(at)).astype(BF16)

    by_core(core_ref, body, prod, sum_ref, v_ref, u_ref, 1)
    for t in range(2 * half):
        side, i = divmod(t, half)
        part = row_grads((turned_a, turned_b), t, 2 * rows, rows, grad_ref[:, t * emb : (t + 1) * emb])
        (far_a, far_b)[side][i] = part.astype(BF16)


def far_rows(core, prod, other, bias, turned, pooled, cot, x1, a, u, v):
    _, rows, samp = turned[0].shape
    half = (turned[0].shape[0] + turned[1].shape[0]) // 2
    rank = v.shape[-1]
    feats = pooled.shape[1]
    piece = pltpu.VMEM((half, rows // 4, feats // (2 * half)), BF16)
    return pl.pallas_call(
        far_kernel,
        in_specs=[smem()] + [vmem()] * 11,
        out_specs=[vmem()] * 4,
        out_shape=[pltpu.VMEM(pooled.shape, BF16)] * 2 + [piece, piece],
        scratch_shapes=[pltpu.VMEM((samp, rank), BF16)],
        compiler_params=params(8),
        cost_estimate=cost(5 << 28, 7 << 20),
        name="far_rows",
    )(core, *kept(prod), other, bias, *kept(*turned, pooled, cot, x1, a, u, v))


def near_kernel(*refs):
    turned, refs = refs[:2], refs[2:]
    grad, made_ref, crossed_ref, p0_ref, p1_a, p1_b, p3_a, p3_b, sem = refs
    copy = pltpu.make_async_copy(made_ref, crossed_ref, sem)
    copy.start()
    half, rows, emb = p1_a.shape
    for t in range(2 * half):
        side, at = divmod(t, half)
        part = grad[:, t * emb : (t + 1) * emb]
        first = row_grads(turned, t, 0, 2 * rows, part)
        p0_ref[t] = first[:rows]
        (p1_a, p1_b)[side][at] = first[rows:].astype(BF16)
        (p3_a, p3_b)[side][at] = row_grads(turned, t, 3 * rows, rows, part).astype(BF16)
    copy.wait()


def near_rows(turned, grad, crossed):
    _, rows, samp = turned[0].shape
    half = (turned[0].shape[0] + turned[1].shape[0]) // 2
    block = (half, rows // 4, grad.shape[1] // (2 * half))
    return pl.pallas_call(
        near_kernel,
        in_specs=[vmem()] * 4,
        out_specs=[anyspace()] + [vmem()] * 5,
        out_shape=[pltpu.HBM(crossed.shape, BF16), pltpu.VMEM((2 * half,) + block[1:], F32)]
        + [pltpu.VMEM(block, BF16)] * 4,
        scratch_shapes=[pltpu.SemaphoreType.DMA],
        compiler_params=params(8),
        cost_estimate=cost(3 << 28, 7 << 20),
        name="near_rows",
    )(*kept(*turned, grad, crossed))


def finish_kernel(p0, near_a, far_a, near_b, far_b, out_ref, held, sems):
    half = near_a.shape[0]
    copies = []
    for side, (near, far) in enumerate(((near_a, far_a), (near_b, far_b))):
        at = pl.ds(side * half, half)
        held[at] = p0[at] + (near[...].astype(F32) + far[...].astype(F32))
        copies += [pltpu.make_async_copy(held.at[at], out_ref.at[at], sems.at[side])]
        copies[-1].start()
    for copy in copies:
        copy.wait()


def finish(p0, *others):
    return pl.pallas_call(
        finish_kernel,
        in_specs=[vmem()] * 5,
        out_specs=anyspace(),
        out_shape=pltpu.HBM(p0.shape, F32),
        scratch_shapes=[pltpu.VMEM(p0.shape, F32), pltpu.SemaphoreType.DMA((2,))],
        compiler_params=params(4),
        cost_estimate=cost(1 << 20, 1 << 20),
        name="finish",
    )(*kept(p0), *others)


def right(arr):
    return lax.ppermute(arr, "row", [(i, (i + 1) & 3) for i in range(4)])


def left(arr):
    return lax.ppermute(arr, "row", [(i, (i + 3) & 3) for i in range(4)])


def add(a, b):
    return a.astype(F32) + b.astype(F32)


def scalar(axis):
    return lax.axis_index(axis).astype(jnp.int32).reshape(1)


def local(emb_rows, entry_ids, entry_sample, cross_v, cross_u, cross_bias, cotangent):
    samp = cotangent.shape[0]
    rows = emb_rows.shape[1] * lax.axis_size("row")
    mine, core = scalar("row"), scalar("c")
    own_a, own_b = cast_halves(emb_rows)
    left_a, right_b = right(own_a), left(own_b)
    left_b, right_a = right(own_b), left(own_a)
    counts_a, edges = make_counts(mine, entry_ids, entry_sample, samp, rows)
    left_a, right_b, edges = lax.optimization_barrier((left_a, right_b, edges))
    far_a, far_b = right(left_a), left(right_b)
    loads = (cotangent, cross_v, cross_u)
    counts_b, cot, v, u = make_counts(mine, entry_ids, entry_sample, samp, rows, edges, loads)
    embs = (own_a, own_b, right_a, right_b, far_a, far_b, left_a, left_b)
    pooled, wide, send = first_sums(core, (counts_a, counts_b), embs, cot, v, u)
    prod, other, turned_a = sum_all(core, send, pooled, wide, v, u, 0, counts_a)
    x1, a, wide, send = middle(core, prod, other, cross_bias, pooled, cot, u, v)
    prod, other, turned_b = sum_all(core, send, x1, wide, v, u, 1, counts_b)
    turned = (turned_a, turned_b)
    crossed, grad, p2a, p2b = far_rows(core, prod, other, cross_bias, turned, pooled, cot, x1, a, u, v)
    from_left, from_right = right(p2a), left(p2b)
    crossed, p0, p1a, p1b, p3a, p3b = near_rows(turned, grad, crossed)
    sum_b, sum_a = right(p1b), left(p3a)
    far_a = right(add(p1a, from_left).astype(BF16))
    far_b = left(add(p3b, from_right).astype(BF16))
    return crossed, finish(p0, sum_a, far_a, sum_b, far_b)


def solution(mesh):
    fine = jax.sharding.Mesh(mesh.devices.reshape(4, 4, 2, 2, 4), ("x", "zh", "zl", "c", "row"))
    table = ("x", "zh", "zl", "c")
    placed = (
        P(table, "row", None),
        P(table, None),
        P(table, None),
        P(None, table, None),
        P(None, None, table),
        P(None, table),
        P("row", table),
    )
    return jax.shard_map(
        local,
        mesh=fine,
        in_specs=placed,
        out_specs=(P("row", table), P(table, "row", None)),
        check_vma=False,
    )
```

```python
import functools

import jax
import jax.numpy as jnp
from jax import lax
from jax.experimental import pallas as pl
from jax.experimental.pallas import tpu as pltpu
from jax.sharding import PartitionSpec as P

F32 = jnp.float32
BF16 = jnp.bfloat16
EB = 512
NT = (((1,), (1,)), ((), ()))
TN = (((0,), (0,)), ((), ()))


def vmem():
    return pl.BlockSpec(memory_space=pltpu.VMEM)


def smem():
    return pl.BlockSpec(memory_space=pltpu.SMEM)


def params(mib):
    return pltpu.CompilerParams(vmem_limit_bytes=mib * 2**20)


def cost(flops, moved):
    return pl.CostEstimate(flops=flops, bytes_accessed=moved, transcendentals=0)


def pinned(arr):
    return pltpu.with_memory_space_constraint(arr, pltpu.HBM)


def kept(*arrs):
    return [pltpu.with_memory_space_constraint(arr, pltpu.VMEM) for arr in arrs]


def hbm():
    return pl.BlockSpec(memory_space=pltpu.HBM)


def cast_kernel(in_ref, a_ref, b_ref, held, sems):
    half = a_ref.shape[0]
    outs = (a_ref, b_ref)
    copies = fetch(sems, [(in_ref.at[pl.ds(i * half, half)], held.at[i]) for i in range(2)])
    for i in range(2):
        copies[i].wait()
        outs[i][...] = held[i].astype(BF16)


def cast_halves(emb_rows):
    tabs, rows, emb = emb_rows.shape
    half = (tabs // 2, rows, emb)
    return pl.pallas_call(
        cast_kernel,
        in_specs=[hbm()],
        out_specs=[vmem()] * 2,
        out_shape=[pltpu.VMEM(half, BF16)] * 2,
        scratch_shapes=[pltpu.VMEM((2,) + half, F32), pltpu.SemaphoreType.DMA((2,))],
        compiler_params=params(4),
        cost_estimate=cost(1 << 18, 3 << 19),
        name="cast",
    )(pinned(emb_rows))


def counts_kernel(mine_ref, ids_ref, own_ref, *refs, first_table):
    refs, (acc_ref, ids, own, sems) = refs[:-4], refs[-4:]
    if first_table:
        edges_ref, *loads = refs[: len(refs) // 2]
        out_ref, *loaded = refs[len(refs) // 2 :]
    else:
        out_ref, edges_ref = refs
        loads = loaded = ()
    copies = fetch(sems, [(own_ref, own), (ids_ref, ids), *zip(loads, loaded)])
    _, rows, samp = acc_ref.shape
    tabs, entries = own.shape
    mine = mine_ref[0]
    low = mine * samp
    turn = mine * (rows // 4)
    copies[0].wait()
    if not first_table:
        owners = own[...]
        first = jnp.sum((owners < low).astype(jnp.int32), axis=1, keepdims=True)
        last = jnp.sum((owners < low + samp).astype(jnp.int32), axis=1, keepdims=True)
        for i in range(tabs):
            edges_ref[i] = first[i, 0]
            edges_ref[tabs + i] = last[i, 0]
    copies[1].wait()
    grid = lax.broadcasted_iota(jnp.int32, (samp, EB), 0).astype(F32).astype(BF16)
    one, zero = jnp.ones((), BF16), jnp.zeros((), BF16)

    @pl.loop(0, out_ref.shape[0] // 2)
    def _(pair):
        tables = [first_table + 2 * pair + j for j in range(2)]
        starts = [edges_ref[t] // 128 for t in tables]
        spans = [edges_ref[tabs + t] - start * 128 for t, start in zip(tables, starts)]
        steps = (jnp.maximum(*spans) + EB - 1) // EB
        starts = [jnp.minimum(start, (entries - steps * EB) // 128) * 128 for start in starts]
        acc_ref[...] = jnp.zeros_like(acc_ref)

        def body(block, carry):
            for j, t in enumerate(tables):
                at = pl.ds(pl.multiple_of(starts[j] + block * EB, 128), EB)
                who = own[pl.ds(t, 1), at] - low
                row = (ids[pl.ds(t, 1), at] - turn) & (rows - 1)
                hot = [
                    jnp.where(grid == values.astype(F32).astype(BF16), one, zero) for values in (who, row, row - samp)
                ]
                acc_ref[j] += lax.dot_general(
                    jnp.concatenate(hot[1:], axis=0), hot[0], NT, preferred_element_type=F32
                )
            return carry

        lax.fori_loop(0, steps, body, 0)
        for j in range(2):
            out_ref[2 * pair + j] = acc_ref[j].astype(BF16).T

    for copy in copies[2:]:
        copy.wait()


def make_counts(mine, ids, owners, samp, rows, edges=None, loads=()):
    tabs, entries = ids.shape
    assert rows == 2 * samp and samp <= 256
    half = tabs // 2
    out_shape = [pltpu.VMEM((half, samp, rows), BF16)]
    args = (mine, pinned(ids), pinned(owners))
    in_specs, out_specs = [smem(), hbm(), hbm()], [vmem()]
    if edges is None:
        out_specs.append(smem())
        out_shape.append(jax.ShapeDtypeStruct((2 * tabs,), jnp.int32))
    else:
        args += (edges, *map(pinned, loads))
        in_specs += [smem()] + [hbm()] * len(loads)
        out_specs += [vmem()] * len(loads)
        out_shape += [pltpu.VMEM(arr.shape, arr.dtype) for arr in loads]
    return pl.pallas_call(
        functools.partial(counts_kernel, first_table=0 if edges is None else half),
        in_specs=in_specs,
        out_specs=out_specs,
        out_shape=out_shape,
        scratch_shapes=[
            pltpu.VMEM((2, rows, samp), F32),
            pltpu.VMEM((tabs, entries), jnp.int32),
            pltpu.VMEM((tabs, entries), jnp.int32),
            pltpu.SemaphoreType.DMA((2 + len(loads),)),
        ],
        compiler_params=params(6),
        cost_estimate=cost(half * samp * rows * 3072, 3 << 20),
        name="counts",
    )(*args)


def turned_kernel(in_ref, out_ref):
    for i in range(out_ref.shape[0]):
        out_ref[i] = in_ref[i].T


def turned_counts(counts):
    half, samp, rows = counts.shape
    return pl.pallas_call(
        turned_kernel,
        in_specs=[vmem()],
        out_specs=vmem(),
        out_shape=pltpu.VMEM((half, rows, samp), BF16),
        compiler_params=params(8),
        cost_estimate=cost(1 << 29, 2 << 20),
        name="turned",
    )(*kept(counts))


WIDE = 512


def fetch(sems, pairs):
    copies = [pltpu.make_async_copy(src, dst, sems.at[i]) for i, (src, dst) in enumerate(pairs)]
    for copy in copies:
        copy.start()
    return copies


def sum_z(x, v_ref, layer):
    return jnp.dot(x[...], v_ref[layer], preferred_element_type=F32)


def sum_g(wide, u_ref, layer):
    return lax.dot_general(wide[...], u_ref[layer], NT, preferred_element_type=F32)


def one_sum(even, x, wide, v_ref, u_ref, layer, out_ref):
    @pl.when(even)
    def _():
        out_ref[...] = sum_z(x, v_ref, layer).astype(out_ref.dtype)

    @pl.when(jnp.logical_not(even))
    def _():
        out_ref[...] = sum_g(wide, u_ref, 1 - layer).astype(out_ref.dtype)


def keep_kernel(core_ref, x, wide, v_ref, u_ref, out_ref, *, layer):
    one_sum(core_ref[0] == 0, x, wide, v_ref, u_ref, layer, out_ref)


def keep_sum(core, x, wide, v, u, layer):
    return pl.pallas_call(
        functools.partial(keep_kernel, layer=layer),
        in_specs=[smem()] + [vmem()] * 4,
        out_specs=vmem(),
        out_shape=pltpu.VMEM((x.shape[0], v.shape[-1]), F32),
        compiler_params=params(8),
        cost_estimate=cost(1 << 29, 4 << 20),
        name="keep_sum",
    )(core, *kept(x, wide, v, u))


def anyspace():
    return pl.BlockSpec(memory_space=pl.ANY)


def first_kernel(core_ref, counts_a, counts_b, *refs):
    embs, (cot, v_ref, u_ref, pooled_ref, wide_ref, send_ref) = refs[:8], refs[8:]
    half, _, emb = embs[0].shape
    for t in range(2 * half):
        side, i = divmod(t, half)
        rows = jnp.concatenate([embs[2 * k + side][i] for k in range(4)], axis=0)
        pooled = jnp.dot((counts_a, counts_b)[side][i], rows, preferred_element_type=F32).astype(BF16)
        at = slice(t * emb, (t + 1) * emb)
        pooled_ref[:, at] = pooled
        wide_ref[:, at] = (cot[:, at].astype(F32) * pooled.astype(F32)).astype(BF16)
    one_sum(core_ref[0] != 0, pooled_ref, wide_ref, v_ref, u_ref, 0, send_ref)


def first_sums(core, counts, embs, cot, v, u):
    half, samp, rows = counts[0].shape
    emb = embs[0].shape[-1]
    rank = v.shape[-1]
    return pl.pallas_call(
        first_kernel,
        in_specs=[smem()] + [vmem()] * 13,
        out_specs=[vmem()] * 3,
        out_shape=[
            pltpu.VMEM((samp, 2 * half * emb), BF16),
            pltpu.VMEM((samp, 2 * half * emb), BF16),
            pltpu.VMEM((samp, rank), BF16),
        ],
        compiler_params=params(8),
        cost_estimate=cost(3 << 29, 10 << 20),
        name="first_sums",
    )(core, *kept(*counts), *embs, *kept(cot, v, u))


def swap(arr, axis):
    return lax.ppermute(arr, axis, [(0, 1), (1, 0)])


def small(kernel, out_shape, name, *args):
    return pl.pallas_call(
        kernel,
        in_specs=[vmem()] * len(args),
        out_specs=jax.tree.map(lambda _: vmem(), out_shape),
        out_shape=out_shape,
        compiler_params=params(8),
        cost_estimate=cost(1 << 20, 1 << 20),
        name=name,
    )(*args)


CHUNKS = 8
CHUNK = (32, 512)


def chunk_at(i):
    return slice(CHUNK[0] * i, CHUNK[0] * (i + 1)), slice(None)


def cut_kernel(keep_ref, got_ref, out_ref):
    for i in range(CHUNKS):
        at = chunk_at(i)
        out_ref[i] = (keep_ref[at] + got_ref[at].astype(F32)).astype(BF16)


def total_kernel(*refs):
    *ins, out_ref = refs
    total = sum(ref[i].astype(F32) for ref in ins for i in range(ref.shape[0])).astype(BF16)
    for i in range(out_ref.shape[0]):
        out_ref[i] = total


def total(copies, *arrays):
    return small(total_kernel, pltpu.VMEM((copies,) + CHUNK, BF16), "total", *arrays)


def swap_all(arr):
    return lax.all_to_all(arr, ("x", "zl"), 0, 0, tiled=True)


def turn(arr, k):
    return lax.ppermute(arr, "zh", [(i, (i + k) & 3) for i in range(4)])


def layout(chunks_ref, sum_ref):
    for i in range(CHUNKS):
        sum_ref[chunk_at(i)] = chunks_ref[i]


def z_u(total, u_ref, layer, at):
    return jnp.dot(total, u_ref[layer, :, at], preferred_element_type=F32)


def g_v(total, v_ref, layer, at):
    return lax.dot_general(total, v_ref[layer, at, :], NT, preferred_element_type=F32)


def steps_of(feats):
    return [slice(f, f + WIDE) for f in range(0, feats, WIDE)]


def product_kernel(core_ref, mine_ref, v_ref, u_ref, out_ref, sum_ref, *, layer):
    layout(mine_ref, sum_ref)

    @pl.when(core_ref[0] == 0)
    def _():
        for at in steps_of(out_ref.shape[1]):
            out_ref[:, at] = z_u(sum_ref[...], u_ref, layer, at)

    @pl.when(core_ref[0] != 0)
    def _():
        for at in steps_of(out_ref.shape[1]):
            out_ref[:, at] = g_v(sum_ref[...], v_ref, 1 - layer, at)


def product(core, mine, v, u, layer):
    samp, rank = CHUNKS * CHUNK[0], CHUNK[1]
    return pl.pallas_call(
        functools.partial(product_kernel, layer=layer),
        in_specs=[smem()] + [vmem()] * 3,
        out_specs=vmem(),
        out_shape=pltpu.VMEM((samp, u.shape[-1]), F32),
        scratch_shapes=[pltpu.VMEM((samp, rank), BF16)],
        compiler_params=params(8),
        cost_estimate=cost(1 << 29, 4 << 20),
        name="product",
    )(core, mine, *kept(v, u))


def by_core(core_ref, body, prod, sum_ref, v_ref, u_ref, layer):
    @pl.when(core_ref[0] == 0)
    def _():
        body(lambda at: prod[:, at], lambda at: g_v(sum_ref[...], v_ref, 1 - layer, at))

    @pl.when(core_ref[0] != 0)
    def _():
        body(lambda at: z_u(sum_ref[...], u_ref, layer, at), lambda at: prod[:, at])


def sum_all(core, send, x, wide, v, u, layer, counts):
    send, x = lax.optimization_barrier((send, x))
    got, keep = lax.optimization_barrier((swap(send, "c"), keep_sum(core, x, wide, v, u, layer)))
    shape = pltpu.VMEM((CHUNKS,) + CHUNK, BF16)
    parts = swap_all(small(cut_kernel, shape, "cut", keep, got))
    own, counts = lax.optimization_barrier((total(1, parts), counts))
    near = (turn(own, 2), turn(own, 1), turn(own, 3), turned_counts(counts))
    *near, turned = lax.optimization_barrier(near)
    mine = swap_all(total(CHUNKS, own, *near))
    prod, other = lax.optimization_barrier((product(core, mine, v, u, layer), swap(mine, "c")))
    return prod, other, turned


def middle_kernel(core_ref, prod, other_ref, b_ref, pooled, cot, u_ref, v_ref, x1_ref, a_ref, wide_ref, send_ref, sum_ref):
    layout(other_ref, sum_ref)

    def body(h, g):
        for at in steps_of(pooled.shape[1]):
            base = pooled[:, at].astype(F32)
            h0 = h(at) + b_ref[0:1, at]
            x1_ref[:, at] = (base * h0 + base).astype(BF16)
            g1 = cot[:, at].astype(F32) + g(at)
            a_ref[:, at] = (g1 * h0 + g1).astype(BF16)
            wide_ref[:, at] = (g1 * base).astype(BF16)

    by_core(core_ref, body, prod, sum_ref, v_ref, u_ref, 0)
    one_sum(core_ref[0] != 0, x1_ref, wide_ref, v_ref, u_ref, 1, send_ref)


def middle(core, prod, other, bias, pooled, cot, u, v):
    samp, feats = pooled.shape
    rank = v.shape[-1]
    feat = pltpu.VMEM((samp, feats), BF16)
    return pl.pallas_call(
        middle_kernel,
        in_specs=[smem()] + [vmem()] * 7,
        out_specs=[vmem()] * 4,
        out_shape=[feat, feat, feat, pltpu.VMEM((samp, rank), BF16)],
        scratch_shapes=[pltpu.VMEM((samp, rank), BF16)],
        compiler_params=params(10),
        cost_estimate=cost(1 << 31, 8 << 20),
        name="middle",
    )(core, *kept(prod), other, bias, *kept(pooled, cot, u, v))


def row_grads(turned_ref, table, first, count, grad):
    return jnp.dot(turned_ref[table, first : first + count, :], grad, preferred_element_type=F32)


def far_kernel(core_ref, prod, other_ref, b_ref, turned_a, turned_b, pooled, cot, x1, a, u_ref, v_ref, *refs):
    crossed_ref, grad_ref, far_a, far_b, sum_ref = refs
    half, rows, emb = far_a.shape
    layout(other_ref, sum_ref)

    def body(h, g):
        for at in steps_of(pooled.shape[1]):
            h1 = h(at) + b_ref[1:2, at]
            crossed_ref[:, at] = (pooled[:, at].astype(F32) * h1 + x1[:, at].astype(F32)).astype(BF16)
            grad_ref[:, at] = (cot[:, at].astype(F32) * h1 + a[:, at].astype(F32) + g(at)).astype(BF16)

    by_core(core_ref, body, prod, sum_ref, v_ref, u_ref, 1)
    for t in range(2 * half):
        side, i = divmod(t, half)
        part = row_grads((turned_a, turned_b)[side], i, 2 * rows, rows, grad_ref[:, t * emb : (t + 1) * emb])
        (far_a, far_b)[side][i] = part.astype(BF16)


def far_rows(core, prod, other, bias, turned, pooled, cot, x1, a, u, v):
    half, rows, samp = turned[0].shape
    rank = v.shape[-1]
    feats = pooled.shape[1]
    piece = pltpu.VMEM((half, rows // 4, feats // (2 * half)), BF16)
    return pl.pallas_call(
        far_kernel,
        in_specs=[smem()] + [vmem()] * 11,
        out_specs=[vmem()] * 4,
        out_shape=[pltpu.VMEM(pooled.shape, BF16)] * 2 + [piece, piece],
        scratch_shapes=[pltpu.VMEM((samp, rank), BF16)],
        compiler_params=params(8),
        cost_estimate=cost(5 << 28, 7 << 20),
        name="far_rows",
    )(core, *kept(prod), other, bias, *kept(*turned, pooled, cot, x1, a, u, v))


def near_kernel(*refs):
    turned, refs = refs[:2], refs[2:]
    grad, made_ref, crossed_ref, p0_ref, p1_a, p1_b, p3_a, p3_b, sem = refs
    copy = pltpu.make_async_copy(made_ref, crossed_ref, sem)
    copy.start()
    half, rows, emb = p1_a.shape
    for t in range(2 * half):
        side, at = divmod(t, half)
        part = grad[:, t * emb : (t + 1) * emb]
        first = row_grads(turned[side], at, 0, 2 * rows, part)
        p0_ref[t] = first[:rows]
        (p1_a, p1_b)[side][at] = first[rows:].astype(BF16)
        (p3_a, p3_b)[side][at] = row_grads(turned[side], at, 3 * rows, rows, part).astype(BF16)
    copy.wait()


def near_rows(turned, grad, crossed):
    half, rows, samp = turned[0].shape
    block = (half, rows // 4, grad.shape[1] // (2 * half))
    return pl.pallas_call(
        near_kernel,
        in_specs=[vmem()] * 4,
        out_specs=[anyspace()] + [vmem()] * 5,
        out_shape=[pltpu.HBM(crossed.shape, BF16), pltpu.VMEM((2 * half,) + block[1:], F32)]
        + [pltpu.VMEM(block, BF16)] * 4,
        scratch_shapes=[pltpu.SemaphoreType.DMA],
        compiler_params=params(8),
        cost_estimate=cost(3 << 28, 7 << 20),
        name="near_rows",
    )(*kept(*turned, grad, crossed))


def finish_kernel(p0, near_a, far_a, near_b, far_b, out_ref, held, sems):
    half = near_a.shape[0]
    copies = []
    for side, (near, far) in enumerate(((near_a, far_a), (near_b, far_b))):
        at = pl.ds(side * half, half)
        held[at] = p0[at] + (near[...].astype(F32) + far[...].astype(F32))
        copies += [pltpu.make_async_copy(held.at[at], out_ref.at[at], sems.at[side])]
        copies[-1].start()
    for copy in copies:
        copy.wait()


def finish(p0, *others):
    return pl.pallas_call(
        finish_kernel,
        in_specs=[vmem()] * 5,
        out_specs=anyspace(),
        out_shape=pltpu.HBM(p0.shape, F32),
        scratch_shapes=[pltpu.VMEM(p0.shape, F32), pltpu.SemaphoreType.DMA((2,))],
        compiler_params=params(4),
        cost_estimate=cost(1 << 20, 1 << 20),
        name="finish",
    )(*kept(p0), *others)


def right(arr):
    return lax.ppermute(arr, "row", [(i, (i + 1) & 3) for i in range(4)])


def left(arr):
    return lax.ppermute(arr, "row", [(i, (i + 3) & 3) for i in range(4)])


def add(a, b):
    return a.astype(F32) + b.astype(F32)


def scalar(axis):
    return lax.axis_index(axis).astype(jnp.int32).reshape(1)


def local(emb_rows, entry_ids, entry_sample, cross_v, cross_u, cross_bias, cotangent):
    samp = cotangent.shape[0]
    rows = emb_rows.shape[1] * lax.axis_size("row")
    mine, core = scalar("row"), scalar("c")
    own_a, own_b = cast_halves(emb_rows)
    left_a, right_b = right(own_a), left(own_b)
    left_b, right_a = right(own_b), left(own_a)
    counts_a, edges = make_counts(mine, entry_ids, entry_sample, samp, rows)
    left_a, right_b, edges = lax.optimization_barrier((left_a, right_b, edges))
    far_a, far_b = right(left_a), left(right_b)
    loads = (cotangent, cross_v, cross_u)
    counts_b, cot, v, u = make_counts(mine, entry_ids, entry_sample, samp, rows, edges, loads)
    embs = (own_a, own_b, right_a, right_b, far_a, far_b, left_a, left_b)
    pooled, wide, send = first_sums(core, (counts_a, counts_b), embs, cot, v, u)
    prod, other, turned_a = sum_all(core, send, pooled, wide, v, u, 0, counts_a)
    x1, a, wide, send = middle(core, prod, other, cross_bias, pooled, cot, u, v)
    prod, other, turned_b = sum_all(core, send, x1, wide, v, u, 1, counts_b)
    turned = (turned_a, turned_b)
    crossed, grad, p2a, p2b = far_rows(core, prod, other, cross_bias, turned, pooled, cot, x1, a, u, v)
    from_left, from_right = right(p2a), left(p2b)
    crossed, p0, p1a, p1b, p3a, p3b = near_rows(turned, grad, crossed)
    sum_b, sum_a = right(p1b), left(p3a)
    far_a = right(add(p1a, from_left).astype(BF16))
    far_b = left(add(p3b, from_right).astype(BF16))
    return crossed, finish(p0, sum_a, far_a, sum_b, far_b)


def solution(mesh):
    fine = jax.sharding.Mesh(mesh.devices.reshape(4, 4, 2, 2, 4), ("x", "zh", "zl", "c", "row"))
    table = ("x", "zh", "zl", "c")
    placed = (
        P(table, "row", None),
        P(table, None),
        P(table, None),
        P(None, table, None),
        P(None, None, table),
        P(None, table),
        P("row", table),
    )
    return jax.shard_map(
        local,
        mesh=fine,
        in_specs=placed,
        out_specs=(P("row", table), P(table, "row", None)),
        check_vma=False,
    )
```

```python
import functools

import jax
import jax.numpy as jnp
from jax import lax
from jax.experimental import pallas as pl
from jax.experimental.pallas import tpu as pltpu
from jax.sharding import PartitionSpec as P

F32 = jnp.float32
BF16 = jnp.bfloat16
EB = 512
NT = (((1,), (1,)), ((), ()))
TN = (((0,), (0,)), ((), ()))


def vmem():
    return pl.BlockSpec(memory_space=pltpu.VMEM)


def smem():
    return pl.BlockSpec(memory_space=pltpu.SMEM)


def params(mib):
    return pltpu.CompilerParams(vmem_limit_bytes=mib * 2**20)


def cost(flops, moved):
    return pl.CostEstimate(flops=flops, bytes_accessed=moved, transcendentals=0)


def pinned(arr):
    return pltpu.with_memory_space_constraint(arr, pltpu.HBM)


def kept(*arrs):
    return [pltpu.with_memory_space_constraint(arr, pltpu.VMEM) for arr in arrs]


def hbm():
    return pl.BlockSpec(memory_space=pltpu.HBM)


def cast_kernel(in_ref, a_ref, b_ref, held, sems):
    half = a_ref.shape[0]
    outs = (a_ref, b_ref)
    copies = fetch(sems, [(in_ref.at[pl.ds(i * half, half)], held.at[i]) for i in range(2)])
    for i in range(2):
        copies[i].wait()
        outs[i][...] = held[i].astype(BF16)


def cast_halves(emb_rows):
    tabs, rows, emb = emb_rows.shape
    half = (tabs // 2, rows, emb)
    return pl.pallas_call(
        cast_kernel,
        in_specs=[hbm()],
        out_specs=[vmem()] * 2,
        out_shape=[pltpu.VMEM(half, BF16)] * 2,
        scratch_shapes=[pltpu.VMEM((2,) + half, F32), pltpu.SemaphoreType.DMA((2,))],
        compiler_params=params(4),
        cost_estimate=cost(1 << 18, 3 << 19),
        name="cast",
    )(pinned(emb_rows))


def counts_kernel(mine_ref, ids_ref, own_ref, *refs, first_table):
    refs, (acc_ref, ids, own, sems) = refs[:-4], refs[-4:]
    if first_table:
        edges_ref, *loads = refs[: len(refs) // 2]
        out_ref, *loaded = refs[len(refs) // 2 :]
    else:
        out_ref, edges_ref = refs
        loads = loaded = ()
    copies = fetch(sems, [(own_ref, own), (ids_ref, ids), *zip(loads, loaded)])
    _, rows, samp = acc_ref.shape
    tabs, entries = own.shape
    mine = mine_ref[0]
    low = mine * samp
    turn = mine * (rows // 4)
    copies[0].wait()
    if not first_table:
        owners = own[...]
        first = jnp.sum((owners < low).astype(jnp.int32), axis=1, keepdims=True)
        last = jnp.sum((owners < low + samp).astype(jnp.int32), axis=1, keepdims=True)
        for i in range(tabs):
            edges_ref[i] = first[i, 0]
            edges_ref[tabs + i] = last[i, 0]
    copies[1].wait()
    grid = lax.broadcasted_iota(jnp.int32, (samp, EB), 0).astype(F32).astype(BF16)
    one, zero = jnp.ones((), BF16), jnp.zeros((), BF16)

    @pl.loop(0, out_ref.shape[0] // 2)
    def _(pair):
        tables = [first_table + 2 * pair + j for j in range(2)]
        starts = [edges_ref[t] // 128 for t in tables]
        spans = [edges_ref[tabs + t] - start * 128 for t, start in zip(tables, starts)]
        steps = (jnp.maximum(*spans) + EB - 1) // EB
        starts = [jnp.minimum(start, (entries - steps * EB) // 128) * 128 for start in starts]
        acc_ref[...] = jnp.zeros_like(acc_ref)

        def body(block, carry):
            for j, t in enumerate(tables):
                at = pl.ds(pl.multiple_of(starts[j] + block * EB, 128), EB)
                who = own[pl.ds(t, 1), at] - low
                row = (ids[pl.ds(t, 1), at] - turn) & (rows - 1)
                hot = [
                    jnp.where(grid == values.astype(F32).astype(BF16), one, zero) for values in (who, row, row - samp)
                ]
                acc_ref[j] += lax.dot_general(
                    jnp.concatenate(hot[1:], axis=0), hot[0], NT, preferred_element_type=F32
                )
            return carry

        lax.fori_loop(0, steps, body, 0)
        for j in range(2):
            out_ref[2 * pair + j] = acc_ref[j].astype(BF16).T

    for copy in copies[2:]:
        copy.wait()


def make_counts(mine, ids, owners, samp, rows, edges=None, loads=()):
    tabs, entries = ids.shape
    assert rows == 2 * samp and samp <= 256
    half = tabs // 2
    out_shape = [pltpu.VMEM((half, samp, rows), BF16)]
    args = (mine, pinned(ids), pinned(owners))
    in_specs, out_specs = [smem(), hbm(), hbm()], [vmem()]
    if edges is None:
        out_specs.append(smem())
        out_shape.append(jax.ShapeDtypeStruct((2 * tabs,), jnp.int32))
    else:
        args += (edges, *map(pinned, loads))
        in_specs += [smem()] + [hbm()] * len(loads)
        out_specs += [vmem()] * len(loads)
        out_shape += [pltpu.VMEM(arr.shape, arr.dtype) for arr in loads]
    return pl.pallas_call(
        functools.partial(counts_kernel, first_table=0 if edges is None else half),
        in_specs=in_specs,
        out_specs=out_specs,
        out_shape=out_shape,
        scratch_shapes=[
            pltpu.VMEM((2, rows, samp), F32),
            pltpu.VMEM((tabs, entries), jnp.int32),
            pltpu.VMEM((tabs, entries), jnp.int32),
            pltpu.SemaphoreType.DMA((2 + len(loads),)),
        ],
        compiler_params=params(6),
        cost_estimate=cost(half * samp * rows * 3072, 3 << 20),
        name="counts",
    )(*args)


def turned_kernel(in_ref, out_ref):
    for i in range(out_ref.shape[0]):
        out_ref[i] = in_ref[i].T


def turned_counts(counts):
    half, samp, rows = counts.shape
    return pl.pallas_call(
        turned_kernel,
        in_specs=[vmem()],
        out_specs=vmem(),
        out_shape=pltpu.VMEM((half, rows, samp), BF16),
        compiler_params=params(8),
        cost_estimate=cost(1 << 29, 2 << 20),
        name="turned",
    )(*kept(counts))


WIDE = 512


def fetch(sems, pairs):
    copies = [pltpu.make_async_copy(src, dst, sems.at[i]) for i, (src, dst) in enumerate(pairs)]
    for copy in copies:
        copy.start()
    return copies


def sum_z(x, v_ref, layer):
    return jnp.dot(x[...], v_ref[layer], preferred_element_type=F32)


def sum_g(wide, u_ref, layer):
    return lax.dot_general(wide[...], u_ref[layer], NT, preferred_element_type=F32)


def one_sum(even, x, wide, v_ref, u_ref, layer, out_ref):
    @pl.when(even)
    def _():
        out_ref[...] = sum_z(x, v_ref, layer).astype(out_ref.dtype)

    @pl.when(jnp.logical_not(even))
    def _():
        out_ref[...] = sum_g(wide, u_ref, 1 - layer).astype(out_ref.dtype)


def keep_kernel(core_ref, x, wide, v_ref, u_ref, out_ref, *, layer):
    one_sum(core_ref[0] == 0, x, wide, v_ref, u_ref, layer, out_ref)


def keep_sum(core, x, wide, v, u, layer):
    return pl.pallas_call(
        functools.partial(keep_kernel, layer=layer),
        in_specs=[smem()] + [vmem()] * 4,
        out_specs=vmem(),
        out_shape=pltpu.VMEM((x.shape[0], v.shape[-1]), F32),
        compiler_params=params(8),
        cost_estimate=cost(1 << 29, 4 << 20),
        name="keep_sum",
    )(core, *kept(x, wide, v, u))


def anyspace():
    return pl.BlockSpec(memory_space=pl.ANY)


def near_kernel_pool(counts_a, counts_b, oa, ob, ra, rb, la, lb, out_ref):
    half, rows, emb = oa.shape
    for t in range(2 * half):
        side, i = divmod(t, half)
        counts = (counts_a, counts_b)[side]
        own, right_rows, left_rows = ((oa, ra, la), (ob, rb, lb))[side]
        two = jnp.concatenate([own[i], right_rows[i]], axis=0)
        part = jnp.dot(counts[i, :, : 2 * rows], two, preferred_element_type=F32)
        part += jnp.dot(counts[i, :, 3 * rows :], left_rows[i], preferred_element_type=F32)
        out_ref[:, t * emb : (t + 1) * emb] = part.astype(BF16)


def near_pooled(counts, embs):
    half, samp, _ = counts[0].shape
    emb = embs[0].shape[-1]
    return pl.pallas_call(
        near_kernel_pool,
        in_specs=[vmem()] * 8,
        out_specs=vmem(),
        out_shape=pltpu.VMEM((samp, 2 * half * emb), BF16),
        compiler_params=params(4),
        cost_estimate=cost(1 << 29, 4 << 20),
        name="near_pooled",
    )(*kept(*counts), *embs)


def first_kernel(core_ref, counts_a, counts_b, part, far_a, far_b, cot, v_ref, u_ref, pooled_ref, wide_ref, send_ref):
    half, rows, emb = far_a.shape
    for t in range(2 * half):
        side, i = divmod(t, half)
        at = slice(t * emb, (t + 1) * emb)
        far = (counts_a, counts_b)[side][i, :, 2 * rows : 3 * rows]
        pooled = jnp.dot(far, (far_a, far_b)[side][i], preferred_element_type=F32)
        pooled = (pooled + part[:, at].astype(F32)).astype(BF16)
        pooled_ref[:, at] = pooled
        wide_ref[:, at] = (cot[:, at].astype(F32) * pooled.astype(F32)).astype(BF16)
    one_sum(core_ref[0] != 0, pooled_ref, wide_ref, v_ref, u_ref, 0, send_ref)


def first_sums(core, counts, part, far, cot, v, u):
    half, samp, rows = counts[0].shape
    emb = far[0].shape[-1]
    rank = v.shape[-1]
    return pl.pallas_call(
        first_kernel,
        in_specs=[smem()] + [vmem()] * 8,
        out_specs=[vmem()] * 3,
        out_shape=[
            pltpu.VMEM((samp, 2 * half * emb), BF16),
            pltpu.VMEM((samp, 2 * half * emb), BF16),
            pltpu.VMEM((samp, rank), BF16),
        ],
        compiler_params=params(8),
        cost_estimate=cost(3 << 29, 10 << 20),
        name="first_sums",
    )(core, *kept(*counts, part), *far, *kept(cot, v, u))


def swap(arr, axis):
    return lax.ppermute(arr, axis, [(0, 1), (1, 0)])


def small(kernel, out_shape, name, *args):
    return pl.pallas_call(
        kernel,
        in_specs=[vmem()] * len(args),
        out_specs=jax.tree.map(lambda _: vmem(), out_shape),
        out_shape=out_shape,
        compiler_params=params(8),
        cost_estimate=cost(1 << 20, 1 << 20),
        name=name,
    )(*args)


CHUNKS = 8
CHUNK = (32, 512)


def chunk_at(i):
    return slice(CHUNK[0] * i, CHUNK[0] * (i + 1)), slice(None)


def cut_kernel(keep_ref, got_ref, out_ref):
    for i in range(CHUNKS):
        at = chunk_at(i)
        out_ref[i] = (keep_ref[at] + got_ref[at].astype(F32)).astype(BF16)


def total_kernel(*refs):
    *ins, out_ref = refs
    total = sum(ref[i].astype(F32) for ref in ins for i in range(ref.shape[0])).astype(BF16)
    for i in range(out_ref.shape[0]):
        out_ref[i] = total


def total(copies, *arrays):
    return small(total_kernel, pltpu.VMEM((copies,) + CHUNK, BF16), "total", *arrays)


def swap_all(arr):
    return lax.all_to_all(arr, ("x", "zl"), 0, 0, tiled=True)


def turn(arr, k):
    return lax.ppermute(arr, "zh", [(i, (i + k) & 3) for i in range(4)])


def layout(chunks_ref, sum_ref):
    for i in range(CHUNKS):
        sum_ref[chunk_at(i)] = chunks_ref[i]


def z_u(total, u_ref, layer, at):
    return jnp.dot(total, u_ref[layer, :, at], preferred_element_type=F32)


def g_v(total, v_ref, layer, at):
    return lax.dot_general(total, v_ref[layer, at, :], NT, preferred_element_type=F32)


def steps_of(feats):
    return [slice(f, f + WIDE) for f in range(0, feats, WIDE)]


def product_kernel(core_ref, mine_ref, v_ref, u_ref, out_ref, sum_ref, *, layer):
    layout(mine_ref, sum_ref)

    @pl.when(core_ref[0] == 0)
    def _():
        for at in steps_of(out_ref.shape[1]):
            out_ref[:, at] = z_u(sum_ref[...], u_ref, layer, at)

    @pl.when(core_ref[0] != 0)
    def _():
        for at in steps_of(out_ref.shape[1]):
            out_ref[:, at] = g_v(sum_ref[...], v_ref, 1 - layer, at)


def product(core, mine, v, u, layer):
    samp, rank = CHUNKS * CHUNK[0], CHUNK[1]
    return pl.pallas_call(
        functools.partial(product_kernel, layer=layer),
        in_specs=[smem()] + [vmem()] * 3,
        out_specs=vmem(),
        out_shape=pltpu.VMEM((samp, u.shape[-1]), F32),
        scratch_shapes=[pltpu.VMEM((samp, rank), BF16)],
        compiler_params=params(8),
        cost_estimate=cost(1 << 29, 4 << 20),
        name="product",
    )(core, mine, *kept(v, u))


def by_core(core_ref, body, prod, sum_ref, v_ref, u_ref, layer):
    @pl.when(core_ref[0] == 0)
    def _():
        body(lambda at: prod[:, at], lambda at: g_v(sum_ref[...], v_ref, 1 - layer, at))

    @pl.when(core_ref[0] != 0)
    def _():
        body(lambda at: z_u(sum_ref[...], u_ref, layer, at), lambda at: prod[:, at])


def sum_all(core, send, x, wide, v, u, layer, counts):
    send, x = lax.optimization_barrier((send, x))
    got, keep = lax.optimization_barrier((swap(send, "c"), keep_sum(core, x, wide, v, u, layer)))
    shape = pltpu.VMEM((CHUNKS,) + CHUNK, BF16)
    parts = swap_all(small(cut_kernel, shape, "cut", keep, got))
    own, counts = lax.optimization_barrier((total(1, parts), counts))
    near = (turn(own, 1), turn(own, 3), turn(own, 2), turned_counts(counts))
    *near, turned = lax.optimization_barrier(near)
    mine = swap_all(total(CHUNKS, own, *near))
    prod, other = lax.optimization_barrier((product(core, mine, v, u, layer), swap(mine, "c")))
    return prod, other, turned


def middle_kernel(core_ref, prod, other_ref, b_ref, pooled, cot, u_ref, v_ref, x1_ref, a_ref, wide_ref, send_ref, sum_ref):
    layout(other_ref, sum_ref)

    def body(h, g):
        for at in steps_of(pooled.shape[1]):
            base = pooled[:, at].astype(F32)
            h0 = h(at) + b_ref[0:1, at]
            x1_ref[:, at] = (base * h0 + base).astype(BF16)
            g1 = cot[:, at].astype(F32) + g(at)
            a_ref[:, at] = (g1 * h0 + g1).astype(BF16)
            wide_ref[:, at] = (g1 * base).astype(BF16)

    by_core(core_ref, body, prod, sum_ref, v_ref, u_ref, 0)
    one_sum(core_ref[0] != 0, x1_ref, wide_ref, v_ref, u_ref, 1, send_ref)


def middle(core, prod, other, bias, pooled, cot, u, v):
    samp, feats = pooled.shape
    rank = v.shape[-1]
    feat = pltpu.VMEM((samp, feats), BF16)
    return pl.pallas_call(
        middle_kernel,
        in_specs=[smem()] + [vmem()] * 7,
        out_specs=[vmem()] * 4,
        out_shape=[feat, feat, feat, pltpu.VMEM((samp, rank), BF16)],
        scratch_shapes=[pltpu.VMEM((samp, rank), BF16)],
        compiler_params=params(10),
        cost_estimate=cost(1 << 31, 8 << 20),
        name="middle",
    )(core, *kept(prod), other, bias, *kept(pooled, cot, u, v))


def row_grads(turned_ref, table, first, count, grad):
    return jnp.dot(turned_ref[table, first : first + count, :], grad, preferred_element_type=F32)


def far_kernel(core_ref, prod, other_ref, b_ref, turned_a, turned_b, pooled, cot, x1, a, u_ref, v_ref, *refs):
    crossed_ref, grad_ref, far_a, far_b, sum_ref = refs
    half, rows, emb = far_a.shape
    layout(other_ref, sum_ref)

    def body(h, g):
        for at in steps_of(pooled.shape[1]):
            h1 = h(at) + b_ref[1:2, at]
            crossed_ref[:, at] = (pooled[:, at].astype(F32) * h1 + x1[:, at].astype(F32)).astype(BF16)
            grad_ref[:, at] = (cot[:, at].astype(F32) * h1 + a[:, at].astype(F32) + g(at)).astype(BF16)

    by_core(core_ref, body, prod, sum_ref, v_ref, u_ref, 1)
    for t in range(2 * half):
        side, i = divmod(t, half)
        part = row_grads((turned_a, turned_b)[side], i, 2 * rows, rows, grad_ref[:, t * emb : (t + 1) * emb])
        (far_a, far_b)[side][i] = part.astype(BF16)


def far_rows(core, prod, other, bias, turned, pooled, cot, x1, a, u, v):
    half, rows, samp = turned[0].shape
    rank = v.shape[-1]
    feats = pooled.shape[1]
    piece = pltpu.VMEM((half, rows // 4, feats // (2 * half)), BF16)
    return pl.pallas_call(
        far_kernel,
        in_specs=[smem()] + [vmem()] * 11,
        out_specs=[vmem()] * 4,
        out_shape=[pltpu.VMEM(pooled.shape, BF16)] * 2 + [piece, piece],
        scratch_shapes=[pltpu.VMEM((samp, rank), BF16)],
        compiler_params=params(8),
        cost_estimate=cost(5 << 28, 7 << 20),
        name="far_rows",
    )(core, *kept(prod), other, bias, *kept(*turned, pooled, cot, x1, a, u, v))


def near_kernel(*refs):
    turned, refs = refs[:2], refs[2:]
    grad, made_ref, crossed_ref, p0_ref, p1_a, p1_b, p3_a, p3_b, sem = refs
    copy = pltpu.make_async_copy(made_ref, crossed_ref, sem)
    copy.start()
    half, rows, emb = p1_a.shape
    for t in range(2 * half):
        side, at = divmod(t, half)
        part = grad[:, t * emb : (t + 1) * emb]
        first = row_grads(turned[side], at, 0, 2 * rows, part)
        p0_ref[t] = first[:rows]
        (p1_a, p1_b)[side][at] = first[rows:].astype(BF16)
        (p3_a, p3_b)[side][at] = row_grads(turned[side], at, 3 * rows, rows, part).astype(BF16)
    copy.wait()


def near_rows(turned, grad, crossed):
    half, rows, samp = turned[0].shape
    block = (half, rows // 4, grad.shape[1] // (2 * half))
    return pl.pallas_call(
        near_kernel,
        in_specs=[vmem()] * 4,
        out_specs=[anyspace()] + [vmem()] * 5,
        out_shape=[pltpu.HBM(crossed.shape, BF16), pltpu.VMEM((2 * half,) + block[1:], F32)]
        + [pltpu.VMEM(block, BF16)] * 4,
        scratch_shapes=[pltpu.SemaphoreType.DMA],
        compiler_params=params(8),
        cost_estimate=cost(3 << 28, 7 << 20),
        name="near_rows",
    )(*kept(*turned, grad, crossed))


def finish_kernel(p0, near_a, far_a, near_b, far_b, out_ref, held, sems):
    half = near_a.shape[0]
    copies = []
    for side, (near, far) in enumerate(((near_a, far_a), (near_b, far_b))):
        at = pl.ds(side * half, half)
        held[at] = p0[at] + (near[...].astype(F32) + far[...].astype(F32))
        copies += [pltpu.make_async_copy(held.at[at], out_ref.at[at], sems.at[side])]
        copies[-1].start()
    for copy in copies:
        copy.wait()


def finish(p0, *others):
    return pl.pallas_call(
        finish_kernel,
        in_specs=[vmem()] * 5,
        out_specs=anyspace(),
        out_shape=pltpu.HBM(p0.shape, F32),
        scratch_shapes=[pltpu.VMEM(p0.shape, F32), pltpu.SemaphoreType.DMA((2,))],
        compiler_params=params(4),
        cost_estimate=cost(1 << 20, 1 << 20),
        name="finish",
    )(*kept(p0), *others)


def right(arr):
    return lax.ppermute(arr, "row", [(i, (i + 1) & 3) for i in range(4)])


def left(arr):
    return lax.ppermute(arr, "row", [(i, (i + 3) & 3) for i in range(4)])


def add(a, b):
    return a.astype(F32) + b.astype(F32)


def scalar(axis):
    return lax.axis_index(axis).astype(jnp.int32).reshape(1)


def local(emb_rows, entry_ids, entry_sample, cross_v, cross_u, cross_bias, cotangent):
    samp = cotangent.shape[0]
    rows = emb_rows.shape[1] * lax.axis_size("row")
    mine, core = scalar("row"), scalar("c")
    own_a, own_b = cast_halves(emb_rows)
    left_a, right_b = right(own_a), left(own_b)
    left_b, right_a = right(own_b), left(own_a)
    counts_a, edges = make_counts(mine, entry_ids, entry_sample, samp, rows)
    left_a, right_b, edges = lax.optimization_barrier((left_a, right_b, edges))
    far_a, far_b = right(left_a), left(right_b)
    loads = (cotangent, cross_v, cross_u)
    counts_b, cot, v, u = make_counts(mine, entry_ids, entry_sample, samp, rows, edges, loads)
    counts = (counts_a, counts_b)
    part = near_pooled(counts, (own_a, own_b, right_a, right_b, left_a, left_b))
    pooled, wide, send = first_sums(core, counts, part, (far_a, far_b), cot, v, u)
    prod, other, turned_a = sum_all(core, send, pooled, wide, v, u, 0, counts_a)
    x1, a, wide, send = middle(core, prod, other, cross_bias, pooled, cot, u, v)
    prod, other, turned_b = sum_all(core, send, x1, wide, v, u, 1, counts_b)
    turned = (turned_a, turned_b)
    crossed, grad, p2a, p2b = far_rows(core, prod, other, cross_bias, turned, pooled, cot, x1, a, u, v)
    from_left, from_right = right(p2a), left(p2b)
    crossed, p0, p1a, p1b, p3a, p3b = near_rows(turned, grad, crossed)
    sum_b, sum_a = right(p1b), left(p3a)
    far_a = right(add(p1a, from_left).astype(BF16))
    far_b = left(add(p3b, from_right).astype(BF16))
    return crossed, finish(p0, sum_a, far_a, sum_b, far_b)


def solution(mesh):
    fine = jax.sharding.Mesh(mesh.devices.reshape(4, 4, 2, 2, 4), ("x", "zh", "zl", "c", "row"))
    table = ("x", "zh", "zl", "c")
    placed = (
        P(table, "row", None),
        P(table, None),
        P(table, None),
        P(None, table, None),
        P(None, None, table),
        P(None, table),
        P("row", table),
    )
    return jax.shard_map(
        local,
        mesh=fine,
        in_specs=placed,
        out_specs=(P("row", table), P(table, "row", None)),
        check_vma=False,
    )
```
